32 devices in a mesh: sec: 4 (over z), row: 2 (over y), col: 4 (over x, core).
Axes of the slice: x: 2, y: 2, z: 4, core: 2. Of those that a mesh axis runs over, the one named last changes fastest.
Arguments:
- labels: int32 [8, 128, 512], P('col', 'row', 'sec'), may hold values 0 or 1
- jitter: float32 [2, 8, 128, 512], P(None, 'col', 'row', 'sec'), may hold values from 0.5 to 1.5
- shells: int32 [128, 512], P('row', 'sec'), may hold values from 0 to 255, as said below
Outputs:
- populations: float32 [38, 8, 128, 512], P(None, 'col', 'row', 'sec')
- spectrum: float32 [8, 256], P('col')
The draws below stay inside these ranges and needn't reach their ends.
Inputs may be any that keep to these rules, and one draw needn't show every extreme that they name: shells are radial bins of |k|: with kx' = kx for kx < 64, else kx - 128 (ky' likewise with 512), shells[kx, ky] = min(floor(sqrt(kx'^2 + ky'^2 + j)), 255), where j is 0 or 1 per wavevector (0 at k = 0); every label from 0 to 255 belongs to at least one wavevector.
All inputs are finite; a program needn't handle non-finite values. No bound on the sum of `labels` on one device may be relied on, other than what follows from the above.
Results may differ from the reference program's by a relative error of at most 0.002.
Values may be sent and summed in bfloat16 or wider, within the bound.
No kernel may reach another device: no remote copies, remote signals or barrier semaphores. Data moves between devices by JAX's collectives and lax.ppermute only.
A program may use at most 64 MiB of HBM per device.

```python
import math
import jax
import jax.numpy as jnp
from jax import lax

NSHELL = 256
NX = 128
NY = 512
NZ = 8


def draw_shells(key, part):
    freq_x = jnp.arange(NX, dtype=jnp.int32)
    freq_y = jnp.arange(NY, dtype=jnp.int32)
    freq_x = jnp.where(freq_x < NX // 2, freq_x, freq_x - NX)
    freq_y = jnp.where(freq_y < NY // 2, freq_y, freq_y - NY)
    radius_sq = freq_x[:, None] * freq_x[:, None] + freq_y[None, :] * freq_y[None, :]
    nudge = jax.random.randint(key, (NX, NY), 0, 2, dtype=jnp.int32)
    nudge = jnp.where(radius_sq > 0, nudge, 0)
    target = radius_sq + nudge
    guess = jnp.floor(jnp.sqrt(target.astype(jnp.float32))).astype(jnp.int32)
    guess = guess - (guess * guess > target).astype(jnp.int32)
    guess = guess + ((guess + 1) * (guess + 1) <= target).astype(jnp.int32)
    return jnp.minimum(guess, NSHELL - 1).astype(jnp.int32)


def place_ends(array, own_key, least, largest):
    longest = array.shape.index(max(array.shape))
    spots = []
    for shift in (0, 1):
        where = [jax.random.randint(jax.random.fold_in(own_key, axis), (), 0, length) for axis, length in enumerate(array.shape)]
        where[longest] = (where[longest] + shift) % array.shape[longest]
        spots.append(tuple(where))
    return array.at[spots[0]].set(least).at[spots[1]].set(largest)


def shard_levels(stream_key, shape, pieces, smallest, top_value):
    level, own = 1.0, jax.random.fold_in(stream_key, 6)
    for position, parts in pieces:
        heights = jnp.exp(jax.random.uniform(jax.random.fold_in(own, position), (parts,), jnp.float32, smallest / len(pieces), top_value / len(pieces)))
        level = level * jnp.repeat(heights, shape[position] // parts).reshape([-1 if axis == position else 1 for axis in range(len(shape))])
    return level


def setup_inputs(seed: int = 0) -> dict:
    streams_of = jax.random.split(jax.random.key(seed), 4)
    labels = place_ends((jax.random.randint(streams_of[0], (NZ, NX, NY), 0, 2) < 1).astype(jnp.int32), jax.random.fold_in(streams_of[0], 1), 0, 1)
    jitter = jnp.clip(0.5 + 1.0 * jax.random.uniform(streams_of[1], (2, NZ, NX, NY), jnp.float32) ** shard_levels(streams_of[1], (2, NZ, NX, NY), ((1, 4), (2, 2), (3, 4)), -0.2, 0.2), 0.5, 1.5)
    shells = draw_shells(jax.random.fold_in(streams_of[3], 71), 0)
    return {"labels": labels, "jitter": jitter, "shells": shells}


LATTICE = ((0, 0, 0), (1, 0, 0), (-1, 0, 0), (0, 1, 0), (0, -1, 0), (0, 0, 1), (0, 0, -1),
           (1, 1, 0), (-1, -1, 0), (1, -1, 0), (-1, 1, 0), (1, 0, 1), (-1, 0, -1), (1, 0, -1), (-1, 0, 1),
           (0, 1, 1), (0, -1, -1), (0, 1, -1), (0, -1, 1))
WEIGHTS = (1.0 / 3.0,) + (1.0 / 18.0,) * 6 + (1.0 / 36.0,) * 12


def density_pair(labels, jitter):
    heavy_a = jnp.where(labels == 1, jnp.float32(1.0), jnp.float32(0.2))
    heavy_b = jnp.where(labels == 1, jnp.float32(0.2), jnp.float32(1.0))
    return jnp.stack([heavy_a * jitter[0], heavy_b * jitter[1]])


def relax_term(density, velocity, offsets, weight):
    squared = velocity[0] * velocity[0] + velocity[1] * velocity[1] + velocity[2] * velocity[2]
    projected = offsets[0] * velocity[0] + offsets[1] * velocity[1] + offsets[2] * velocity[2]
    return weight * density * (1.0 + 1.25 * (3.0 * projected + 4.5 * projected * projected - 1.5 * squared))


def reference(labels, jitter, shells):
    densities = density_pair(labels, jitter)
    zeros_field = jnp.zeros_like(densities)
    totals_axis = [zeros_field, zeros_field, zeros_field]
    for offsets, weight in zip(LATTICE[1:], WEIGHTS[1:]):
        shifted = jnp.roll(densities, (-offsets[2], -offsets[0], -offsets[1]), axis=(1, 2, 3))
        for axis_id in range(3):
            if offsets[axis_id] != 0:
                totals_axis[axis_id] = totals_axis[axis_id] + (weight * offsets[axis_id]) * shifted
    pull_terms = jnp.stack(totals_axis, axis=1)
    velocities = (-1.6 * pull_terms[1], -1.6 * pull_terms[0])
    term_list = []
    for component in range(2):
        for offsets, weight in zip(LATTICE, WEIGHTS):
            term = relax_term(densities[component], velocities[component], offsets, weight)
            term_list.append(jnp.roll(term, (offsets[2], offsets[0], offsets[1]), axis=(0, 1, 2)))
    populations = jnp.stack(term_list)

    order_b = lax.optimization_barrier((densities[0] - densities[1]).astype(jnp.bfloat16))
    rows_x = jnp.arange(NX, dtype=jnp.int32)
    angles_x = ((rows_x[:, None] * rows_x[None, :]) % NX).astype(jnp.float32) * (2.0 * math.pi / NX)
    table_x = jnp.concatenate([jnp.cos(angles_x).astype(jnp.bfloat16), (-jnp.sin(angles_x)).astype(jnp.bfloat16)], 0)
    half_step = jnp.einsum('kx,zxy->zky', table_x.astype(jnp.float32), order_b.astype(jnp.float32)).astype(jnp.bfloat16)
    half_step = lax.optimization_barrier(half_step)
    rows_y = jnp.arange(NY, dtype=jnp.int32)
    angles_y = ((rows_y[:, None] * rows_y[None, :]) % NY).astype(jnp.float32) * (2.0 * math.pi / NY)
    cos_y = jnp.cos(angles_y).astype(jnp.bfloat16)
    sin_y = jnp.sin(angles_y).astype(jnp.bfloat16)
    right_side = jnp.concatenate([jnp.concatenate([cos_y, -sin_y], 1), jnp.concatenate([sin_y, cos_y], 1)], 0)
    left_side = jnp.concatenate([half_step[:, :NX], half_step[:, NX:]], axis=2)
    transform = jnp.einsum('zkv,vw->zkw', left_side.astype(jnp.float32), right_side.astype(jnp.float32))
    real_part = transform[..., :NY]
    imag_part = transform[..., NY:]
    power_map = real_part * real_part + imag_part * imag_part
    flat_shells = shells.reshape(NX * NY)
    totals = jax.ops.segment_sum(power_map.reshape(NZ, NX * NY).T, flat_shells, num_segments=NSHELL)
    counts = jax.ops.segment_sum(jnp.ones((NX * NY,), jnp.float32), flat_shells, num_segments=NSHELL)
    spectrum = (totals / (counts[:, None] * float(NX * NY))).T
    return populations, spectrum
```

```python
import functools
import math

import jax
import jax.numpy as jnp
import ml_dtypes
import numpy as np
from jax import lax
from jax.experimental import pallas as pl
from jax.experimental.pallas import tpu as pltpu
from jax.sharding import PartitionSpec as P

NSHELL = 256
LO = 16
ROWS = 72
F32 = jnp.float32
BF16 = jnp.bfloat16

LATTICE = (
    (0, 0, 0),
    (1, 0, 0),
    (-1, 0, 0),
    (0, 1, 0),
    (0, -1, 0),
    (0, 0, 1),
    (0, 0, -1),
    (1, 1, 0),
    (-1, -1, 0),
    (1, -1, 0),
    (-1, 1, 0),
    (1, 0, 1),
    (-1, 0, -1),
    (1, 0, -1),
    (-1, 0, 1),
    (0, 1, 1),
    (0, -1, -1),
    (0, 1, -1),
    (0, -1, 1),
)
WEIGHTS = (1.0 / 3.0,) + (1.0 / 18.0,) * 6 + (1.0 / 36.0,) * 12


def xor_pairs(count, bits):
    return [(i, i ^ bits) for i in range(count)]


def shift_pairs(count, step):
    return [(i, (i + step) % count) for i in range(count)]


def ring_moves(count):
    if count == 2:
        return [xor_pairs(2, 1)]
    if count == 4:
        return [xor_pairs(4, 1), xor_pairs(4, 3)]
    return [shift_pairs(count, 1), shift_pairs(count, -1)]


def ring_pick(count, index):
    if count == 2:
        return 0, 0
    if count == 4:
        odd = lax.rem(index, 2)
        return 1 - odd, odd
    return 0, 1


def pair_product(first, second, count_second):
    return [
        (a * count_second + b, c * count_second + d) for a, c in first for b, d in second
    ]


def choose(items, which):
    if isinstance(which, int):
        return items[which]
    value = items[0]
    for number in range(1, len(items)):
        value = jnp.where(which == number, items[number], value)
    return value


def bf16_table(values):
    return np.asarray(values, np.float32).astype(ml_dtypes.bfloat16)


def angle_table(freq, pos, full):
    step = np.float32(2.0 * math.pi / full)
    return ((freq * pos) % full).astype(np.float32) * step


@functools.lru_cache(maxsize=None)
def make_tables(full_x, full_y, n_row, n_sec, wx, wy):
    half_x, half_y = full_x // 2, full_y // 2
    freq = np.arange(half_x)[:, None]
    pos = np.arange(full_x)[None, :]
    angles = angle_table(freq, pos, full_x)
    lower = -np.sin(angles)
    lower[0] = np.cos(angle_table(np.array([[half_x]]), pos, full_x))[0]
    table_x = np.concatenate([np.cos(angles), lower], 0)
    table_x = np.stack([table_x[:, r * wx : (r + 1) * wx] for r in range(n_row)])
    lanes = half_y + 128
    freq_y = np.arange(lanes)[None, :]
    angles = angle_table(np.arange(full_y)[:, None], freq_y, full_y)
    live = freq_y <= half_y
    table_y = np.concatenate([np.cos(angles) * live, np.sin(angles) * live], 1)
    hrows = half_x + 8
    radius = np.arange(hrows)[:, None] ** 2 + np.arange(lanes)[None, :] ** 2
    base = np.minimum(np.floor(np.sqrt(radius.astype(np.float64))).astype(np.int64), NSHELL - 1)
    valid = (np.arange(hrows)[:, None] <= half_x) & (np.arange(lanes)[None, :] <= half_y)
    hi = np.where(valid, base // LO, -1).astype(np.float32)
    lo = np.where(valid, base % LO, -1).astype(np.float32)
    mult_y = np.where(freq_y > half_y, 0, np.where((freq_y == 0) | (freq_y == half_y), 1, 2))
    signed_x = np.arange(full_x)
    signed_x = np.where(signed_x < half_x, signed_x, signed_x - full_x)
    signed_y = np.arange(full_y)
    signed_y = np.where(signed_y < half_y, signed_y, signed_y - full_y)
    square = signed_x[:, None] ** 2 + signed_y[None, :] ** 2
    root = np.floor(np.sqrt(square + 1.0) + 1e-9).astype(np.int64)
    special = (root * root == square + 1) & (root < NSHELL) & (square > 0)
    low_label = np.minimum(np.floor(np.sqrt(square.astype(np.float64))), NSHELL - 1)
    counts = np.bincount(low_label.astype(np.int64).ravel(), minlength=NSHELL)
    blocks = {}
    for r in range(n_row):
        for s in range(n_sec):
            where = np.argwhere(special[r * wx : (r + 1) * wx, s * wy : (s + 1) * wy])
            blocks[r, s] = [(int(a) + r * wx, int(b) + s * wy) for a, b in where]
    slots = max(len(v) for v in blocks.values())
    width = 128 * (-(-(n_row * slots) // 128))
    take_row = np.zeros((n_row * n_sec, wx, width))
    take_col = np.zeros((n_row * n_sec, wy, width))
    low = np.zeros((n_sec * width,))
    put_row = np.zeros((2 * hrows, n_sec * width))
    put_col = np.zeros((n_sec * width, lanes))
    for (r, s), points in blocks.items():
        for number, (kx, ky) in enumerate(points):
            lane = r * slots + number
            take_row[r * n_sec + s, kx - r * wx, lane] = 1
            take_col[r * n_sec + s, ky - s * wy, lane] = 1
            place = s * width + lane
            low[place] = root[kx, ky] - 1
            ax, ay = abs(int(signed_x[kx])), abs(int(signed_y[ky]))
            same = int(signed_x[kx]) * int(signed_y[ky]) >= 0 or ax == half_x or ay == half_y
            put_row[ax + (0 if same else hrows), place] = 1
            put_col[place, ay] = 1
    spread = (np.arange(NSHELL)[None, :] % LO == np.arange(LO)[:, None]).astype(np.float32)
    return dict(
        width=width,
        table_x=bf16_table(table_x),
        table_y=bf16_table(table_y),
        hi=hi,
        lo=lo,
        mult_y=mult_y.astype(np.float32),
        counts=counts.astype(np.float32)[None, :],
        take_row=np.asarray(take_row, np.float32),
        take_col=bf16_table(take_col),
        low=low.astype(np.float32)[None, :],
        put_row=np.asarray(put_row, np.float32),
        put_col=bf16_table(put_col),
        spread=spread,
    )


def own_densities(labels_ref, jitter_ref, z):
    heavy = labels_ref[z] == 1
    first = jnp.where(heavy, F32(1.0), F32(0.2)) * jitter_ref[0, z]
    second = jnp.where(heavy, F32(0.2), F32(1.0)) * jitter_ref[1, z]
    return first, second


def pack_kernel(n_sec, labels_ref, jitter_ref, shells_ref, take_row_ref, take_col_ref,
                col_ref, row_ref, edge_ref):
    depth, wx, wy = labels_ref.shape
    densities = [own_densities(labels_ref, jitter_ref, z) for z in range(depth)]
    edges = []
    for c in range(2):
        for z in range(depth):
            tile = densities[z][c]
            at = (c * depth + z) * wx
            col_ref[at : at + wx] = tile.astype(BF16)
            edges += [tile[0:2], tile[wx - 2 : wx]]
    for z in range(depth):
        row_ref[z * wx : (z + 1) * wx] = (densities[z][0] - densities[z][1]).astype(BF16)
    edge = jnp.concatenate(edges, axis=0).astype(BF16)
    edge_ref[...] = edge
    at = depth * wx
    count = edge.shape[0]
    row_ref[at : at + count] = edge
    block = lax.axis_index("row") * n_sec + lax.axis_index("sec")
    picked = jnp.dot(
        shells_ref[...].astype(F32).astype(BF16), take_col_ref[block], preferred_element_type=F32
    )
    marks = jnp.sum(picked * take_row_ref[block], axis=0, keepdims=True)
    width = marks.shape[1]
    lines = [marks[:, g * 128 : (g + 1) * 128] for g in range(width // 128)]
    lines.append(jnp.zeros((16 - len(lines), 128), F32))
    row_ref[at + count :] = jnp.concatenate(lines, axis=0).astype(BF16)


def middle_kernel(n_row, n_col, labels_ref, jitter_ref, *refs):
    depth, wx, wy = labels_ref.shape
    col_moves, row_moves = len(ring_moves(n_col)), len(ring_moves(n_row))
    col_refs, refs = refs[:col_moves], refs[col_moves:]
    row_refs, refs = refs[:n_row], refs[n_row:]
    diag_refs, refs = refs[: col_moves * row_moves], refs[col_moves * row_moves :]
    table_ref, msg_ref, dens_ref, lanes_ref = refs
    row, col = lax.axis_index("row"), lax.axis_index("col")
    full_x = table_ref.shape[1]

    for z in range(depth):
        half = None
        for k in range(n_row):
            part = jnp.dot(
                table_ref[row ^ k],
                row_refs[k][z * wx : (z + 1) * wx],
                preferred_element_type=F32,
            )
            half = part if half is None else half + part
        msg_ref[z * full_x : (z + 1) * full_x] = half.astype(BF16)

    at = depth * wx
    count = 8 * depth
    marks = sum(ref[at + count : at + count + 16].astype(F32) for ref in row_refs)

    own = [own_densities(labels_ref, jitter_ref, z) for z in range(depth)]
    col_prev, col_next = ring_pick(n_col, col)
    before = choose([r[...] for r in col_refs], col_prev).astype(F32)
    after = choose([r[...] for r in col_refs], col_next).astype(F32)
    edge_list = [r[at : at + count].astype(F32) for r in row_refs]
    edge_prev = choose(edge_list, row ^ lax.rem(row + n_row - 1, n_row)) if n_row > 2 else edge_list[1]
    edge_next = choose(edge_list, row ^ lax.rem(row + 1, n_row)) if n_row > 2 else edge_list[1]
    row_prev, row_next = ring_pick(n_row, row)
    diag = [r[...].astype(F32) for r in diag_refs]

    def diag_of(row_which, col_which):
        lines = [
            choose(diag[m * col_moves : (m + 1) * col_moves], col_which) for m in range(row_moves)
        ]
        return choose(lines, row_which)

    corner = {
        (0, -1): diag_of(row_prev, col_prev),
        (0, 1): diag_of(row_prev, col_next),
        (1, -1): diag_of(row_next, col_prev),
        (1, 1): diag_of(row_next, col_next),
    }
    lane = lax.broadcasted_iota(jnp.int32, (ROWS, wy), 1)
    gap = jnp.zeros((ROWS - wx - 4, wy), F32)
    strips = jnp.zeros((ROWS, wy), F32)
    layers = depth + 4
    for c in range(2):
        for layer in range(layers):
            z = layer - 2
            if z < 0:
                source, plane, low, high = before, depth + z, corner[0, -1], corner[1, -1]
            elif z >= depth:
                source, plane, low, high = after, z - depth, corner[0, 1], corner[1, 1]
            else:
                source, plane, low, high = None, z, edge_prev, edge_next
            where = c * depth + plane
            if source is None:
                body = own[plane][c]
            else:
                body = source[where * wx : (where + 1) * wx]
            tail = jnp.concatenate(
                [high[where * 4 : where * 4 + 2], gap, low[where * 4 + 2 : where * 4 + 4]], axis=0
            )
            tile = jnp.concatenate([body, tail], axis=0)
            group = c * layers + layer
            dens_ref[group] = tile
            at_lane = 8 * group
            moved = pltpu.roll(tile, (at_lane + 2) % wy, 1)
            strips = jnp.where((lane >= at_lane) & (lane < at_lane + 4), moved, strips)
    strips = strips + pltpu.roll(strips, 4, 1)
    lanes_ref[...] = strips
    at = depth * full_x
    pad = jnp.zeros((80 - ROWS, wy), F32)
    msg_ref[at : at + 80] = jnp.concatenate([strips, pad], axis=0).astype(BF16)
    msg_ref[at + 80 : at + 96] = marks.astype(BF16)


def turn(tile, shift, axis):
    shift = shift % tile.shape[axis]
    return tile if shift == 0 else pltpu.roll(tile, shift, axis)


def pull_of(below, here, above):
    around = below + above
    line_y = turn(here, -1, 1) + turn(here, 1, 1)
    line_x = turn(here, -1, 0) + turn(here, 1, 0)
    flat = 2.0 * here + around
    mix = flat + line_y
    pull_x = turn(mix, -1, 0) - turn(mix, 1, 0)
    mix = flat + line_x
    pull_y = turn(mix, -1, 1) - turn(mix, 1, 1)
    gap = above - below
    pull_z = 2.0 * gap + turn(gap, -1, 0) + turn(gap, 1, 0) + turn(gap, -1, 1) + turn(gap, 1, 1)
    return pull_x, pull_y, pull_z


def relax_terms(density, velocity):
    vx, vy, vz = velocity
    squared = vx * vx + vy * vy + vz * vz
    rest = density * (1.0 - 1.875 * squared)
    terms = [WEIGHTS[0] * rest]
    for number in range(1, 19, 2):
        offsets = LATTICE[number]
        projected = None
        for axis in range(3):
            if offsets[axis]:
                part = velocity[axis] if offsets[axis] > 0 else -velocity[axis]
                projected = part if projected is None else projected + part
        weighted = density * projected
        even = WEIGHTS[number] * (rest + 5.625 * (weighted * projected))
        odd = (WEIGHTS[number] * 3.75) * weighted
        terms += [even + odd, even - odd]
    return terms


def cells_kernel(dens_ref, out_ref):
    _, depth, wx, _ = out_ref.shape
    layers = depth + 4
    scale = -1.6 / 36.0
    for layer in range(1, layers - 1):
        for c in range(2):
            other = (1 - c) * layers + layer
            pulls = pull_of(dens_ref[other - 1], dens_ref[other], dens_ref[other + 1])
            velocity = [scale * p for p in pulls]
            terms = relax_terms(dens_ref[c * layers + layer], velocity)
            for number in range(19):
                cx, cy, cz = LATTICE[number]
                z = layer - 2 + cz
                if 0 <= z < depth:
                    tile = turn(turn(terms[number], cx, 0), cy, 1)
                    out_ref[c * 19 + number, z] = tile[:wx]


def final_kernel(n_sec, width, msg_own_ref, *refs):
    msg_refs = [msg_own_ref] + list(refs[: n_sec - 1])
    (lanes_ref, cells_ref, table_ref, hi_ref, lo_ref, mult_ref, counts_ref, low_ref, put_row_ref,
     put_col_ref, spread_ref, out_ref, spec_ref, lhs_ref, mark_ref, quant_ref) = refs[n_sec - 1 :]
    _, depth, wx, wy = out_ref.shape
    layers = depth + 4
    sec = lax.axis_index("sec")
    half_y = table_ref.shape[1] // 2 - 128
    lanes = half_y + 128
    full_y = table_ref.shape[0]
    full_x = lhs_ref.shape[0] // depth
    half_x = full_x // 2
    hrows = half_x + 8
    at = depth * full_x

    for k in range(n_sec):
        start = pl.multiple_of((sec ^ k) * wy, wy)
        lhs_ref[:, pl.ds(start, wy)] = msg_refs[k][:at]
        mark_ref[sec ^ k] = msg_refs[k][at + 80 : at + 96].astype(F32)
    transform = jnp.dot(lhs_ref[...], table_ref[...], preferred_element_type=F32)
    marks = jnp.concatenate(
        [mark_ref[s][g : g + 1] for s in range(n_sec) for g in range(width // 128)], axis=1
    )
    nudge = marks - low_ref[...]
    nudges = jnp.dot(
        (put_row_ref[...] * nudge).astype(BF16), put_col_ref[...], preferred_element_type=F32
    )
    plus, minus = nudges[:hrows], nudges[hrows:]
    mult = mult_ref[...]
    row_zero = lax.broadcasted_iota(jnp.int32, (half_x, lanes), 0) == 0
    rest = jnp.zeros((7, lanes), F32)
    slot = 0
    for z in range(depth):
        real = transform[z * full_x : z * full_x + half_x]
        imag = transform[z * full_x + half_x : (z + 1) * full_x]
        rc, rs = real[:, :lanes], real[:, lanes:]
        ic, is_ = imag[:, :lanes], imag[:, lanes:]
        top = rc * rc + rs * rs
        low = ic * ic + is_ * is_
        both = top + low
        cross = 2.0 * (rc * is_ - ic * rs)
        total = mult * jnp.where(row_zero, top, 2.0 * both)
        total = jnp.concatenate([total, mult * low[0:1], rest], axis=0)
        shifted = plus[:half_x] * jnp.where(row_zero, top, both + cross) + minus[:half_x] * (
            both - cross
        )
        shifted = jnp.concatenate([shifted, plus[half_x : half_x + 1] * low[0:1], rest], axis=0)
        for value in (total, shifted):
            head = value.astype(BF16).astype(F32)
            quant_ref[slot] = head
            quant_ref[slot + 1] = value - head
            slot += 2
    quant_ref[slot] = plus + minus
    slots = slot + 1

    digit = lax.broadcasted_iota(jnp.int32, (LO, lanes), 0).astype(F32)

    def add_rows(step, acc):
        start = pl.multiple_of(step * 8, 8)
        hi8 = hi_ref[pl.ds(start, 8)]
        lo8 = lo_ref[pl.ds(start, 8)]
        q8 = [quant_ref[q, pl.ds(start, 8)] for q in range(slots)]
        left, right = [], []
        for r in range(8):
            mask = hi8[r : r + 1] == digit
            right.append(jnp.where(lo8[r : r + 1] == digit, F32(1.0), F32(0.0)).astype(BF16))
            left.append(
                jnp.concatenate(
                    [jnp.where(mask, q[r : r + 1], F32(0.0)).astype(BF16) for q in q8], axis=0
                )
            )
        return acc + lax.dot_general(
            jnp.concatenate(left, axis=1),
            jnp.concatenate(right, axis=1),
            (((1,), (1,)), ((), ())),
            preferred_element_type=F32,
        )

    acc = lax.fori_loop(0, hrows // 8, add_rows, jnp.zeros((slots * LO, LO), F32))
    wide = lax.dot_general(
        acc, spread_ref[...], (((1,), (0,)), ((), ())),
        precision=lax.Precision.HIGHEST, preferred_element_type=F32,
    )
    at_hi = lax.broadcasted_iota(jnp.int32, (LO, NSHELL), 1) // LO
    keep = at_hi == lax.broadcasted_iota(jnp.int32, (LO, NSHELL), 0)

    def line(q):
        return jnp.sum(
            jnp.where(keep, wide[q * LO : (q + 1) * LO], 0.0), axis=0, keepdims=True
        )

    def moved(value):
        return pltpu.roll(jnp.broadcast_to(value, (8, NSHELL)), 1, 1)[0:1] - value

    counts = counts_ref[...] + moved(line(slots - 1))
    norm = counts * float(full_x * full_y)
    spectrum = [
        (line(4 * z) + line(4 * z + 1) + moved(line(4 * z + 2) + line(4 * z + 3))) / norm
        for z in range(depth)
    ]
    spec_ref[...] = jnp.concatenate(spectrum, axis=0)

    index = sec
    prev_k = index ^ lax.rem(index + n_sec - 1, n_sec)
    next_k = index ^ lax.rem(index + 1, n_sec)
    strips = [r[at : at + 80].astype(F32)[:ROWS] for r in msg_refs]
    place = lax.rem(lax.broadcasted_iota(jnp.int32, (ROWS, wy), 1), 8)
    tile = jnp.where(
        place < 2,
        choose(strips, prev_k),
        jnp.where(place >= 6, choose(strips, next_k), lanes_ref[...]),
    )
    pulls = pull_of(turn(tile, 8, 1), tile, turn(tile, -8, 1))
    span = 8 * layers
    first = lax.broadcasted_iota(jnp.int32, (ROWS, wy), 1) < span
    scale = -1.6 / 36.0
    velocity = [scale * jnp.where(first, turn(p, -span, 1), turn(p, span, 1)) for p in pulls]
    terms = relax_terms(tile, velocity)
    lane = lax.broadcasted_iota(jnp.int32, (wx, wy), 1)
    for number in range(19):
        cx, cy, cz = LATTICE[number]
        term = turn(terms[number], cx, 0)[:wx]
        if cy == 0:
            term = jnp.where(place[:wx] == 1, turn(term, -4, 1), term)
            mask = (lane == 0) | (lane == wy - 1)
        else:
            mask = lane < 2 if cy > 0 else lane >= wy - 2
        for c in range(2):
            for z in range(depth):
                group = 8 * (c * layers + 2 + z - cz)
                back = {1: group + 1, -1: group + 5 - (wy - 2), 0: group + 2}[cy]
                q = c * 19 + number
                out_ref[q, z] = jnp.where(mask, turn(term, -back, 1), cells_ref[q, z])


def call(kernel, outs, scratch=(), flops=0, moved=0):
    return pl.pallas_call(
        kernel,
        out_shape=outs,
        scratch_shapes=list(scratch),
        compiler_params=pltpu.CompilerParams(vmem_limit_bytes=48 * 1024 * 1024),
        cost_estimate=pl.CostEstimate(flops=flops, bytes_accessed=moved, transcendentals=0),
    )


def on_device(n_sec, n_row, n_col, labels, jitter, shells):
    depth, wx, wy = labels.shape
    full_x, full_y = wx * n_row, wy * n_sec
    tables = make_tables(full_x, full_y, n_row, n_sec, wx, wy)
    width = tables["width"]
    layers = depth + 4
    count = 8 * depth
    shape = jax.ShapeDtypeStruct

    col_msg, row_msg, edge_msg = call(
        functools.partial(pack_kernel, n_sec),
        [
            shape((2 * depth * wx, wy), BF16),
            shape((depth * wx + count + 16, wy), BF16),
            shape((count, wy), BF16),
        ],
    )(labels, jitter, shells, tables["take_row"], tables["take_col"])

    col_got = [lax.ppermute(col_msg, "col", m) for m in ring_moves(n_col)]
    row_got = [lax.ppermute(row_msg, "row", xor_pairs(n_row, k)) for k in range(1, n_row)]
    diag_got = [
        lax.ppermute(edge_msg, ("row", "col"), pair_product(a, b, n_col))
        for a in ring_moves(n_row)
        for b in ring_moves(n_col)
    ]

    msg_rows = depth * full_x + 96
    msg, dens, strips = call(
        functools.partial(middle_kernel, n_row, n_col),
        [
            shape((msg_rows, wy), BF16),
            shape((2 * layers, ROWS, wy), F32),
            shape((ROWS, wy), F32),
        ],
    )(labels, jitter, *col_got, row_msg, *row_got, *diag_got, tables["table_x"])

    sec_got = [lax.ppermute(msg, "sec", xor_pairs(n_sec, k)) for k in range(1, n_sec)]

    cells = call(
        cells_kernel,
        shape((38, depth, wx, wy), F32),
        flops=38 * depth * wx * wy * 40,
        moved=4 * 38 * depth * wx * wy,
    )(dens)

    hrows, lanes = full_x // 2 + 8, full_y // 2 + 128
    populations, spectrum = call(
        functools.partial(final_kernel, n_sec, width),
        [shape((38, depth, wx, wy), F32), shape((depth, NSHELL), F32)],
        [
            pltpu.VMEM((depth * full_x, full_y), BF16),
            pltpu.VMEM((n_sec, 16, 128), F32),
            pltpu.VMEM((4 * depth + 1, hrows, lanes), F32),
        ],
    )(
        msg, *sec_got, strips, cells, tables["table_y"], tables["hi"], tables["lo"],
        tables["mult_y"], tables["counts"], tables["low"], tables["put_row"], tables["put_col"],
        tables["spread"],
    )
    return populations, spectrum


def solution(mesh):
    in_specs = (P("col", "row", "sec"), P(None, "col", "row", "sec"), P("row", "sec"))
    out_specs = (P(None, "col", "row", "sec"), P("col", None))
    sizes = [mesh.shape[name] for name in ("sec", "row", "col")]
    return jax.shard_map(
        functools.partial(on_device, *sizes),
        mesh=mesh,
        in_specs=in_specs,
        out_specs=out_specs,
        check_vma=False,
    )
```

```python
import functools
import math

import jax
import jax.numpy as jnp
import ml_dtypes
import numpy as np
from jax import lax
from jax.experimental import pallas as pl
from jax.experimental.pallas import tpu as pltpu
from jax.sharding import PartitionSpec as P

NSHELL = 256
UNUSED = -(1 << 20)
TOP = 40
ROWS = 72
F32 = jnp.float32
BF16 = jnp.bfloat16

LATTICE = (
    (0, 0, 0),
    (1, 0, 0),
    (-1, 0, 0),
    (0, 1, 0),
    (0, -1, 0),
    (0, 0, 1),
    (0, 0, -1),
    (1, 1, 0),
    (-1, -1, 0),
    (1, -1, 0),
    (-1, 1, 0),
    (1, 0, 1),
    (-1, 0, -1),
    (1, 0, -1),
    (-1, 0, 1),
    (0, 1, 1),
    (0, -1, -1),
    (0, 1, -1),
    (0, -1, 1),
)
WEIGHTS = (1.0 / 3.0,) + (1.0 / 18.0,) * 6 + (1.0 / 36.0,) * 12


def xor_pairs(count, bits):
    return [(i, i ^ bits) for i in range(count)]


def shift_pairs(count, step):
    return [(i, (i + step) % count) for i in range(count)]


def ring_moves(count):
    if count == 2:
        return [xor_pairs(2, 1)]
    if count == 4:
        return [xor_pairs(4, 1), xor_pairs(4, 3)]
    return [shift_pairs(count, 1), shift_pairs(count, -1)]


def ring_pick(count, index):
    if count == 2:
        return 0, 0
    if count == 4:
        odd = lax.rem(index, 2)
        return 1 - odd, odd
    return 0, 1


def pair_product(first, second, count_second):
    return [
        (a * count_second + b, c * count_second + d) for a, c in first for b, d in second
    ]


def whole(rows):
    return 16 * (-(-rows // 16))


def choose(items, which):
    if isinstance(which, int):
        return items[which]
    value = items[0]
    for number in range(1, len(items)):
        value = jnp.where(which == number, items[number], value)
    return value


def bf16_table(values):
    return np.asarray(values, np.float32).astype(ml_dtypes.bfloat16)


def angle_table(freq, pos, full):
    step = np.float32(2.0 * math.pi / full)
    return ((freq * pos) % full).astype(np.float32) * step


@functools.lru_cache(maxsize=None)
def make_tables(full_x, full_y, n_row, n_sec, wx, wy):
    half_x, half_y = full_x // 2, full_y // 2
    lanes = half_y + 128
    freq_y = np.arange(lanes)[None, :]
    angles = angle_table(np.arange(full_y)[:, None], freq_y, full_y)
    live = freq_y <= half_y
    table_y = np.concatenate([np.cos(angles) * live, np.sin(angles) * live], 1)
    hrows = half_x + 8
    radius = np.arange(hrows)[:, None] ** 2 + np.arange(lanes)[None, :] ** 2
    base = np.minimum(np.floor(np.sqrt(radius.astype(np.float64))).astype(np.int64), NSHELL - 1)
    valid = (np.arange(hrows)[:, None] <= half_x) & (np.arange(lanes)[None, :] <= half_y)
    move = np.where(valid, base - np.arange(lanes)[None, :], UNUSED)
    mult_y = np.where(freq_y > half_y, 0, np.where((freq_y == 0) | (freq_y == half_y), 1, 2))
    signed_x = np.arange(full_x)
    signed_x = np.where(signed_x < half_x, signed_x, signed_x - full_x)
    signed_y = np.arange(full_y)
    signed_y = np.where(signed_y < half_y, signed_y, signed_y - full_y)
    square = signed_x[:, None] ** 2 + signed_y[None, :] ** 2
    root = np.floor(np.sqrt(square + 1.0) + 1e-9).astype(np.int64)
    special = (root * root == square + 1) & (root < NSHELL) & (square > 0)
    low_label = np.minimum(np.floor(np.sqrt(square.astype(np.float64))), NSHELL - 1)
    counts = np.bincount(low_label.astype(np.int64).ravel(), minlength=NSHELL)
    rank = np.zeros(special.shape, np.int64)
    for r in range(n_row):
        rows = special[r * wx : (r + 1) * wx]
        rank[r * wx : (r + 1) * wx] = np.cumsum(rows, axis=0) - rows
    per = int(rank[special].max()) + 1
    section = 8 * (-(-(n_row * per) // 8))
    total = 128 * (-(-int(special.sum()) // 128))
    put = np.zeros((n_row * per, total))
    lanes_of = np.zeros((total, full_y))
    mark_row = np.zeros((2, hrows, total))
    mark_col = np.zeros((lanes, total))
    step = np.zeros((total, NSHELL))
    for entry, (kx, ky) in enumerate(np.argwhere(special).tolist()):
        ax, ay = abs(int(signed_x[kx])), abs(int(signed_y[ky]))
        same = int(signed_x[kx]) * int(signed_y[ky]) >= 0 or ax == half_x or ay == half_y
        put[kx // wx * per + rank[kx, ky], entry] = 1
        lanes_of[entry, ky] = 1
        mark_row[0 if same else 1, ax, entry] = 1
        mark_col[ay, entry] = 1
        step[entry, root[kx, ky]] += 1
        step[entry, root[kx, ky] - 1] -= 1
    return dict(
        per=per,
        section=section,
        table_y=bf16_table(table_y),
        move=move,
        mult_y=mult_y.astype(np.float32),
        counts=counts.astype(np.float32)[None, :],
        put=np.asarray(put, np.float32),
        lanes_of=bf16_table(lanes_of.T),
        mark_row=np.asarray(mark_row, np.float32),
        mark_col=bf16_table(mark_col),
        step=np.asarray(step, np.float32),
    )


def x_table(n_row, wx):
    full_x = n_row * wx
    half_x = full_x // 2
    freq = lax.broadcasted_iota(jnp.int32, (n_row, full_x, wx), 1)
    block = lax.broadcasted_iota(jnp.int32, (n_row, full_x, wx), 0) ^ lax.axis_index("row")
    pos = block * wx + lax.broadcasted_iota(jnp.int32, (n_row, full_x, wx), 2)
    is_cos = freq <= half_x
    freq = jnp.where(is_cos, freq, freq - half_x)
    angles = (freq * pos % full_x).astype(F32) * (2.0 * math.pi / full_x)
    return jnp.where(is_cos, jnp.cos(angles), -jnp.sin(angles)).astype(BF16)


def pack_kernel(n_row, n_sec, per, own_ref, shells_ref, col_ref, row_ref, edge_ref):
    _, depth, wx, wy = own_ref.shape
    edges = []
    densities = [[own_ref[c, z] for z in range(depth)] for c in range(2)]
    for c in range(2):
        for z in range(depth):
            tile = densities[c][z]
            at = (c * depth + z) * wx
            col_ref[at : at + wx] = tile.astype(BF16)
            edges += [tile[0:2], tile[wx - 2 : wx]]
    for z in range(depth):
        row_ref[z * wx : (z + 1) * wx] = (densities[0][z] - densities[1][z]).astype(BF16)
    edge = jnp.concatenate(edges, axis=0).astype(BF16)
    edge_ref[...] = edge
    at = depth * wx
    count = edge.shape[0]
    row_ref[at : at + count] = edge

    row, sec = lax.axis_index("row"), lax.axis_index("sec")
    square, root = shell_root(row * wx, sec * wy, wx * n_row, wy * n_sec, wx, wy)
    special = (root * root == square + 1.0) & (root < NSHELL) & (square > 0.0)
    nudge = jnp.where(special, shells_ref[...].astype(F32) - (root - 1.0), 0.0)
    one = jnp.where(special, F32(1.0), F32(0.0)).astype(BF16)
    down = lax.broadcasted_iota(jnp.int32, (wx, wx), 0)
    above = (lax.broadcasted_iota(jnp.int32, (wx, wx), 1) < down).astype(F32).astype(BF16)
    rank = jnp.dot(above, one, preferred_element_type=F32)
    section = row_ref.shape[0] - at - count
    line = lax.broadcasted_iota(jnp.int32, (section, wy), 0)
    marks = jnp.zeros((section, wy), F32)
    for number in range(per):
        found = jnp.sum(jnp.where(rank == number, nudge, 0.0), axis=0, keepdims=True)
        marks = jnp.where(line == row * per + number, found, marks)
    row_ref[at + count :] = marks.astype(BF16)


def shell_root(first_x, first_y, full_x, full_y, wx, wy):
    kx = first_x + lax.broadcasted_iota(jnp.int32, (wx, wy), 0)
    ky = first_y + lax.broadcasted_iota(jnp.int32, (wx, wy), 1)
    kx = jnp.where(kx < full_x // 2, kx, kx - full_x)
    ky = jnp.where(ky < full_y // 2, ky, ky - full_y)
    square = (kx * kx + ky * ky).astype(F32)
    return square, jnp.floor(jnp.sqrt(square + 1.0) + 0.5)


def middle_kernel(n_row, n_col, section, own_ref, *refs):
    _, depth, wx, wy = own_ref.shape
    col_moves, row_moves = len(ring_moves(n_col)), len(ring_moves(n_row))
    col_refs, refs = refs[:col_moves], refs[col_moves:]
    row_refs, refs = refs[:n_row], refs[n_row:]
    diag_refs, refs = refs[: col_moves * row_moves], refs[col_moves * row_moves :]
    table_ref, msg_ref, short_ref, dens_ref, lanes_ref = refs
    row, col = lax.axis_index("row"), lax.axis_index("col")
    full_x = table_ref.shape[1]

    for z in range(depth):
        half = None
        for k in range(n_row):
            part = jnp.dot(
                table_ref[k],
                row_refs[k][z * wx : (z + 1) * wx],
                preferred_element_type=F32,
            )
            half = part if half is None else half + part
        half = half.astype(BF16)
        msg_ref[z * full_x : (z + 1) * full_x] = half
        short_ref[z * full_x : (z + 1) * full_x] = half

    at = depth * wx
    count = 8 * depth
    marks = sum(ref[at + count :].astype(F32) for ref in row_refs)[:section]

    col_prev, col_next = ring_pick(n_col, col)
    before = choose([r[...] for r in col_refs], col_prev).astype(F32)
    after = choose([r[...] for r in col_refs], col_next).astype(F32)
    edge_list = [r[at : at + count].astype(F32) for r in row_refs]
    edge_prev = choose(edge_list, row ^ lax.rem(row + n_row - 1, n_row)) if n_row > 2 else edge_list[1]
    edge_next = choose(edge_list, row ^ lax.rem(row + 1, n_row)) if n_row > 2 else edge_list[1]
    row_prev, row_next = ring_pick(n_row, row)
    diag = [r[...].astype(F32) for r in diag_refs]

    def diag_of(row_which, col_which):
        lines = [
            choose(diag[m * col_moves : (m + 1) * col_moves], col_which) for m in range(row_moves)
        ]
        return choose(lines, row_which)

    corner = {
        (0, -1): diag_of(row_prev, col_prev),
        (0, 1): diag_of(row_prev, col_next),
        (1, -1): diag_of(row_next, col_prev),
        (1, 1): diag_of(row_next, col_next),
    }
    lane = lax.broadcasted_iota(jnp.int32, (ROWS, wy), 1)
    gap = jnp.zeros((ROWS - wx - 4, wy), F32)
    strips = jnp.zeros((ROWS, wy), F32)
    layers = depth + 4
    for c in range(2):
        for layer in range(layers):
            z = layer - 2
            if z < 0:
                source, plane, low, high = before, depth + z, corner[0, -1], corner[1, -1]
            elif z >= depth:
                source, plane, low, high = after, z - depth, corner[0, 1], corner[1, 1]
            else:
                source, plane, low, high = None, z, edge_prev, edge_next
            where = c * depth + plane
            if source is None:
                body = own_ref[c, plane]
            else:
                body = source[where * wx : (where + 1) * wx]
            tail = jnp.concatenate(
                [high[where * 4 : where * 4 + 2], gap, low[where * 4 + 2 : where * 4 + 4]], axis=0
            )
            tile = jnp.concatenate([body, tail], axis=0)
            group = c * layers + layer
            dens_ref[group] = tile
            at_lane = 8 * group
            moved = pltpu.roll(tile, (at_lane + 2) % wy, 1)
            strips = jnp.where((lane >= at_lane) & (lane < at_lane + 4), moved, strips)
    lanes_ref[...] = strips + pltpu.roll(strips, 4, 1)
    at = depth * full_x
    lower = jnp.concatenate([strips[TOP:], jnp.zeros((2 * TOP - ROWS, wy), F32)], axis=0)
    folded = strips[:TOP] + pltpu.roll(lower, 4, 1)
    for ref, parts in ((msg_ref, [marks, folded]), (short_ref, [marks])):
        missing = ref.shape[0] - at - sum(p.shape[0] for p in parts)
        if missing:
            parts = parts + [jnp.zeros((missing, wy), F32)]
        ref[at:] = jnp.concatenate(parts, axis=0).astype(BF16)


def turn(tile, shift, axis):
    shift = shift % tile.shape[axis]
    return tile if shift == 0 else pltpu.roll(tile, shift, axis)


def pull_of(below, here, above):
    around = below + above
    line_y = turn(here, -1, 1) + turn(here, 1, 1)
    line_x = turn(here, -1, 0) + turn(here, 1, 0)
    flat = 2.0 * here + around
    mix = flat + line_y
    pull_x = turn(mix, -1, 0) - turn(mix, 1, 0)
    mix = flat + line_x
    pull_y = turn(mix, -1, 1) - turn(mix, 1, 1)
    gap = above - below
    pull_z = 2.0 * gap + turn(gap, -1, 0) + turn(gap, 1, 0) + turn(gap, -1, 1) + turn(gap, 1, 1)
    return pull_x, pull_y, pull_z


def relax_terms(density, velocity):
    vx, vy, vz = velocity
    squared = vx * vx + vy * vy + vz * vz
    rest = density * (1.0 - 1.875 * squared)
    terms = [WEIGHTS[0] * rest]
    for number in range(1, 19, 2):
        offsets = LATTICE[number]
        projected = None
        for axis in range(3):
            if offsets[axis]:
                part = velocity[axis] if offsets[axis] > 0 else -velocity[axis]
                projected = part if projected is None else projected + part
        weighted = density * projected
        even = WEIGHTS[number] * (rest + 5.625 * (weighted * projected))
        odd = (WEIGHTS[number] * 3.75) * weighted
        terms += [even + odd, even - odd]
    return terms


def cells_kernel(dens_ref, out_ref):
    _, depth, wx, _ = out_ref.shape
    layers = depth + 4
    scale = -1.6 / 36.0
    for layer in range(1, layers - 1):
        for c in range(2):
            other = (1 - c) * layers + layer
            pulls = pull_of(dens_ref[other - 1], dens_ref[other], dens_ref[other + 1])
            velocity = [scale * p for p in pulls]
            terms = relax_terms(dens_ref[c * layers + layer], velocity)
            for number in range(19):
                cx, cy, cz = LATTICE[number]
                z = layer - 2 + cz
                if 0 <= z < depth:
                    tile = turn(turn(terms[number], cx, 0), cy, 1)
                    out_ref[c * 19 + number, z] = tile[:wx]


def set_ends(n_sec, start, at, msg_refs, lanes_ref, cells_ref, out_hbm, out_ref, sems):
    _, depth, wx, wy = out_ref.shape
    layers = depth + 4
    strips = [r[start:].astype(F32)[at - start :][:TOP] for r in msg_refs]
    index = lax.axis_index("sec")
    prev_which, next_which = ring_pick(n_sec, index)
    before, after = choose(strips, prev_which), choose(strips, next_which)
    rest = ROWS - TOP
    before = jnp.concatenate([before, turn(before, -4, 1)[:rest]], axis=0)
    after = jnp.concatenate([turn(after, 4, 1), after[:rest]], axis=0)
    place = lax.rem(lax.broadcasted_iota(jnp.int32, (ROWS, wy), 1), 8)
    tile = jnp.where(place < 2, before, jnp.where(place >= 6, after, lanes_ref[...]))
    pulls = pull_of(turn(tile, 8, 1), tile, turn(tile, -8, 1))
    span = 8 * layers
    first = lax.broadcasted_iota(jnp.int32, (ROWS, wy), 1) < span
    scale = -1.6 / 36.0
    velocity = [scale * jnp.where(first, turn(p, -span, 1), turn(p, span, 1)) for p in pulls]
    terms = relax_terms(tile, velocity)
    lane = lax.broadcasted_iota(jnp.int32, (wx, wy), 1)
    copies = []
    for number in range(19):
        cx, cy, cz = LATTICE[number]
        term = turn(terms[number], cx, 0)[:wx]
        if cy == 0:
            term = jnp.where(place[:wx] == 1, turn(term, -4, 1), term)
            mask = (lane == 0) | (lane == wy - 1)
        else:
            mask = lane < 2 if cy > 0 else lane >= wy - 2
        for c in range(2):
            for z in range(depth):
                group = 8 * (c * layers + 2 + z - cz)
                back = {1: group + 1, -1: group + 5 - (wy - 2), 0: group + 2}[cy]
                q = c * 19 + number
                out_ref[q, z] = jnp.where(mask, turn(term, -back, 1), cells_ref[q, z])
            copy = pltpu.make_async_copy(out_ref.at[q], out_hbm.at[q], sems.at[q])
            copy.start()
            copies.append(copy)
    return copies


def final_kernel(n_sec, section, move, msg_own_ref, *refs):
    msg_refs = [msg_own_ref] + list(refs[: n_sec - 1])
    strips_ref, cells_ref = refs[n_sec - 1 : n_sec + 1]
    refs = refs[n_sec + 1 :]
    (table_ref, move_ref, mult_ref, counts_ref, put_ref, lanes_ref, row_ref, col_ref, step_ref,
     out_hbm, spec_ref, lhs_ref, mark_ref, part_ref, out_ref, sems) = refs
    depth = spec_ref.shape[0]
    sec = lax.axis_index("sec")
    full_y, lanes = table_ref.shape[0], table_ref.shape[1] // 2
    wy = full_y // n_sec
    full_x = lhs_ref.shape[0] // depth
    half_x = full_x // 2
    hrows = half_x + 8
    at = depth * full_x
    lines_used = put_ref.shape[0]
    ring = [msg_refs[move_[0][1]] for move_ in ring_moves(n_sec)]
    copies = set_ends(n_sec, at, at + section, ring, strips_ref, cells_ref, out_hbm, out_ref, sems)

    for k in range(n_sec):
        start = pl.multiple_of((sec ^ k) * wy, wy)
        lhs_ref[:, pl.ds(start, wy)] = msg_refs[k][:at]
        mark_ref[:, pl.ds(start, wy)] = msg_refs[k][at : at + mark_ref.shape[0]]
    transform = jnp.dot(lhs_ref[...], table_ref[...], preferred_element_type=F32)

    found = jnp.dot(mark_ref[...], lanes_ref[...], preferred_element_type=F32)
    nudge = jnp.sum(found[:lines_used] * put_ref[...], axis=0, keepdims=True)

    mult = mult_ref[...]
    row_zero = lax.broadcasted_iota(jnp.int32, (half_x, lanes), 0) == 0
    rest = jnp.zeros((7, lanes), F32)
    picks = []
    for z in range(depth):
        real = transform[z * full_x : z * full_x + half_x]
        imag = transform[z * full_x + half_x : (z + 1) * full_x]
        rc, rs = real[:, :lanes], real[:, lanes:]
        ic, is_ = imag[:, :lanes], imag[:, lanes:]
        top = rc * rc + rs * rs
        low = ic * ic + is_ * is_
        both = top + low
        cross = 2.0 * (rc * is_ - ic * rs)
        part_ref[z, :half_x] = mult * jnp.where(row_zero, top, 2.0 * both)
        part_ref[z, half_x:] = jnp.concatenate([mult * low[0:1], rest], axis=0)
        plus = jnp.concatenate([jnp.where(row_zero, top, both + cross), low[0:1], rest], axis=0)
        minus = jnp.concatenate([both - cross, low[0:1], rest], axis=0)
        value = 0.0
        for number, power in enumerate((plus, minus)):
            head = power.astype(BF16)
            tail = (power - head.astype(F32)).astype(BF16)
            found = jnp.dot(head, col_ref[...], preferred_element_type=F32) + jnp.dot(
                tail, col_ref[...], preferred_element_type=F32
            )
            value = value + jnp.sum(found * row_ref[number], axis=0, keepdims=True)
        picks.append(value)
    picks.append(jnp.ones_like(picks[0]))
    picks.append(jnp.zeros((8 - len(picks), picks[0].shape[1]), F32))
    moved = lax.dot_general(
        jnp.concatenate(picks, axis=0) * nudge, step_ref[...], (((1,), (0,)), ((), ())),
        precision=lax.Precision.HIGHEST, preferred_element_type=F32,
    )

    tiles = NSHELL // 128
    lane = lax.broadcasted_iota(jnp.int32, (8, 128), 1)
    sums = [[jnp.zeros((8, 128), F32) for _ in range(tiles)] for _ in range(depth)]
    for tile in range(lanes // 128):
        block = move[:, tile * 128 : (tile + 1) * 128]
        at_lanes = slice(tile * 128, (tile + 1) * 128)
        for value in np.unique(block):
            if value == UNUSED:
                continue
            value = int(value)
            totals = [None] * depth
            for group in range(hrows // 8):
                if not (block[group * 8 : group * 8 + 8] == value).any():
                    continue
                rows = slice(group * 8, group * 8 + 8)
                same = move_ref[rows, at_lanes] == value
                for z in range(depth):
                    term = jnp.where(same, part_ref[z, rows, at_lanes], 0.0)
                    totals[z] = term if totals[z] is None else totals[z] + term
            shift = value % 128
            goal = tile + value // 128
            for z in range(depth):
                total = turn(totals[z], shift, 1)
                if 0 <= goal < tiles:
                    sums[z][goal] += jnp.where(lane >= shift, total, 0.0)
                if shift and 0 <= goal + 1 < tiles:
                    sums[z][goal + 1] += jnp.where(lane < shift, total, 0.0)
    norm = (counts_ref[...] + moved[depth : depth + 1]) * float(full_x * full_y)
    lines = []
    for z in range(depth):
        line = jnp.sum(jnp.concatenate(sums[z], axis=1), axis=0, keepdims=True)
        lines.append((line + moved[z : z + 1]) / norm)
    spec_ref[...] = jnp.concatenate(lines, axis=0)
    for copy in copies:
        copy.wait()


def call(kernel, outs, scratch=(), flops=0, moved=0, limit=48 << 20, **specs):
    return pl.pallas_call(
        kernel,
        out_shape=outs,
        scratch_shapes=list(scratch),
        compiler_params=pltpu.CompilerParams(vmem_limit_bytes=limit),
        cost_estimate=pl.CostEstimate(flops=flops, bytes_accessed=moved, transcendentals=0),
        **specs,
    )


def on_device(n_sec, n_row, n_col, labels, jitter, shells):
    depth, wx, wy = labels.shape
    full_x, full_y = wx * n_row, wy * n_sec
    tables = make_tables(full_x, full_y, n_row, n_sec, wx, wy)
    per, section = tables["per"], tables["section"]
    layers = depth + 4
    count = 8 * depth
    shape = jax.ShapeDtypeStruct

    other = lax.broadcasted_iota(jnp.int32, jitter.shape, 0)
    own = jnp.where((labels[None] ^ other) == 1, F32(1.0), F32(0.2)) * jitter
    col_msg, row_msg, edge_msg = call(
        functools.partial(pack_kernel, n_row, n_sec, per),
        [
            shape((2 * depth * wx, wy), BF16),
            shape((depth * wx + count + whole(section), wy), BF16),
            shape((count, wy), BF16),
        ],
    )(own, shells)

    col_got = [lax.ppermute(col_msg, "col", m) for m in ring_moves(n_col)]
    row_got = [lax.ppermute(row_msg, "row", xor_pairs(n_row, k)) for k in range(1, n_row)]
    diag_got = [
        lax.ppermute(edge_msg, ("row", "col"), pair_product(a, b, n_col))
        for a in ring_moves(n_row)
        for b in ring_moves(n_col)
    ]

    at = depth * full_x
    msg, short, dens, lanes_own = call(
        functools.partial(middle_kernel, n_row, n_col, section),
        [
            shape((at + whole(section + TOP), wy), BF16),
            shape((at + whole(section), wy), BF16),
            shape((2 * layers, ROWS, wy), F32),
            shape((ROWS, wy), F32),
        ],
    )(own, *col_got, row_msg, *row_got, *diag_got, x_table(n_row, wx))

    ring = ring_moves(n_sec)
    sec_got = []
    for k in range(1, n_sec):
        move = xor_pairs(n_sec, k)
        sec_got.append(lax.ppermute(msg if move in ring else short, "sec", move))

    cells = call(
        cells_kernel,
        shape((38, depth, wx, wy), F32),
        flops=38 * depth * wx * wy * 40,
        moved=4 * 38 * depth * wx * wy,
    )(dens)

    hrows, lanes = full_x // 2 + 8, full_y // 2 + 128
    names = ("mult_y", "counts", "put", "lanes_of", "mark_row", "mark_col", "step")
    return call(
        functools.partial(final_kernel, n_sec, section, tables["move"]),
        (shape((38, depth, wx, wy), F32), shape((depth, NSHELL), F32)),
        [
            pltpu.VMEM((depth * full_x, full_y), BF16),
            pltpu.VMEM((whole(section), full_y), BF16),
            pltpu.VMEM((depth, hrows, lanes), F32),
            pltpu.VMEM((38, depth, wx, wy), F32),
            pltpu.SemaphoreType.DMA((38,)),
        ],
        out_specs=(
            pl.BlockSpec(memory_space=pltpu.HBM),
            pl.BlockSpec(memory_space=pltpu.VMEM),
        ),
    )(msg, *sec_got, lanes_own, cells, tables["table_y"], tables["move"].astype(np.int32),
      *[tables[name] for name in names])


def solution(mesh):
    in_specs = (P("col", "row", "sec"), P(None, "col", "row", "sec"), P("row", "sec"))
    out_specs = (P(None, "col", "row", "sec"), P("col", None))
    sizes = [mesh.shape[name] for name in ("sec", "row", "col")]
    return jax.shard_map(
        functools.partial(on_device, *sizes),
        mesh=mesh,
        in_specs=in_specs,
        out_specs=out_specs,
        check_vma=False,
    )
```

```python
import functools
import math

import jax
import jax.numpy as jnp
import ml_dtypes
import numpy as np
from jax import lax
from jax.experimental import pallas as pl
from jax.experimental.pallas import tpu as pltpu
from jax.sharding import PartitionSpec as P

NSHELL = 256
UNUSED = -(1 << 20)
ENDS = (10, 19, 29, 38)
FIRST_ROUND = (("col", 0), ("diag", 0), ("row", 1), ("col", 1), ("diag", 1))
SWAPS = {4: (1, 3, 2)}
TOP = 40
ROWS = 72
F32 = jnp.float32
BF16 = jnp.bfloat16

LATTICE = (
    (0, 0, 0),
    (1, 0, 0),
    (-1, 0, 0),
    (0, 1, 0),
    (0, -1, 0),
    (0, 0, 1),
    (0, 0, -1),
    (1, 1, 0),
    (-1, -1, 0),
    (1, -1, 0),
    (-1, 1, 0),
    (1, 0, 1),
    (-1, 0, -1),
    (1, 0, -1),
    (-1, 0, 1),
    (0, 1, 1),
    (0, -1, -1),
    (0, 1, -1),
    (0, -1, 1),
)
WEIGHTS = (1.0 / 3.0,) + (1.0 / 18.0,) * 6 + (1.0 / 36.0,) * 12


def xor_pairs(count, bits):
    return [(i, i ^ bits) for i in range(count)]


def shift_pairs(count, step):
    return [(i, (i + step) % count) for i in range(count)]


def ring_moves(count):
    if count == 2:
        return [xor_pairs(2, 1)]
    if count == 4:
        return [xor_pairs(4, 1), xor_pairs(4, 3)]
    return [shift_pairs(count, 1), shift_pairs(count, -1)]


def ring_pick(count, index):
    if count == 2:
        return 0, 0
    if count == 4:
        odd = lax.rem(index, 2)
        return 1 - odd, odd
    return 0, 1


def swap_order(count):
    return SWAPS.get(count, tuple(range(1, count)))


def pair_product(first, second, count_second):
    return [
        (a * count_second + b, c * count_second + d) for a, c in first for b, d in second
    ]


def whole(rows):
    return 16 * (-(-rows // 16))


def choose(items, which):
    if isinstance(which, int):
        return items[which]
    value = items[0]
    for number in range(1, len(items)):
        value = jnp.where(which == number, items[number], value)
    return value


def bf16_table(values):
    return np.asarray(values, np.float32).astype(ml_dtypes.bfloat16)


def angle_table(freq, pos, full):
    step = np.float32(2.0 * math.pi / full)
    return ((freq * pos) % full).astype(np.float32) * step


@functools.lru_cache(maxsize=None)
def make_tables(full_x, full_y, n_row, n_sec, wx, wy):
    half_x, half_y = full_x // 2, full_y // 2
    lanes = half_y + 128
    freq_y = np.arange(lanes)[None, :]
    angles = angle_table(np.arange(full_y)[:, None], freq_y, full_y)
    live = freq_y <= half_y
    table_y = np.concatenate([np.cos(angles) * live, np.sin(angles) * live], 1)
    hrows = half_x + 8
    radius = np.arange(hrows)[:, None] ** 2 + np.arange(lanes)[None, :] ** 2
    base = np.minimum(np.floor(np.sqrt(radius.astype(np.float64))).astype(np.int64), NSHELL - 1)
    valid = (np.arange(hrows)[:, None] <= half_x) & (np.arange(lanes)[None, :] <= half_y)
    move = np.where(valid, base - np.arange(lanes)[None, :], UNUSED)
    mult_y = np.where(freq_y > half_y, 0, np.where((freq_y == 0) | (freq_y == half_y), 1, 2))
    signed_x = np.arange(full_x)
    signed_x = np.where(signed_x < half_x, signed_x, signed_x - full_x)
    signed_y = np.arange(full_y)
    signed_y = np.where(signed_y < half_y, signed_y, signed_y - full_y)
    square = signed_x[:, None] ** 2 + signed_y[None, :] ** 2
    root = np.floor(np.sqrt(square + 1.0) + 1e-9).astype(np.int64)
    special = (root * root == square + 1) & (root < NSHELL) & (square > 0)
    low_label = np.minimum(np.floor(np.sqrt(square.astype(np.float64))), NSHELL - 1)
    counts = np.bincount(low_label.astype(np.int64).ravel(), minlength=NSHELL)
    rank = np.zeros(special.shape, np.int64)
    for r in range(n_row):
        rows = special[r * wx : (r + 1) * wx]
        rank[r * wx : (r + 1) * wx] = np.cumsum(rows, axis=0) - rows
    per = int(rank[special].max()) + 1
    section = 8 * (-(-(n_row * per) // 8))
    total = 128 * (-(-int(special.sum()) // 128))
    put = np.zeros((n_row * per, total))
    lanes_of = np.zeros((total, full_y))
    mark_row = np.zeros((2, hrows, total))
    mark_col = np.zeros((lanes, total))
    step = np.zeros((total, NSHELL))
    for entry, (kx, ky) in enumerate(np.argwhere(special).tolist()):
        ax, ay = abs(int(signed_x[kx])), abs(int(signed_y[ky]))
        same = int(signed_x[kx]) * int(signed_y[ky]) >= 0 or ax == half_x or ay == half_y
        put[kx // wx * per + rank[kx, ky], entry] = 1
        lanes_of[entry, ky] = 1
        mark_row[0 if same else 1, ax, entry] = 1
        mark_col[ay, entry] = 1
        step[entry, root[kx, ky]] += 1
        step[entry, root[kx, ky] - 1] -= 1
    return dict(
        per=per,
        section=section,
        table_y=bf16_table(table_y),
        move=move,
        mult_y=mult_y.astype(np.float32),
        counts=counts.astype(np.float32)[None, :],
        put=np.asarray(put, np.float32),
        lanes_of=bf16_table(lanes_of.T),
        mark_row=np.asarray(mark_row, np.float32),
        mark_col=bf16_table(mark_col),
        step=np.asarray(step, np.float32),
    )


def turn_table(steps, full):
    quarter = (4 * steps + full // 2) // full
    rest = (steps - quarter * (full // 4)).astype(F32) * F32(2.0 * math.pi / full)
    square = rest * rest
    cos, sin = F32(1.0), F32(1.0)
    for order in (8, 6, 4, 2):
        cos = 1.0 - square * cos * F32(1.0 / (order * (order - 1)))
        sin = 1.0 - square * sin * F32(1.0 / (order * (order + 1)))
    sin = sin * rest
    odd = quarter % 2 == 1
    cos, sin = jnp.where(odd, sin, cos), jnp.where(odd, cos, sin)
    cos = jnp.where((quarter == 1) | (quarter == 2), -cos, cos)
    return cos, jnp.where((quarter == 2) | (quarter == 3), -sin, sin)


def x_table(row, n_row, wx):
    full_x = n_row * wx
    half_x = full_x // 2
    freq = lax.broadcasted_iota(jnp.int32, (full_x, full_x), 0)
    lane = lax.broadcasted_iota(jnp.int32, (full_x, full_x), 1)
    pos = (lane // wx ^ row) * wx + lane % wx
    is_cos = freq <= half_x
    cos, sin = turn_table(jnp.where(is_cos, freq, freq - half_x) * pos % full_x, full_x)
    return jnp.where(is_cos, cos, -sin).astype(BF16)


def pack_kernel(n_row, n_sec, per, own_ref, col_ref, row_ref, edge_ref, table_ref):
    _, depth, wx, wy = own_ref.shape
    edges = []
    densities = [[own_ref[c, z] for z in range(depth)] for c in range(2)]
    for c in range(2):
        for z in range(depth):
            tile = densities[c][z]
            at = (c * depth + z) * wx
            col_ref[at : at + wx] = tile.astype(BF16)
            edges += [tile[0:2], tile[wx - 2 : wx]]
    for z in range(depth):
        row_ref[z * wx : (z + 1) * wx] = (densities[0][z] - densities[1][z]).astype(BF16)
    edge = jnp.concatenate(edges, axis=0).astype(BF16)
    edge_ref[...] = edge
    at = depth * wx
    count = edge.shape[0]
    row_ref[at : at + count] = edge

    table_ref[...] = x_table(lax.axis_index("row"), n_row, wx)

    row, sec = lax.axis_index("row"), lax.axis_index("sec")
    square, root = shell_root(row * wx, sec * wy, wx * n_row, wy * n_sec, wx, wy)
    special = (root * root == square + 1.0) & (root < NSHELL) & (square > 0.0)
    nudge = jnp.where(special, own_ref[2, 0] - (root - 1.0), 0.0)
    one = jnp.where(special, F32(1.0), F32(0.0)).astype(BF16)
    down = lax.broadcasted_iota(jnp.int32, (wx, wx), 0)
    above = (lax.broadcasted_iota(jnp.int32, (wx, wx), 1) < down).astype(F32).astype(BF16)
    rank = jnp.dot(above, one, preferred_element_type=F32)
    section = row_ref.shape[0] - at - count
    line = lax.broadcasted_iota(jnp.int32, (section, wy), 0)
    marks = jnp.zeros((section, wy), F32)
    for number in range(per):
        found = jnp.sum(jnp.where(rank == number, nudge, 0.0), axis=0, keepdims=True)
        marks = jnp.where(line == row * per + number, found, marks)
    row_ref[at + count :] = marks.astype(BF16)


def shell_root(first_x, first_y, full_x, full_y, wx, wy):
    kx = first_x + lax.broadcasted_iota(jnp.int32, (wx, wy), 0)
    ky = first_y + lax.broadcasted_iota(jnp.int32, (wx, wy), 1)
    kx = jnp.where(kx < full_x // 2, kx, kx - full_x)
    ky = jnp.where(ky < full_y // 2, ky, ky - full_y)
    square = (kx * kx + ky * ky).astype(F32)
    return square, jnp.floor(jnp.sqrt(square + 1.0) + 0.5)


def half_kernel(depth, wx, n_row, *refs):
    row_refs, table_ref, bulk_ref = refs[:n_row], refs[n_row], refs[n_row + 1]
    full_x = table_ref.shape[0]
    for z in range(depth):
        lines = jnp.concatenate([r[z * wx : (z + 1) * wx] for r in row_refs], axis=0)
        half = jnp.dot(table_ref[...], lines, preferred_element_type=F32)
        bulk_ref[z * full_x : (z + 1) * full_x] = half.astype(BF16)
    at = depth * wx + 8 * depth
    marks = sum(ref[at:].astype(F32) for ref in row_refs)
    bulk_ref[depth * full_x :] = marks.astype(BF16)


def middle_kernel(n_row, n_col, names, own_ref, row_ref, *refs):
    _, depth, wx, wy = own_ref.shape
    col_moves, row_moves = len(ring_moves(n_col)), len(ring_moves(n_row))
    by_name, refs = dict(zip(names, refs)), refs[len(names) :]
    msg_ref, dens_ref, lanes_ref = refs
    col_refs = [by_name["col", i] for i in range(col_moves)]
    row_refs = [row_ref] + [by_name["row", k] for k in range(1, n_row)]
    diag_refs = [by_name["diag", i] for i in range(col_moves * row_moves)]
    row, col = lax.axis_index("row"), lax.axis_index("col")
    at = depth * wx
    count = 8 * depth
    col_prev, col_next = ring_pick(n_col, col)
    before = choose([r[...].astype(F32) for r in col_refs], col_prev)
    after = choose([r[...].astype(F32) for r in col_refs], col_next)
    edge_list = [r[at : at + count].astype(F32) for r in row_refs]
    edge_prev = choose(edge_list, row ^ lax.rem(row + n_row - 1, n_row)) if n_row > 2 else edge_list[1]
    edge_next = choose(edge_list, row ^ lax.rem(row + 1, n_row)) if n_row > 2 else edge_list[1]
    row_prev, row_next = ring_pick(n_row, row)
    diag = [r[...].astype(F32) for r in diag_refs]

    def diag_of(row_which, col_which):
        lines = [
            choose(diag[m * col_moves : (m + 1) * col_moves], col_which) for m in range(row_moves)
        ]
        return choose(lines, row_which)

    corner = {
        (0, -1): diag_of(row_prev, col_prev),
        (0, 1): diag_of(row_prev, col_next),
        (1, -1): diag_of(row_next, col_prev),
        (1, 1): diag_of(row_next, col_next),
    }
    lane = lax.broadcasted_iota(jnp.int32, (ROWS, wy), 1)
    gap = jnp.zeros((ROWS - wx - 4, wy), F32)
    strips = jnp.zeros((ROWS, wy), F32)
    layers = depth + 4
    for c in range(2):
        for layer in range(layers):
            z = layer - 2
            if z < 0:
                source, plane, low, high = before, depth + z, corner[0, -1], corner[1, -1]
            elif z >= depth:
                source, plane, low, high = after, z - depth, corner[0, 1], corner[1, 1]
            else:
                source, plane, low, high = None, z, edge_prev, edge_next
            where = c * depth + plane
            if source is None:
                body = own_ref[c, plane]
            else:
                body = source[where * wx : (where + 1) * wx]
            tail = jnp.concatenate(
                [high[where * 4 : where * 4 + 2], gap, low[where * 4 + 2 : where * 4 + 4]], axis=0
            )
            tile = jnp.concatenate([body, tail], axis=0)
            group = c * layers + layer
            dens_ref[group] = tile
            at_lane = 8 * group
            moved = pltpu.roll(tile, (at_lane + 2) % wy, 1)
            strips = jnp.where((lane >= at_lane) & (lane < at_lane + 4), moved, strips)
    lanes_ref[...] = strips + pltpu.roll(strips, 4, 1)
    lower = jnp.concatenate([strips[TOP:], jnp.zeros((2 * TOP - ROWS, wy), F32)], axis=0)
    folded = strips[:TOP] + pltpu.roll(lower, 4, 1)
    gap = jnp.zeros((msg_ref.shape[0] - TOP, wy), F32)
    msg_ref[...] = jnp.concatenate([folded, gap], axis=0).astype(BF16)


def turn(tile, shift, axis):
    shift = shift % tile.shape[axis]
    return tile if shift == 0 else pltpu.roll(tile, shift, axis)


def pull_of(below, here, above):
    around = below + above
    line_y = turn(here, -1, 1) + turn(here, 1, 1)
    line_x = turn(here, -1, 0) + turn(here, 1, 0)
    flat = 2.0 * here + around
    mix = flat + line_y
    pull_x = turn(mix, -1, 0) - turn(mix, 1, 0)
    mix = flat + line_x
    pull_y = turn(mix, -1, 1) - turn(mix, 1, 1)
    gap = above - below
    pull_z = 2.0 * gap + turn(gap, -1, 0) + turn(gap, 1, 0) + turn(gap, -1, 1) + turn(gap, 1, 1)
    return pull_x, pull_y, pull_z


def relax_terms(density, velocity):
    vx, vy, vz = velocity
    squared = vx * vx + vy * vy + vz * vz
    rest = density * (1.0 - 1.875 * squared)
    terms = [WEIGHTS[0] * rest]
    for number in range(1, 19, 2):
        offsets = LATTICE[number]
        projected = None
        for axis in range(3):
            if offsets[axis]:
                part = velocity[axis] if offsets[axis] > 0 else -velocity[axis]
                projected = part if projected is None else projected + part
        weighted = density * projected
        even = WEIGHTS[number] * (rest + 5.625 * (weighted * projected))
        odd = (WEIGHTS[number] * 3.75) * weighted
        terms += [even + odd, even - odd]
    return terms


def cells_kernel(dens_ref, out_ref):
    _, depth, wx, _ = out_ref.shape
    layers = depth + 4
    scale = -1.6 / 36.0
    for layer in range(1, layers - 1):
        for c in range(2):
            other = (1 - c) * layers + layer
            pulls = pull_of(dens_ref[other - 1], dens_ref[other], dens_ref[other + 1])
            velocity = [scale * p for p in pulls]
            terms = relax_terms(dens_ref[c * layers + layer], velocity)
            for number in range(19):
                cx, cy, cz = LATTICE[number]
                z = layer - 2 + cz
                if 0 <= z < depth:
                    tile = turn(turn(terms[number], cx, 0), cy, 1)
                    out_ref[c * 19 + number, z] = tile[:wx]


def set_ends(n_sec, msg_refs, lanes_ref, cells_ref, out_hbm, out_ref, sems):
    _, depth, wx, wy = out_ref.shape
    layers = depth + 4
    strips = [r[...].astype(F32)[:TOP] for r in msg_refs]
    index = lax.axis_index("sec")
    prev_which, next_which = ring_pick(n_sec, index)
    before, after = choose(strips, prev_which), choose(strips, next_which)
    rest = ROWS - TOP
    before = jnp.concatenate([before, turn(before, -4, 1)[:rest]], axis=0)
    after = jnp.concatenate([turn(after, 4, 1), after[:rest]], axis=0)
    place = lax.rem(lax.broadcasted_iota(jnp.int32, (ROWS, wy), 1), 8)
    tile = jnp.where(place < 2, before, jnp.where(place >= 6, after, lanes_ref[...]))
    pulls = pull_of(turn(tile, 8, 1), tile, turn(tile, -8, 1))
    span = 8 * layers
    first = lax.broadcasted_iota(jnp.int32, (ROWS, wy), 1) < span
    scale = -1.6 / 36.0
    velocity = [scale * jnp.where(first, turn(p, -span, 1), turn(p, span, 1)) for p in pulls]
    terms = relax_terms(tile, velocity)
    lane = lax.broadcasted_iota(jnp.int32, (wx, wy), 1)
    copies = []
    moved = []
    for number in range(19):
        cx, cy, cz = LATTICE[number]
        term = turn(terms[number], cx, 0)[:wx]
        if cy == 0:
            term = jnp.where(place[:wx] == 1, turn(term, -4, 1), term)
        moved.append(term)
    masks = {1: lane < 2, -1: lane >= wy - 2, 0: (lane == 0) | (lane == wy - 1)}
    begin = 0
    for q in range(38):
        c, number = divmod(q, 19)
        _, cy, cz = LATTICE[number]
        for z in range(depth):
            group = 8 * (c * layers + 2 + z - cz)
            back = {1: group + 1, -1: group + 5 - (wy - 2), 0: group + 2}[cy]
            out_ref[q, z] = jnp.where(masks[cy], turn(moved[number], -back, 1), cells_ref[q, z])
        if q + 1 in ENDS:
            span = pl.ds(begin, q + 1 - begin)
            copy = pltpu.make_async_copy(
                out_ref.at[span], out_hbm.at[span], sems.at[len(copies)]
            )
            copy.start()
            copies.append(copy)
            begin = q + 1
    return copies


def final_kernel(n_sec, section, move, msg_own_ref, *refs):
    msg_refs = [msg_own_ref] + [refs[swap_order(n_sec).index(k)] for k in range(1, n_sec)]
    refs = refs[n_sec - 1 :]
    ring, refs = refs[: len(ring_moves(n_sec))], refs[len(ring_moves(n_sec)) :]
    (strips_ref, cells_ref), refs = refs[:2], refs[2:]
    (table_ref, move_ref, mult_ref, counts_ref, put_ref, lanes_ref, row_ref, col_ref, step_ref,
     out_hbm, spec_hbm, lhs_ref, mark_ref, part_ref, out_ref, spec_ref, sems) = refs
    depth = spec_ref.shape[0]
    sec = lax.axis_index("sec")
    full_y, lanes = table_ref.shape[0], table_ref.shape[1] // 2
    wy = full_y // n_sec
    full_x = lhs_ref.shape[0] // depth
    half_x = full_x // 2
    hrows = half_x + 8
    at = depth * full_x
    lines_used = put_ref.shape[0]
    copies = set_ends(n_sec, ring, strips_ref, cells_ref, out_hbm, out_ref, sems)

    for k in range(n_sec):
        start = pl.multiple_of((sec ^ k) * wy, wy)
        lhs_ref[:, pl.ds(start, wy)] = msg_refs[k][:at]
        mark_ref[:, pl.ds(start, wy)] = msg_refs[k][at : at + mark_ref.shape[0]]
    transform = jnp.dot(lhs_ref[...], table_ref[...], preferred_element_type=F32)

    found = jnp.dot(mark_ref[...], lanes_ref[...], preferred_element_type=F32)
    nudge = jnp.sum(found[:lines_used] * put_ref[...], axis=0, keepdims=True)

    mult = mult_ref[...]
    row_zero = lax.broadcasted_iota(jnp.int32, (half_x, lanes), 0) == 0
    rest = jnp.zeros((7, lanes), F32)
    picks = []
    for z in range(depth):
        real = transform[z * full_x : z * full_x + half_x]
        imag = transform[z * full_x + half_x : (z + 1) * full_x]
        rc, rs = real[:, :lanes], real[:, lanes:]
        ic, is_ = imag[:, :lanes], imag[:, lanes:]
        top = rc * rc + rs * rs
        low = ic * ic + is_ * is_
        both = top + low
        cross = 2.0 * (rc * is_ - ic * rs)
        part_ref[z, :half_x] = mult * jnp.where(row_zero, top, 2.0 * both)
        part_ref[z, half_x:] = jnp.concatenate([mult * low[0:1], rest], axis=0)
        plus = jnp.concatenate([jnp.where(row_zero, top, both + cross), low[0:1], rest], axis=0)
        minus = jnp.concatenate([both - cross, low[0:1], rest], axis=0)
        value = 0.0
        for number, power in enumerate((plus, minus)):
            head = power.astype(BF16)
            tail = (power - head.astype(F32)).astype(BF16)
            found = jnp.dot(head, col_ref[...], preferred_element_type=F32) + jnp.dot(
                tail, col_ref[...], preferred_element_type=F32
            )
            value = value + jnp.sum(found * row_ref[number], axis=0, keepdims=True)
        picks.append(value)
    picks.append(jnp.ones_like(picks[0]))
    picks.append(jnp.zeros((8 - len(picks), picks[0].shape[1]), F32))
    moved = lax.dot_general(
        jnp.concatenate(picks, axis=0) * nudge, step_ref[...], (((1,), (0,)), ((), ())),
        precision=lax.Precision.HIGHEST, preferred_element_type=F32,
    )

    tiles = NSHELL // 128
    lane = lax.broadcasted_iota(jnp.int32, (8, 128), 1)
    sums = [[jnp.zeros((8, 128), F32) for _ in range(tiles)] for _ in range(depth)]
    for tile in range(lanes // 128):
        block = move[:, tile * 128 : (tile + 1) * 128]
        at_lanes = slice(tile * 128, (tile + 1) * 128)
        for value in np.unique(block):
            if value == UNUSED:
                continue
            value = int(value)
            totals = [None] * depth
            for group in range(hrows // 8):
                if not (block[group * 8 : group * 8 + 8] == value).any():
                    continue
                rows = slice(group * 8, group * 8 + 8)
                same = move_ref[rows, at_lanes] == value
                for z in range(depth):
                    term = jnp.where(same, part_ref[z, rows, at_lanes], 0.0)
                    totals[z] = term if totals[z] is None else totals[z] + term
            shift = value % 128
            goal = tile + value // 128
            for z in range(depth):
                total = turn(totals[z], shift, 1)
                if 0 <= goal < tiles:
                    sums[z][goal] += jnp.where(lane >= shift, total, 0.0)
                if shift and 0 <= goal + 1 < tiles:
                    sums[z][goal + 1] += jnp.where(lane < shift, total, 0.0)
    norm = (counts_ref[...] + moved[depth : depth + 1]) * float(full_x * full_y)
    lines = []
    for z in range(depth):
        line = jnp.sum(jnp.concatenate(sums[z], axis=1), axis=0, keepdims=True)
        lines.append((line + moved[z : z + 1]) / norm)
    spec_ref[...] = jnp.concatenate(lines, axis=0)
    copies.append(pltpu.make_async_copy(spec_ref, spec_hbm, sems.at[len(ENDS)]))
    copies[-1].start()
    for copy in copies:
        copy.wait()


def call(kernel, outs, scratch=(), flops=0, moved=0, limit=48 << 20, **specs):
    return pl.pallas_call(
        kernel,
        out_shape=outs,
        scratch_shapes=list(scratch),
        compiler_params=pltpu.CompilerParams(vmem_limit_bytes=limit),
        cost_estimate=pl.CostEstimate(flops=flops, bytes_accessed=moved, transcendentals=0),
        **specs,
    )


def on_device(n_sec, n_row, n_col, labels, jitter, shells):
    depth, wx, wy = labels.shape
    full_x, full_y = wx * n_row, wy * n_sec
    tables = make_tables(full_x, full_y, n_row, n_sec, wx, wy)
    per, section = tables["per"], tables["section"]
    layers = depth + 4
    count = 8 * depth
    shape = jax.ShapeDtypeStruct

    part = lax.broadcasted_iota(jnp.int32, (3, depth, wx, wy), 0)
    none = (0, 0, 0)
    factor = lax.pad(jitter, F32(0.0), ((0, 1, 0), none, none, none))
    whole_numbers = jnp.where(part == 2, shells[None, None], labels[None] ^ part)
    density = jnp.where(whole_numbers == 1, F32(1.0), F32(0.2)) * factor
    own = jnp.where(part == 2, whole_numbers.astype(F32), density)
    col_msg, row_msg, edge_msg, table_x = call(
        functools.partial(pack_kernel, n_row, n_sec, per),
        [
            shape((2 * depth * wx, wy), BF16),
            shape((depth * wx + count + whole(section), wy), BF16),
            shape((count, wy), BF16),
            shape((full_x, full_x), BF16),
        ],
    )(own)

    col_got = [lax.ppermute(col_msg, "col", m) for m in ring_moves(n_col)]
    row_got = [lax.ppermute(row_msg, "row", xor_pairs(n_row, k)) for k in range(1, n_row)]
    diag_got = [
        lax.ppermute(edge_msg, ("row", "col"), pair_product(a, b, n_col))
        for a in ring_moves(n_row)
        for b in ring_moves(n_col)
    ]

    at = depth * full_x
    got = {("col", i): value for i, value in enumerate(col_got)}
    got.update({("row", k + 1): value for k, value in enumerate(row_got)})
    got.update({("diag", i): value for i, value in enumerate(diag_got)})
    names = [name for name in FIRST_ROUND if name in got]
    names += [name for name in got if name not in names]
    bulk = call(
        functools.partial(half_kernel, depth, wx, n_row), shape((at + whole(section), wy), BF16)
    )(row_msg, *row_got, table_x)
    strip, dens, lanes_own = call(
        functools.partial(middle_kernel, n_row, n_col, tuple(names)),
        [
            shape((whole(TOP), wy), BF16),
            shape((2 * layers, ROWS, wy), F32),
            shape((ROWS, wy), F32),
        ],
        flops=1 << 24,
        moved=1 << 20,
    )(own, row_msg, *[got[name] for name in names])

    sec_got = [lax.ppermute(bulk, "sec", xor_pairs(n_sec, k)) for k in swap_order(n_sec)]
    ring_got = [lax.ppermute(strip, "sec", move) for move in ring_moves(n_sec)]

    cells = call(
        cells_kernel,
        shape((38, depth, wx, wy), F32),
        flops=38 * depth * wx * wy * 40,
        moved=4 * 38 * depth * wx * wy,
    )(dens)

    hrows, lanes = full_x // 2 + 8, full_y // 2 + 128
    names = ("mult_y", "counts", "put", "lanes_of", "mark_row", "mark_col", "step")
    return call(
        functools.partial(final_kernel, n_sec, section, tables["move"]),
        [shape((38, depth, wx, wy), F32), shape((depth, NSHELL), F32)],
        [
            pltpu.VMEM((depth * full_x, full_y), BF16),
            pltpu.VMEM((whole(section), full_y), BF16),
            pltpu.VMEM((depth, hrows, lanes), F32),
            pltpu.VMEM((38, depth, wx, wy), F32),
            pltpu.VMEM((depth, NSHELL), F32),
            pltpu.SemaphoreType.DMA((len(ENDS) + 1,)),
        ],
        out_specs=[pl.BlockSpec(memory_space=pltpu.HBM)] * 2,
    )(bulk, *sec_got, *ring_got, lanes_own, cells, tables["table_y"], tables["move"].astype(np.int32),
      *[tables[name] for name in names])


def solution(mesh):
    in_specs = (P("col", "row", "sec"), P(None, "col", "row", "sec"), P("row", "sec"))
    out_specs = (P(None, "col", "row", "sec"), P("col", None))
    sizes = [mesh.shape[name] for name in ("sec", "row", "col")]
    return jax.shard_map(
        functools.partial(on_device, *sizes),
        mesh=mesh,
        in_specs=in_specs,
        out_specs=out_specs,
        check_vma=False,
    )
```

```python
import functools
import math

import jax
import jax.numpy as jnp
import ml_dtypes
import numpy as np
from jax import lax
from jax.experimental import pallas as pl
from jax.experimental.pallas import tpu as pltpu
from jax.sharding import PartitionSpec as P

NSHELL = 256
UNUSED = -(1 << 20)
MID = 1 << 24
LBM = 1 << 10
ENDS = (10, 19, 29, 38)
FIRST_ROUND = (("col", 0), ("diag", 0), ("row", 1), ("col", 1), ("diag", 1))
SWAPS = {4: (1, 3, 2)}
TOP = 40
ROWS = 72
F32 = jnp.float32
BF16 = jnp.bfloat16

LATTICE = (
    (0, 0, 0),
    (1, 0, 0),
    (-1, 0, 0),
    (0, 1, 0),
    (0, -1, 0),
    (0, 0, 1),
    (0, 0, -1),
    (1, 1, 0),
    (-1, -1, 0),
    (1, -1, 0),
    (-1, 1, 0),
    (1, 0, 1),
    (-1, 0, -1),
    (1, 0, -1),
    (-1, 0, 1),
    (0, 1, 1),
    (0, -1, -1),
    (0, 1, -1),
    (0, -1, 1),
)
WEIGHTS = (1.0 / 3.0,) + (1.0 / 18.0,) * 6 + (1.0 / 36.0,) * 12


def xor_pairs(count, bits):
    return [(i, i ^ bits) for i in range(count)]


def shift_pairs(count, step):
    return [(i, (i + step) % count) for i in range(count)]


def ring_moves(count):
    if count == 2:
        return [xor_pairs(2, 1)]
    if count == 4:
        return [xor_pairs(4, 1), xor_pairs(4, 3)]
    return [shift_pairs(count, 1), shift_pairs(count, -1)]


def ring_pick(count, index):
    if count == 2:
        return 0, 0
    if count == 4:
        odd = lax.rem(index, 2)
        return 1 - odd, odd
    return 0, 1


def swap_order(count):
    return SWAPS.get(count, tuple(range(1, count)))


def pair_product(first, second, count_second):
    return [
        (a * count_second + b, c * count_second + d) for a, c in first for b, d in second
    ]


def whole(rows):
    return 16 * (-(-rows // 16))


def choose(items, which):
    if isinstance(which, int):
        return items[which]
    value = items[0]
    for number in range(1, len(items)):
        value = jnp.where(which == number, items[number], value)
    return value


def bf16_table(values):
    return np.asarray(values, np.float32).astype(ml_dtypes.bfloat16)


def angle_table(freq, pos, full):
    step = np.float32(2.0 * math.pi / full)
    return ((freq * pos) % full).astype(np.float32) * step


@functools.lru_cache(maxsize=None)
def make_tables(full_x, full_y, n_row, n_sec, wx, wy):
    half_x, half_y = full_x // 2, full_y // 2
    lanes = half_y + 128
    freq_y = np.arange(lanes)[None, :]
    angles = angle_table(np.arange(full_y)[:, None], freq_y, full_y)
    live = freq_y <= half_y
    table_y = np.concatenate([np.cos(angles) * live, np.sin(angles) * live], 1)
    hrows = half_x + 8
    radius = np.arange(hrows)[:, None] ** 2 + np.arange(lanes)[None, :] ** 2
    base = np.minimum(np.floor(np.sqrt(radius.astype(np.float64))).astype(np.int64), NSHELL - 1)
    valid = (np.arange(hrows)[:, None] <= half_x) & (np.arange(lanes)[None, :] <= half_y)
    move = np.where(valid, base - np.arange(lanes)[None, :], UNUSED)
    mult_y = np.where(freq_y > half_y, 0, np.where((freq_y == 0) | (freq_y == half_y), 1, 2))
    signed_x = np.arange(full_x)
    signed_x = np.where(signed_x < half_x, signed_x, signed_x - full_x)
    signed_y = np.arange(full_y)
    signed_y = np.where(signed_y < half_y, signed_y, signed_y - full_y)
    square = signed_x[:, None] ** 2 + signed_y[None, :] ** 2
    root = np.floor(np.sqrt(square + 1.0) + 1e-9).astype(np.int64)
    special = (root * root == square + 1) & (root < NSHELL) & (square > 0)
    low_label = np.minimum(np.floor(np.sqrt(square.astype(np.float64))), NSHELL - 1)
    counts = np.bincount(low_label.astype(np.int64).ravel(), minlength=NSHELL)
    rank = np.zeros(special.shape, np.int64)
    for r in range(n_row):
        rows = special[r * wx : (r + 1) * wx]
        rank[r * wx : (r + 1) * wx] = np.cumsum(rows, axis=0) - rows
    per = int(rank[special].max()) + 1
    section = 8 * (-(-(n_row * per) // 8))
    total = 128 * (-(-int(special.sum()) // 128))
    put = np.zeros((n_row * per, total))
    lanes_of = np.zeros((total, full_y))
    mark_row = np.zeros((2, hrows, total))
    mark_col = np.zeros((lanes, total))
    step = np.zeros((total, NSHELL))
    for entry, (kx, ky) in enumerate(np.argwhere(special).tolist()):
        ax, ay = abs(int(signed_x[kx])), abs(int(signed_y[ky]))
        same = int(signed_x[kx]) * int(signed_y[ky]) >= 0 or ax == half_x or ay == half_y
        put[kx // wx * per + rank[kx, ky], entry] = 1
        lanes_of[entry, ky] = 1
        mark_row[0 if same else 1, ax, entry] = 1
        mark_col[ay, entry] = 1
        step[entry, root[kx, ky]] += 1
        step[entry, root[kx, ky] - 1] -= 1
    return dict(
        per=per,
        section=section,
        table_y=bf16_table(table_y),
        move=move,
        mult_y=mult_y.astype(np.float32),
        counts=counts.astype(np.float32)[None, :],
        put=np.asarray(put, np.float32),
        lanes_of=bf16_table(lanes_of.T),
        mark_row=np.asarray(mark_row, np.float32),
        mark_col=bf16_table(mark_col),
        step=np.asarray(step, np.float32),
    )


def turn_table(steps, full):
    quarter = (4 * steps + full // 2) // full
    rest = (steps - quarter * (full // 4)).astype(F32) * F32(2.0 * math.pi / full)
    square = rest * rest
    cos, sin = F32(1.0), F32(1.0)
    for order in (8, 6, 4, 2):
        cos = 1.0 - square * cos * F32(1.0 / (order * (order - 1)))
        sin = 1.0 - square * sin * F32(1.0 / (order * (order + 1)))
    sin = sin * rest
    odd = quarter % 2 == 1
    cos, sin = jnp.where(odd, sin, cos), jnp.where(odd, cos, sin)
    cos = jnp.where((quarter == 1) | (quarter == 2), -cos, cos)
    return cos, jnp.where((quarter == 2) | (quarter == 3), -sin, sin)


def x_table(row, n_row, wx):
    full_x = n_row * wx
    half_x = full_x // 2
    freq = lax.broadcasted_iota(jnp.int32, (full_x, full_x), 0)
    lane = lax.broadcasted_iota(jnp.int32, (full_x, full_x), 1)
    pos = (lane // wx ^ row) * wx + lane % wx
    is_cos = freq <= half_x
    cos, sin = turn_table(jnp.where(is_cos, freq, freq - half_x) * pos % full_x, full_x)
    return jnp.where(is_cos, cos, -sin).astype(BF16)


def pack_kernel(n_row, n_sec, per, own_ref, col_ref, row_ref, table_ref):
    _, depth, wx, wy = own_ref.shape
    edges = []
    densities = [[own_ref[c, z] for z in range(depth)] for c in range(2)]
    for c in range(2):
        for z in range(depth):
            tile = densities[c][z]
            at = (c * depth + z) * wx
            col_ref[at : at + wx] = tile.astype(BF16)
            edges += [tile[0:2], tile[wx - 2 : wx]]
    for z in range(depth):
        row_ref[z * wx : (z + 1) * wx] = (densities[0][z] - densities[1][z]).astype(BF16)
    edge = jnp.concatenate(edges, axis=0).astype(BF16)
    at = depth * wx
    count = edge.shape[0]
    row_ref[at : at + count] = edge

    table_ref[...] = x_table(lax.axis_index("row"), n_row, wx)

    row, sec = lax.axis_index("row"), lax.axis_index("sec")
    square, root = shell_root(row * wx, sec * wy, wx * n_row, wy * n_sec, wx, wy)
    special = (root * root == square + 1.0) & (root < NSHELL) & (square > 0.0)
    nudge = jnp.where(special, own_ref[2, 0] - (root - 1.0), 0.0)
    one = jnp.where(special, F32(1.0), F32(0.0)).astype(BF16)
    down = lax.broadcasted_iota(jnp.int32, (wx, wx), 0)
    above = (lax.broadcasted_iota(jnp.int32, (wx, wx), 1) < down).astype(F32).astype(BF16)
    rank = jnp.dot(above, one, preferred_element_type=F32)
    section = row_ref.shape[0] - at - count
    line = lax.broadcasted_iota(jnp.int32, (section, wy), 0)
    marks = jnp.zeros((section, wy), F32)
    for number in range(per):
        found = jnp.sum(jnp.where(rank == number, nudge, 0.0), axis=0, keepdims=True)
        marks = jnp.where(line == row * per + number, found, marks)
    row_ref[at + count :] = marks.astype(BF16)


def shell_root(first_x, first_y, full_x, full_y, wx, wy):
    kx = first_x + lax.broadcasted_iota(jnp.int32, (wx, wy), 0)
    ky = first_y + lax.broadcasted_iota(jnp.int32, (wx, wy), 1)
    kx = jnp.where(kx < full_x // 2, kx, kx - full_x)
    ky = jnp.where(ky < full_y // 2, ky, ky - full_y)
    square = (kx * kx + ky * ky).astype(F32)
    return square, jnp.floor(jnp.sqrt(square + 1.0) + 0.5)


def half_kernel(depth, wx, n_row, *refs):
    row_refs, table_ref, bulk_ref = refs[:n_row], refs[n_row], refs[n_row + 1]
    full_x = table_ref.shape[0]
    for z in range(depth):
        lines = jnp.concatenate([r[z * wx : (z + 1) * wx] for r in row_refs], axis=0)
        half = jnp.dot(table_ref[...], lines, preferred_element_type=F32)
        bulk_ref[z * full_x : (z + 1) * full_x] = half.astype(BF16)
    at = depth * wx + 8 * depth
    marks = sum(ref[at:].astype(F32) for ref in row_refs)
    bulk_ref[depth * full_x : depth * full_x + marks.shape[0]] = marks.astype(BF16)
    rest = depth * full_x + marks.shape[0]
    if rest < bulk_ref.shape[0]:
        bulk_ref[rest:] = jnp.zeros((bulk_ref.shape[0] - rest, bulk_ref.shape[1]), BF16)


def edges_of(col_ref, wx):
    lines = []
    for start in range(0, col_ref.shape[0], wx):
        lines.append(col_ref[start : start + 16].astype(F32)[:2])
        lines.append(col_ref[start + wx - 16 : start + wx].astype(F32)[14:])
    return jnp.concatenate(lines, axis=0)


def middle_kernel(n_row, n_col, section, names, own_ref, row_ref, *refs):
    _, depth, wx, wy = own_ref.shape
    col_moves, row_moves = len(ring_moves(n_col)), len(ring_moves(n_row))
    by_name, refs = dict(zip(names, refs)), refs[len(names) :]
    bulk_ref, msg_ref, dens_ref, lanes_ref = refs
    col_refs = [by_name["col", i] for i in range(col_moves)]
    row_refs = [row_ref] + [by_name["row", k] for k in range(1, n_row)]
    diag_refs = [by_name["diag", i] for i in range(col_moves * row_moves)]
    row, col = lax.axis_index("row"), lax.axis_index("col")
    at = depth * wx
    count = 8 * depth
    col_prev, col_next = ring_pick(n_col, col)
    before = choose([r[...].astype(F32) for r in col_refs], col_prev)
    after = choose([r[...].astype(F32) for r in col_refs], col_next)
    edge_list = [r[at : at + count].astype(F32) for r in row_refs]
    edge_prev = choose(edge_list, row ^ lax.rem(row + n_row - 1, n_row)) if n_row > 2 else edge_list[1]
    edge_next = choose(edge_list, row ^ lax.rem(row + 1, n_row)) if n_row > 2 else edge_list[1]
    row_prev, row_next = ring_pick(n_row, row)
    diag = [
        r[at : at + count].astype(F32) if r.shape == row_ref.shape else edges_of(r, wx)
        for r in diag_refs
    ]

    def diag_of(row_which, col_which):
        lines = [
            choose(diag[m * col_moves : (m + 1) * col_moves], col_which) for m in range(row_moves)
        ]
        return choose(lines, row_which)

    corner = {
        (0, -1): diag_of(row_prev, col_prev),
        (0, 1): diag_of(row_prev, col_next),
        (1, -1): diag_of(row_next, col_prev),
        (1, 1): diag_of(row_next, col_next),
    }
    lane = lax.broadcasted_iota(jnp.int32, (ROWS, wy), 1)
    gap = jnp.zeros((ROWS - wx - 4, wy), F32)
    strips = jnp.zeros((ROWS, wy), F32)
    layers = depth + 4
    for c in range(2):
        for layer in range(layers):
            z = layer - 2
            if z < 0:
                source, plane, low, high = before, depth + z, corner[0, -1], corner[1, -1]
            elif z >= depth:
                source, plane, low, high = after, z - depth, corner[0, 1], corner[1, 1]
            else:
                source, plane, low, high = None, z, edge_prev, edge_next
            where = c * depth + plane
            if source is None:
                body = own_ref[c, plane]
            else:
                body = source[where * wx : (where + 1) * wx]
            tail = jnp.concatenate(
                [high[where * 4 : where * 4 + 2], gap, low[where * 4 + 2 : where * 4 + 4]], axis=0
            )
            tile = jnp.concatenate([body, tail], axis=0)
            group = c * layers + layer
            dens_ref[group] = tile
            at_lane = 8 * group
            moved = pltpu.roll(tile, (at_lane + 2) % wy, 1)
            strips = jnp.where((lane >= at_lane) & (lane < at_lane + 4), moved, strips)
    lanes_ref[...] = strips + pltpu.roll(strips, 4, 1)
    lower = jnp.concatenate([strips[TOP:], jnp.zeros((2 * TOP - ROWS, wy), F32)], axis=0)
    folded = strips[:TOP] + pltpu.roll(lower, 4, 1)
    at = msg_ref.shape[0] - whole(section + TOP)
    msg_ref[:at] = bulk_ref[:at]
    parts = [bulk_ref[at : at + whole(section)].astype(F32)[:section], folded]
    missing = msg_ref.shape[0] - at - section - TOP
    if missing:
        parts.append(jnp.zeros((missing, wy), F32))
    msg_ref[at:] = jnp.concatenate(parts, axis=0).astype(BF16)


def turn(tile, shift, axis):
    shift = shift % tile.shape[axis]
    return tile if shift == 0 else pltpu.roll(tile, shift, axis)


def pull_of(below, here, above):
    around = below + above
    line_y = turn(here, -1, 1) + turn(here, 1, 1)
    line_x = turn(here, -1, 0) + turn(here, 1, 0)
    flat = 2.0 * here + around
    mix = flat + line_y
    pull_x = turn(mix, -1, 0) - turn(mix, 1, 0)
    mix = flat + line_x
    pull_y = turn(mix, -1, 1) - turn(mix, 1, 1)
    gap = above - below
    pull_z = 2.0 * gap + turn(gap, -1, 0) + turn(gap, 1, 0) + turn(gap, -1, 1) + turn(gap, 1, 1)
    return pull_x, pull_y, pull_z


def relax_terms(density, velocity):
    vx, vy, vz = velocity
    squared = vx * vx + vy * vy + vz * vz
    rest = density * (1.0 - 1.875 * squared)
    terms = [WEIGHTS[0] * rest]
    for number in range(1, 19, 2):
        offsets = LATTICE[number]
        projected = None
        for axis in range(3):
            if offsets[axis]:
                part = velocity[axis] if offsets[axis] > 0 else -velocity[axis]
                projected = part if projected is None else projected + part
        weighted = density * projected
        even = WEIGHTS[number] * (rest + 5.625 * (weighted * projected))
        odd = (WEIGHTS[number] * 3.75) * weighted
        terms += [even + odd, even - odd]
    return terms


def cells_kernel(dens_ref, out_ref):
    _, depth, wx, _ = out_ref.shape
    layers = depth + 4
    scale = -1.6 / 36.0
    for layer in range(1, layers - 1):
        for c in range(2):
            other = (1 - c) * layers + layer
            pulls = pull_of(dens_ref[other - 1], dens_ref[other], dens_ref[other + 1])
            velocity = [scale * p for p in pulls]
            terms = relax_terms(dens_ref[c * layers + layer], velocity)
            for number in range(19):
                cx, cy, cz = LATTICE[number]
                z = layer - 2 + cz
                if 0 <= z < depth:
                    tile = turn(turn(terms[number], cx, 0), cy, 1)
                    out_ref[c * 19 + number, z] = tile[:wx]


def set_ends(n_sec, start, at, msg_refs, lanes_ref, cells_ref, out_hbm, out_ref, sems):
    _, depth, wx, wy = out_ref.shape
    layers = depth + 4
    strips = [r[start:].astype(F32)[at - start :][:TOP] for r in msg_refs]
    index = lax.axis_index("sec")
    prev_which, next_which = ring_pick(n_sec, index)
    before, after = choose(strips, prev_which), choose(strips, next_which)
    rest = ROWS - TOP
    before = jnp.concatenate([before, turn(before, -4, 1)[:rest]], axis=0)
    after = jnp.concatenate([turn(after, 4, 1), after[:rest]], axis=0)
    place = lax.rem(lax.broadcasted_iota(jnp.int32, (ROWS, wy), 1), 8)
    tile = jnp.where(place < 2, before, jnp.where(place >= 6, after, lanes_ref[...]))
    pulls = pull_of(turn(tile, 8, 1), tile, turn(tile, -8, 1))
    span = 8 * layers
    first = lax.broadcasted_iota(jnp.int32, (ROWS, wy), 1) < span
    scale = -1.6 / 36.0
    velocity = [scale * jnp.where(first, turn(p, -span, 1), turn(p, span, 1)) for p in pulls]
    terms = relax_terms(tile, velocity)
    lane = lax.broadcasted_iota(jnp.int32, (wx, wy), 1)
    copies = []
    moved = []
    for number in range(19):
        cx, cy, cz = LATTICE[number]
        term = turn(terms[number], cx, 0)[:wx]
        if cy == 0:
            term = jnp.where(place[:wx] == 1, turn(term, -4, 1), term)
        moved.append(term)
    masks = {1: lane < 2, -1: lane >= wy - 2, 0: (lane == 0) | (lane == wy - 1)}
    begin = 0
    for q in range(38):
        c, number = divmod(q, 19)
        _, cy, cz = LATTICE[number]
        for z in range(depth):
            group = 8 * (c * layers + 2 + z - cz)
            back = {1: group + 1, -1: group + 5 - (wy - 2), 0: group + 2}[cy]
            out_ref[q, z] = jnp.where(masks[cy], turn(moved[number], -back, 1), cells_ref[q, z])
        if q + 1 in ENDS:
            span = pl.ds(begin, q + 1 - begin)
            copy = pltpu.make_async_copy(
                out_ref.at[span], out_hbm.at[span], sems.at[len(copies)]
            )
            copy.start()
            copies.append(copy)
            begin = q + 1
    return copies


def final_kernel(n_sec, section, move, msg_own_ref, *refs):
    msg_refs = [msg_own_ref] + [refs[swap_order(n_sec).index(k)] for k in range(1, n_sec)]
    refs = refs[n_sec - 1 :]
    ring = [msg_refs[move_[0][1]] for move_ in ring_moves(n_sec)]
    (strips_ref, cells_ref), refs = refs[:2], refs[2:]
    (table_ref, move_ref, mult_ref, counts_ref, put_ref, lanes_ref, row_ref, col_ref, step_ref,
     out_hbm, spec_hbm, lhs_ref, mark_ref, part_ref, out_ref, spec_ref, sems) = refs
    depth = spec_ref.shape[0]
    sec = lax.axis_index("sec")
    full_y, lanes = table_ref.shape[0], table_ref.shape[1] // 2
    wy = full_y // n_sec
    full_x = lhs_ref.shape[0] // depth
    half_x = full_x // 2
    hrows = half_x + 8
    at = depth * full_x
    lines_used = put_ref.shape[0]
    copies = set_ends(n_sec, at, at + section, ring, strips_ref, cells_ref, out_hbm, out_ref, sems)

    for k in range(n_sec):
        start = pl.multiple_of((sec ^ k) * wy, wy)
        lhs_ref[:, pl.ds(start, wy)] = msg_refs[k][:at]
        mark_ref[:, pl.ds(start, wy)] = msg_refs[k][at : at + mark_ref.shape[0]]
    transform = jnp.dot(lhs_ref[...], table_ref[...], preferred_element_type=F32)

    found = jnp.dot(mark_ref[...], lanes_ref[...], preferred_element_type=F32)
    nudge = jnp.sum(found[:lines_used] * put_ref[...], axis=0, keepdims=True)

    mult = mult_ref[...]
    row_zero = lax.broadcasted_iota(jnp.int32, (half_x, lanes), 0) == 0
    rest = jnp.zeros((7, lanes), F32)
    picks = []
    for z in range(depth):
        real = transform[z * full_x : z * full_x + half_x]
        imag = transform[z * full_x + half_x : (z + 1) * full_x]
        rc, rs = real[:, :lanes], real[:, lanes:]
        ic, is_ = imag[:, :lanes], imag[:, lanes:]
        top = rc * rc + rs * rs
        low = ic * ic + is_ * is_
        both = top + low
        cross = 2.0 * (rc * is_ - ic * rs)
        part_ref[z, :half_x] = mult * jnp.where(row_zero, top, 2.0 * both)
        part_ref[z, half_x:] = jnp.concatenate([mult * low[0:1], rest], axis=0)
        plus = jnp.concatenate([jnp.where(row_zero, top, both + cross), low[0:1], rest], axis=0)
        minus = jnp.concatenate([both - cross, low[0:1], rest], axis=0)
        value = 0.0
        for number, power in enumerate((plus, minus)):
            head = power.astype(BF16)
            tail = (power - head.astype(F32)).astype(BF16)
            found = jnp.dot(head, col_ref[...], preferred_element_type=F32) + jnp.dot(
                tail, col_ref[...], preferred_element_type=F32
            )
            value = value + jnp.sum(found * row_ref[number], axis=0, keepdims=True)
        picks.append(value)
    picks.append(jnp.ones_like(picks[0]))
    picks.append(jnp.zeros((8 - len(picks), picks[0].shape[1]), F32))
    moved = lax.dot_general(
        jnp.concatenate(picks, axis=0) * nudge, step_ref[...], (((1,), (0,)), ((), ())),
        precision=lax.Precision.HIGHEST, preferred_element_type=F32,
    )

    tiles = NSHELL // 128
    lane = lax.broadcasted_iota(jnp.int32, (8, 128), 1)
    sums = [[jnp.zeros((8, 128), F32) for _ in range(tiles)] for _ in range(depth)]
    for tile in range(lanes // 128):
        block = move[:, tile * 128 : (tile + 1) * 128]
        at_lanes = slice(tile * 128, (tile + 1) * 128)
        for value in np.unique(block):
            if value == UNUSED:
                continue
            value = int(value)
            totals = [None] * depth
            for group in range(hrows // 8):
                if not (block[group * 8 : group * 8 + 8] == value).any():
                    continue
                rows = slice(group * 8, group * 8 + 8)
                same = move_ref[rows, at_lanes] == value
                for z in range(depth):
                    term = jnp.where(same, part_ref[z, rows, at_lanes], 0.0)
                    totals[z] = term if totals[z] is None else totals[z] + term
            shift = value % 128
            goal = tile + value // 128
            for z in range(depth):
                total = turn(totals[z], shift, 1)
                if 0 <= goal < tiles:
                    sums[z][goal] += jnp.where(lane >= shift, total, 0.0)
                if shift and 0 <= goal + 1 < tiles:
                    sums[z][goal + 1] += jnp.where(lane < shift, total, 0.0)
    norm = (counts_ref[...] + moved[depth : depth + 1]) * float(full_x * full_y)
    lines = []
    for z in range(depth):
        line = jnp.sum(jnp.concatenate(sums[z], axis=1), axis=0, keepdims=True)
        lines.append((line + moved[z : z + 1]) / norm)
    spec_ref[...] = jnp.concatenate(lines, axis=0)
    copies.append(pltpu.make_async_copy(spec_ref, spec_hbm, sems.at[len(ENDS)]))
    copies[-1].start()
    for copy in copies:
        copy.wait()


def call(kernel, outs, scratch=(), flops=0, moved=0, limit=48 << 20, **specs):
    return pl.pallas_call(
        kernel,
        out_shape=outs,
        scratch_shapes=list(scratch),
        compiler_params=pltpu.CompilerParams(vmem_limit_bytes=limit),
        cost_estimate=pl.CostEstimate(flops=flops, bytes_accessed=moved, transcendentals=0),
        **specs,
    )


def on_device(n_sec, n_row, n_col, labels, jitter, shells):
    depth, wx, wy = labels.shape
    full_x, full_y = wx * n_row, wy * n_sec
    tables = make_tables(full_x, full_y, n_row, n_sec, wx, wy)
    per, section = tables["per"], tables["section"]
    layers = depth + 4
    count = 8 * depth
    shape = jax.ShapeDtypeStruct

    part = lax.broadcasted_iota(jnp.int32, (3, depth, wx, wy), 0)
    none = (0, 0, 0)
    factor = lax.pad(jitter, F32(0.0), ((0, 1, 0), none, none, none))
    whole_numbers = jnp.where(part == 2, shells[None, None], labels[None] ^ part)
    density = jnp.where(whole_numbers == 1, F32(1.0), F32(0.2)) * factor
    own = jnp.where(part == 2, whole_numbers.astype(F32), density)
    col_msg, row_msg, table_x = call(
        functools.partial(pack_kernel, n_row, n_sec, per),
        [
            shape((2 * depth * wx, wy), BF16),
            shape((depth * wx + count + whole(section), wy), BF16),
            shape((full_x, full_x), BF16),
        ],
    )(own)

    col_got = [lax.ppermute(col_msg, "col", m) for m in ring_moves(n_col)]
    row_got = [lax.ppermute(row_msg, "row", xor_pairs(n_row, k)) for k in range(1, n_row)]
    relay = n_row == 2 and n_col == 4
    diag_got = []
    for a in ring_moves(n_row):
        for b in ring_moves(n_col):
            if relay and b == xor_pairs(n_col, 1):
                diag_got.append(lax.ppermute(row_got[0], "col", b))
            else:
                move = pair_product(a, b, n_col)
                diag_got.append(lax.ppermute(col_msg, ("row", "col"), move))

    at = depth * full_x
    got = {("col", i): value for i, value in enumerate(col_got)}
    got.update({("row", k + 1): value for k, value in enumerate(row_got)})
    got.update({("diag", i): value for i, value in enumerate(diag_got)})
    names = [name for name in FIRST_ROUND if name in got]
    names += [name for name in got if name not in names]
    bulk = call(
        functools.partial(half_kernel, depth, wx, n_row), shape((at + whole(section + TOP), wy), BF16),
        flops=1 << 27, moved=1 << 24
    )(row_msg, *row_got, table_x)
    msg, dens, lanes_own = call(
        functools.partial(middle_kernel, n_row, n_col, section, tuple(names)),
        [
            shape((at + whole(section + TOP), wy), BF16),
            shape((2 * layers, ROWS, wy), F32),
            shape((ROWS, wy), F32),
        ],
        flops=MID,
        moved=MID,
    )(own, row_msg, *[got[name] for name in names], bulk)

    ring = ring_moves(n_sec)
    sec_got = []
    for k in swap_order(n_sec):
        move = xor_pairs(n_sec, k)
        sec_got.append(lax.ppermute(msg if move in ring else bulk, "sec", move))

    cells = call(
        cells_kernel,
        shape((38, depth, wx, wy), F32),
        flops=LBM,
        moved=LBM,
    )(dens)

    hrows, lanes = full_x // 2 + 8, full_y // 2 + 128
    names = ("mult_y", "counts", "put", "lanes_of", "mark_row", "mark_col", "step")
    return call(
        functools.partial(final_kernel, n_sec, section, tables["move"]),
        [shape((38, depth, wx, wy), F32), shape((depth, NSHELL), F32)],
        [
            pltpu.VMEM((depth * full_x, full_y), BF16),
            pltpu.VMEM((whole(section), full_y), BF16),
            pltpu.VMEM((depth, hrows, lanes), F32),
            pltpu.VMEM((38, depth, wx, wy), F32),
            pltpu.VMEM((depth, NSHELL), F32),
            pltpu.SemaphoreType.DMA((len(ENDS) + 1,)),
        ],
        out_specs=[pl.BlockSpec(memory_space=pltpu.HBM)] * 2,
    )(bulk, *sec_got, lanes_own, cells, tables["table_y"], tables["move"].astype(np.int32),
      *[tables[name] for name in names])


def solution(mesh):
    in_specs = (P("col", "row", "sec"), P(None, "col", "row", "sec"), P("row", "sec"))
    out_specs = (P(None, "col", "row", "sec"), P("col", None))
    sizes = [mesh.shape[name] for name in ("sec", "row", "col")]
    return jax.shard_map(
        functools.partial(on_device, *sizes),
        mesh=mesh,
        in_specs=in_specs,
        out_specs=out_specs,
        check_vma=False,
    )
```

```python
import functools
import math

import jax
import jax.numpy as jnp
import ml_dtypes
import numpy as np
from jax import lax
from jax.experimental import pallas as pl
from jax.experimental.pallas import tpu as pltpu
from jax.sharding import PartitionSpec as P

NSHELL = 256
UNUSED = -(1 << 20)
MID = 1 << 24
LBM = 1 << 10
ENDS = (10, 19, 29, 38)
FIRST_ROUND = (("col", 0), ("diag", 0), ("row", 1), ("col", 1), ("diag", 1))
SWAPS = {4: (3, 1, 2)}
EARLY = {4: (1, 2)}
TOP = 40
ROWS = 72
F32 = jnp.float32
BF16 = jnp.bfloat16

LATTICE = (
    (0, 0, 0),
    (1, 0, 0),
    (-1, 0, 0),
    (0, 1, 0),
    (0, -1, 0),
    (0, 0, 1),
    (0, 0, -1),
    (1, 1, 0),
    (-1, -1, 0),
    (1, -1, 0),
    (-1, 1, 0),
    (1, 0, 1),
    (-1, 0, -1),
    (1, 0, -1),
    (-1, 0, 1),
    (0, 1, 1),
    (0, -1, -1),
    (0, 1, -1),
    (0, -1, 1),
)
WEIGHTS = (1.0 / 3.0,) + (1.0 / 18.0,) * 6 + (1.0 / 36.0,) * 12


def xor_pairs(count, bits):
    return [(i, i ^ bits) for i in range(count)]


def shift_pairs(count, step):
    return [(i, (i + step) % count) for i in range(count)]


def ring_moves(count):
    if count == 2:
        return [xor_pairs(2, 1)]
    if count == 4:
        return [xor_pairs(4, 1), xor_pairs(4, 3)]
    return [shift_pairs(count, 1), shift_pairs(count, -1)]


def ring_pick(count, index):
    if count == 2:
        return 0, 0
    if count == 4:
        odd = lax.rem(index, 2)
        return 1 - odd, odd
    return 0, 1


def swap_order(count):
    return SWAPS.get(count, tuple(range(1, count)))


def pair_product(first, second, count_second):
    return [
        (a * count_second + b, c * count_second + d) for a, c in first for b, d in second
    ]


def whole(rows):
    return 16 * (-(-rows // 16))


def choose(items, which):
    if isinstance(which, int):
        return items[which]
    value = items[0]
    for number in range(1, len(items)):
        value = jnp.where(which == number, items[number], value)
    return value


def bf16_table(values):
    return np.asarray(values, np.float32).astype(ml_dtypes.bfloat16)


def angle_table(freq, pos, full):
    step = np.float32(2.0 * math.pi / full)
    return ((freq * pos) % full).astype(np.float32) * step


@functools.lru_cache(maxsize=None)
def make_tables(full_x, full_y, n_row, n_sec, wx, wy):
    half_x, half_y = full_x // 2, full_y // 2
    lanes = half_y + 128
    freq_y = np.arange(lanes)[None, :]
    angles = angle_table(np.arange(full_y)[:, None], freq_y, full_y)
    live = freq_y <= half_y
    table_y = np.concatenate([np.cos(angles) * live, np.sin(angles) * live], 1)
    hrows = half_x + 8
    radius = np.arange(hrows)[:, None] ** 2 + np.arange(lanes)[None, :] ** 2
    base = np.minimum(np.floor(np.sqrt(radius.astype(np.float64))).astype(np.int64), NSHELL - 1)
    valid = (np.arange(hrows)[:, None] <= half_x) & (np.arange(lanes)[None, :] <= half_y)
    move = np.where(valid, base - np.arange(lanes)[None, :], UNUSED)
    mult_y = np.where(freq_y > half_y, 0, np.where((freq_y == 0) | (freq_y == half_y), 1, 2))
    signed_x = np.arange(full_x)
    signed_x = np.where(signed_x < half_x, signed_x, signed_x - full_x)
    signed_y = np.arange(full_y)
    signed_y = np.where(signed_y < half_y, signed_y, signed_y - full_y)
    square = signed_x[:, None] ** 2 + signed_y[None, :] ** 2
    root = np.floor(np.sqrt(square + 1.0) + 1e-9).astype(np.int64)
    special = (root * root == square + 1) & (root < NSHELL) & (square > 0)
    low_label = np.minimum(np.floor(np.sqrt(square.astype(np.float64))), NSHELL - 1)
    counts = np.bincount(low_label.astype(np.int64).ravel(), minlength=NSHELL)
    rank = np.zeros(special.shape, np.int64)
    for r in range(n_row):
        rows = special[r * wx : (r + 1) * wx]
        rank[r * wx : (r + 1) * wx] = np.cumsum(rows, axis=0) - rows
    per = int(rank[special].max()) + 1
    section = 8 * (-(-(n_row * per) // 8))
    total = 128 * (-(-int(special.sum()) // 128))
    put = np.zeros((n_row * per, total))
    lanes_of = np.zeros((total, full_y))
    mark_row = np.zeros((2, hrows, total))
    mark_col = np.zeros((lanes, total))
    step = np.zeros((total, NSHELL))
    for entry, (kx, ky) in enumerate(np.argwhere(special).tolist()):
        ax, ay = abs(int(signed_x[kx])), abs(int(signed_y[ky]))
        same = int(signed_x[kx]) * int(signed_y[ky]) >= 0 or ax == half_x or ay == half_y
        put[kx // wx * per + rank[kx, ky], entry] = 1
        lanes_of[entry, ky] = 1
        mark_row[0 if same else 1, ax, entry] = 1
        mark_col[ay, entry] = 1
        step[entry, root[kx, ky]] += 1
        step[entry, root[kx, ky] - 1] -= 1
    return dict(
        per=per,
        section=section,
        table_y=bf16_table(table_y),
        move=move,
        mult_y=mult_y.astype(np.float32),
        counts=counts.astype(np.float32)[None, :],
        put=np.asarray(put, np.float32),
        lanes_of=bf16_table(lanes_of.T),
        mark_row=np.asarray(mark_row, np.float32),
        mark_col=bf16_table(mark_col),
        step=np.asarray(step, np.float32),
    )


def turn_table(steps, full):
    quarter = (4 * steps + full // 2) // full
    rest = (steps - quarter * (full // 4)).astype(F32) * F32(2.0 * math.pi / full)
    square = rest * rest
    cos, sin = F32(1.0), F32(1.0)
    for order in (8, 6, 4, 2):
        cos = 1.0 - square * cos * F32(1.0 / (order * (order - 1)))
        sin = 1.0 - square * sin * F32(1.0 / (order * (order + 1)))
    sin = sin * rest
    odd = quarter % 2 == 1
    cos, sin = jnp.where(odd, sin, cos), jnp.where(odd, cos, sin)
    cos = jnp.where((quarter == 1) | (quarter == 2), -cos, cos)
    return cos, jnp.where((quarter == 2) | (quarter == 3), -sin, sin)


def x_table(row, n_row, wx):
    full_x = n_row * wx
    half_x = full_x // 2
    freq = lax.broadcasted_iota(jnp.int32, (full_x, full_x), 0)
    lane = lax.broadcasted_iota(jnp.int32, (full_x, full_x), 1)
    pos = (lane // wx ^ row) * wx + lane % wx
    is_cos = freq <= half_x
    cos, sin = turn_table(jnp.where(is_cos, freq, freq - half_x) * pos % full_x, full_x)
    return jnp.where(is_cos, cos, -sin).astype(BF16)


def planes_kernel(n_row, own_ref, col_ref, table_ref):
    _, depth, wx, _ = own_ref.shape
    for c in range(2):
        for z in range(depth):
            at = (c * depth + z) * wx
            col_ref[at : at + wx] = own_ref[c, z].astype(BF16)
    table_ref[...] = x_table(lax.axis_index("row"), n_row, wx)


def pack_kernel(n_row, n_sec, per, own_ref, row_ref):
    _, depth, wx, wy = own_ref.shape
    edges = []
    densities = [[own_ref[c, z] for z in range(depth)] for c in range(2)]
    for c in range(2):
        for z in range(depth):
            tile = densities[c][z]
            edges += [tile[0:2], tile[wx - 2 : wx]]
    for z in range(depth):
        row_ref[z * wx : (z + 1) * wx] = (densities[0][z] - densities[1][z]).astype(BF16)
    edge = jnp.concatenate(edges, axis=0).astype(BF16)
    at = depth * wx
    count = edge.shape[0]
    row_ref[at : at + count] = edge

    row, sec = lax.axis_index("row"), lax.axis_index("sec")
    square, root = shell_root(row * wx, sec * wy, wx * n_row, wy * n_sec, wx, wy)
    special = (root * root == square + 1.0) & (root < NSHELL) & (square > 0.0)
    nudge = jnp.where(special, own_ref[2, 0] - (root - 1.0), 0.0)
    one = jnp.where(special, F32(1.0), F32(0.0)).astype(BF16)
    down = lax.broadcasted_iota(jnp.int32, (wx, wx), 0)
    above = (lax.broadcasted_iota(jnp.int32, (wx, wx), 1) < down).astype(F32).astype(BF16)
    rank = jnp.dot(above, one, preferred_element_type=F32)
    section = row_ref.shape[0] - at - count
    line = lax.broadcasted_iota(jnp.int32, (section, wy), 0)
    marks = jnp.zeros((section, wy), F32)
    for number in range(per):
        found = jnp.sum(jnp.where(rank == number, nudge, 0.0), axis=0, keepdims=True)
        marks = jnp.where(line == row * per + number, found, marks)
    row_ref[at + count :] = marks.astype(BF16)


def shell_root(first_x, first_y, full_x, full_y, wx, wy):
    kx = first_x + lax.broadcasted_iota(jnp.int32, (wx, wy), 0)
    ky = first_y + lax.broadcasted_iota(jnp.int32, (wx, wy), 1)
    kx = jnp.where(kx < full_x // 2, kx, kx - full_x)
    ky = jnp.where(ky < full_y // 2, ky, ky - full_y)
    square = (kx * kx + ky * ky).astype(F32)
    return square, jnp.floor(jnp.sqrt(square + 1.0) + 0.5)


def half_kernel(depth, wx, n_row, *refs):
    row_refs, table_ref, bulk_ref = refs[:n_row], refs[n_row], refs[n_row + 1]
    full_x = table_ref.shape[0]
    for z in range(depth):
        lines = jnp.concatenate([r[z * wx : (z + 1) * wx] for r in row_refs], axis=0)
        half = jnp.dot(table_ref[...], lines, preferred_element_type=F32)
        bulk_ref[z * full_x : (z + 1) * full_x] = half.astype(BF16)
    at = depth * wx + 8 * depth
    marks = sum(ref[at:].astype(F32) for ref in row_refs)
    bulk_ref[depth * full_x : depth * full_x + marks.shape[0]] = marks.astype(BF16)
    rest = depth * full_x + marks.shape[0]
    if rest < bulk_ref.shape[0]:
        bulk_ref[rest:] = jnp.zeros((bulk_ref.shape[0] - rest, bulk_ref.shape[1]), BF16)


def edges_of(col_ref, wx):
    lines = []
    for start in range(0, col_ref.shape[0], wx):
        lines.append(col_ref[start : start + 16].astype(F32)[:2])
        lines.append(col_ref[start + wx - 16 : start + wx].astype(F32)[14:])
    return jnp.concatenate(lines, axis=0)


def middle_kernel(n_row, n_col, section, names, own_ref, row_ref, *refs):
    _, depth, wx, wy = own_ref.shape
    col_moves, row_moves = len(ring_moves(n_col)), len(ring_moves(n_row))
    by_name, refs = dict(zip(names, refs)), refs[len(names) :]
    bulk_ref, msg_ref, strip_ref, dens_ref, lanes_ref = refs
    col_refs = [by_name["col", i] for i in range(col_moves)]
    row_refs = [row_ref] + [by_name["row", k] for k in range(1, n_row)]
    diag_refs = [by_name["diag", i] for i in range(col_moves * row_moves)]
    row, col = lax.axis_index("row"), lax.axis_index("col")
    at = depth * wx
    count = 8 * depth
    col_prev, col_next = ring_pick(n_col, col)
    before = choose([r[...].astype(F32) for r in col_refs], col_prev)
    after = choose([r[...].astype(F32) for r in col_refs], col_next)
    edge_list = [r[at : at + count].astype(F32) for r in row_refs]
    edge_prev = choose(edge_list, row ^ lax.rem(row + n_row - 1, n_row)) if n_row > 2 else edge_list[1]
    edge_next = choose(edge_list, row ^ lax.rem(row + 1, n_row)) if n_row > 2 else edge_list[1]
    row_prev, row_next = ring_pick(n_row, row)
    diag = [
        r[at : at + count].astype(F32) if r.shape == row_ref.shape else edges_of(r, wx)
        for r in diag_refs
    ]

    def diag_of(row_which, col_which):
        lines = [
            choose(diag[m * col_moves : (m + 1) * col_moves], col_which) for m in range(row_moves)
        ]
        return choose(lines, row_which)

    corner = {
        (0, -1): diag_of(row_prev, col_prev),
        (0, 1): diag_of(row_prev, col_next),
        (1, -1): diag_of(row_next, col_prev),
        (1, 1): diag_of(row_next, col_next),
    }
    lane = lax.broadcasted_iota(jnp.int32, (ROWS, wy), 1)
    gap = jnp.zeros((ROWS - wx - 4, wy), F32)
    strips = jnp.zeros((ROWS, wy), F32)
    layers = depth + 4
    for c in range(2):
        for layer in range(layers):
            z = layer - 2
            if z < 0:
                source, plane, low, high = before, depth + z, corner[0, -1], corner[1, -1]
            elif z >= depth:
                source, plane, low, high = after, z - depth, corner[0, 1], corner[1, 1]
            else:
                source, plane, low, high = None, z, edge_prev, edge_next
            where = c * depth + plane
            if source is None:
                body = own_ref[c, plane]
            else:
                body = source[where * wx : (where + 1) * wx]
            tail = jnp.concatenate(
                [high[where * 4 : where * 4 + 2], gap, low[where * 4 + 2 : where * 4 + 4]], axis=0
            )
            tile = jnp.concatenate([body, tail], axis=0)
            group = c * layers + layer
            dens_ref[group] = tile
            at_lane = 8 * group
            moved = pltpu.roll(tile, (at_lane + 2) % wy, 1)
            strips = jnp.where((lane >= at_lane) & (lane < at_lane + 4), moved, strips)
    lanes_ref[...] = strips + pltpu.roll(strips, 4, 1)
    lower = jnp.concatenate([strips[TOP:], jnp.zeros((2 * TOP - ROWS, wy), F32)], axis=0)
    folded = strips[:TOP] + pltpu.roll(lower, 4, 1)
    gap = jnp.zeros((strip_ref.shape[0] - TOP, wy), F32)
    strip_ref[...] = jnp.concatenate([folded, gap], axis=0).astype(BF16)
    at = msg_ref.shape[0] - whole(section + TOP)
    msg_ref[:at] = bulk_ref[:at]
    parts = [bulk_ref[at : at + whole(section)].astype(F32)[:section], folded]
    missing = msg_ref.shape[0] - at - section - TOP
    if missing:
        parts.append(jnp.zeros((missing, wy), F32))
    msg_ref[at:] = jnp.concatenate(parts, axis=0).astype(BF16)


def turn(tile, shift, axis):
    shift = shift % tile.shape[axis]
    return tile if shift == 0 else pltpu.roll(tile, shift, axis)


def pull_of(below, here, above):
    around = below + above
    line_y = turn(here, -1, 1) + turn(here, 1, 1)
    line_x = turn(here, -1, 0) + turn(here, 1, 0)
    flat = 2.0 * here + around
    mix = flat + line_y
    pull_x = turn(mix, -1, 0) - turn(mix, 1, 0)
    mix = flat + line_x
    pull_y = turn(mix, -1, 1) - turn(mix, 1, 1)
    gap = above - below
    pull_z = 2.0 * gap + turn(gap, -1, 0) + turn(gap, 1, 0) + turn(gap, -1, 1) + turn(gap, 1, 1)
    return pull_x, pull_y, pull_z


def relax_terms(density, velocity):
    vx, vy, vz = velocity
    squared = vx * vx + vy * vy + vz * vz
    rest = density * (1.0 - 1.875 * squared)
    terms = [WEIGHTS[0] * rest]
    for number in range(1, 19, 2):
        offsets = LATTICE[number]
        projected = None
        for axis in range(3):
            if offsets[axis]:
                part = velocity[axis] if offsets[axis] > 0 else -velocity[axis]
                projected = part if projected is None else projected + part
        weighted = density * projected
        even = WEIGHTS[number] * (rest + 5.625 * (weighted * projected))
        odd = (WEIGHTS[number] * 3.75) * weighted
        terms += [even + odd, even - odd]
    return terms


def cells_kernel(dens_ref, out_ref):
    _, depth, wx, _ = out_ref.shape
    layers = depth + 4
    scale = -1.6 / 36.0
    for layer in range(1, layers - 1):
        for c in range(2):
            other = (1 - c) * layers + layer
            pulls = pull_of(dens_ref[other - 1], dens_ref[other], dens_ref[other + 1])
            velocity = [scale * p for p in pulls]
            terms = relax_terms(dens_ref[c * layers + layer], velocity)
            for number in range(19):
                cx, cy, cz = LATTICE[number]
                z = layer - 2 + cz
                if 0 <= z < depth:
                    tile = turn(turn(terms[number], cx, 0), cy, 1)
                    out_ref[c * 19 + number, z] = tile[:wx]


def set_ends(n_sec, start, at, msg_refs, lanes_ref, cells_ref, out_hbm, out_ref, sems):
    _, depth, wx, wy = out_ref.shape
    layers = depth + 4
    strips = [
        r[:].astype(F32)[:TOP] if r.shape[0] < start else r[start:].astype(F32)[at - start :][:TOP]
        for r in msg_refs
    ]
    index = lax.axis_index("sec")
    prev_which, next_which = ring_pick(n_sec, index)
    before, after = choose(strips, prev_which), choose(strips, next_which)
    rest = ROWS - TOP
    before = jnp.concatenate([before, turn(before, -4, 1)[:rest]], axis=0)
    after = jnp.concatenate([turn(after, 4, 1), after[:rest]], axis=0)
    place = lax.rem(lax.broadcasted_iota(jnp.int32, (ROWS, wy), 1), 8)
    tile = jnp.where(place < 2, before, jnp.where(place >= 6, after, lanes_ref[...]))
    pulls = pull_of(turn(tile, 8, 1), tile, turn(tile, -8, 1))
    span = 8 * layers
    first = lax.broadcasted_iota(jnp.int32, (ROWS, wy), 1) < span
    scale = -1.6 / 36.0
    velocity = [scale * jnp.where(first, turn(p, -span, 1), turn(p, span, 1)) for p in pulls]
    terms = relax_terms(tile, velocity)
    lane = lax.broadcasted_iota(jnp.int32, (wx, wy), 1)
    copies = []
    moved = []
    for number in range(19):
        cx, cy, cz = LATTICE[number]
        term = turn(terms[number], cx, 0)[:wx]
        if cy == 0:
            term = jnp.where(place[:wx] == 1, turn(term, -4, 1), term)
        moved.append(term)
    masks = {1: lane < 2, -1: lane >= wy - 2, 0: (lane == 0) | (lane == wy - 1)}
    begin = 0
    for q in range(38):
        c, number = divmod(q, 19)
        _, cy, cz = LATTICE[number]
        for z in range(depth):
            group = 8 * (c * layers + 2 + z - cz)
            back = {1: group + 1, -1: group + 5 - (wy - 2), 0: group + 2}[cy]
            out_ref[q, z] = jnp.where(masks[cy], turn(moved[number], -back, 1), cells_ref[q, z])
        if q + 1 in ENDS:
            span = pl.ds(begin, q + 1 - begin)
            copy = pltpu.make_async_copy(
                out_ref.at[span], out_hbm.at[span], sems.at[len(copies)]
            )
            copy.start()
            copies.append(copy)
            begin = q + 1
    return copies


def final_kernel(n_sec, section, move, msg_own_ref, *refs):
    msg_refs = [msg_own_ref] + [refs[swap_order(n_sec).index(k)] for k in range(1, n_sec)]
    refs = refs[n_sec - 1 :]
    ring = []
    for move_ in ring_moves(n_sec):
        k = move_[0][1]
        if k in EARLY.get(n_sec, ()):
            ring.append(refs[0])
            refs = refs[1:]
        else:
            ring.append(msg_refs[k])
    (strips_ref, cells_ref), refs = refs[:2], refs[2:]
    (table_ref, move_ref, mult_ref, counts_ref, put_ref, lanes_ref, row_ref, col_ref, step_ref,
     out_hbm, spec_hbm, lhs_ref, mark_ref, part_ref, out_ref, spec_ref, sems) = refs
    depth = spec_ref.shape[0]
    sec = lax.axis_index("sec")
    full_y, lanes = table_ref.shape[0], table_ref.shape[1] // 2
    wy = full_y // n_sec
    full_x = lhs_ref.shape[0] // depth
    half_x = full_x // 2
    hrows = half_x + 8
    at = depth * full_x
    lines_used = put_ref.shape[0]
    copies = set_ends(n_sec, at, at + section, ring, strips_ref, cells_ref, out_hbm, out_ref, sems)

    for k in range(n_sec):
        start = pl.multiple_of((sec ^ k) * wy, wy)
        lhs_ref[:, pl.ds(start, wy)] = msg_refs[k][:at]
        mark_ref[:, pl.ds(start, wy)] = msg_refs[k][at : at + mark_ref.shape[0]]
    transform = jnp.dot(lhs_ref[...], table_ref[...], preferred_element_type=F32)

    found = jnp.dot(mark_ref[...], lanes_ref[...], preferred_element_type=F32)
    nudge = jnp.sum(found[:lines_used] * put_ref[...], axis=0, keepdims=True)

    mult = mult_ref[...]
    row_zero = lax.broadcasted_iota(jnp.int32, (half_x, lanes), 0) == 0
    rest = jnp.zeros((7, lanes), F32)
    picks = []
    for z in range(depth):
        real = transform[z * full_x : z * full_x + half_x]
        imag = transform[z * full_x + half_x : (z + 1) * full_x]
        rc, rs = real[:, :lanes], real[:, lanes:]
        ic, is_ = imag[:, :lanes], imag[:, lanes:]
        top = rc * rc + rs * rs
        low = ic * ic + is_ * is_
        both = top + low
        cross = 2.0 * (rc * is_ - ic * rs)
        part_ref[z, :half_x] = mult * jnp.where(row_zero, top, 2.0 * both)
        part_ref[z, half_x:] = jnp.concatenate([mult * low[0:1], rest], axis=0)
        plus = jnp.concatenate([jnp.where(row_zero, top, both + cross), low[0:1], rest], axis=0)
        minus = jnp.concatenate([both - cross, low[0:1], rest], axis=0)
        value = 0.0
        for number, power in enumerate((plus, minus)):
            head = power.astype(BF16)
            tail = (power - head.astype(F32)).astype(BF16)
            found = jnp.dot(head, col_ref[...], preferred_element_type=F32) + jnp.dot(
                tail, col_ref[...], preferred_element_type=F32
            )
            value = value + jnp.sum(found * row_ref[number], axis=0, keepdims=True)
        picks.append(value)
    picks.append(jnp.ones_like(picks[0]))
    picks.append(jnp.zeros((8 - len(picks), picks[0].shape[1]), F32))
    moved = lax.dot_general(
        jnp.concatenate(picks, axis=0) * nudge, step_ref[...], (((1,), (0,)), ((), ())),
        precision=lax.Precision.HIGHEST, preferred_element_type=F32,
    )

    tiles = NSHELL // 128
    lane = lax.broadcasted_iota(jnp.int32, (8, 128), 1)
    sums = [[jnp.zeros((8, 128), F32) for _ in range(tiles)] for _ in range(depth)]
    for tile in range(lanes // 128):
        block = move[:, tile * 128 : (tile + 1) * 128]
        at_lanes = slice(tile * 128, (tile + 1) * 128)
        for value in np.unique(block):
            if value == UNUSED:
                continue
            value = int(value)
            totals = [None] * depth
            for group in range(hrows // 8):
                if not (block[group * 8 : group * 8 + 8] == value).any():
                    continue
                rows = slice(group * 8, group * 8 + 8)
                same = move_ref[rows, at_lanes] == value
                for z in range(depth):
                    term = jnp.where(same, part_ref[z, rows, at_lanes], 0.0)
                    totals[z] = term if totals[z] is None else totals[z] + term
            shift = value % 128
            goal = tile + value // 128
            for z in range(depth):
                total = turn(totals[z], shift, 1)
                if 0 <= goal < tiles:
                    sums[z][goal] += jnp.where(lane >= shift, total, 0.0)
                if shift and 0 <= goal + 1 < tiles:
                    sums[z][goal + 1] += jnp.where(lane < shift, total, 0.0)
    norm = (counts_ref[...] + moved[depth : depth + 1]) * float(full_x * full_y)
    lines = []
    for z in range(depth):
        line = jnp.sum(jnp.concatenate(sums[z], axis=1), axis=0, keepdims=True)
        lines.append((line + moved[z : z + 1]) / norm)
    spec_ref[...] = jnp.concatenate(lines, axis=0)
    copies.append(pltpu.make_async_copy(spec_ref, spec_hbm, sems.at[len(ENDS)]))
    copies[-1].start()
    for copy in copies:
        copy.wait()


def call(kernel, outs, scratch=(), flops=0, moved=0, limit=48 << 20, **specs):
    return pl.pallas_call(
        kernel,
        out_shape=outs,
        scratch_shapes=list(scratch),
        compiler_params=pltpu.CompilerParams(vmem_limit_bytes=limit),
        cost_estimate=pl.CostEstimate(flops=flops, bytes_accessed=moved, transcendentals=0),
        **specs,
    )


def on_device(n_sec, n_row, n_col, labels, jitter, shells):
    depth, wx, wy = labels.shape
    full_x, full_y = wx * n_row, wy * n_sec
    tables = make_tables(full_x, full_y, n_row, n_sec, wx, wy)
    per, section = tables["per"], tables["section"]
    layers = depth + 4
    count = 8 * depth
    shape = jax.ShapeDtypeStruct

    part = lax.broadcasted_iota(jnp.int32, (3, depth, wx, wy), 0)
    none = (0, 0, 0)
    factor = lax.pad(jitter, F32(0.0), ((0, 1, 0), none, none, none))
    whole_numbers = jnp.where(part == 2, shells[None, None], labels[None] ^ part)
    density = jnp.where(whole_numbers == 1, F32(1.0), F32(0.2)) * factor
    own = jnp.where(part == 2, whole_numbers.astype(F32), density)
    row_msg = call(
        functools.partial(pack_kernel, n_row, n_sec, per),
        shape((depth * wx + count + whole(section), wy), BF16),
    )(own)
    col_msg, table_x = call(
        functools.partial(planes_kernel, n_row),
        [shape((2 * depth * wx, wy), BF16), shape((full_x, full_x), BF16)],
    )(own)

    col_got = [lax.ppermute(col_msg, "col", m) for m in ring_moves(n_col)]
    row_got = [lax.ppermute(row_msg, "row", xor_pairs(n_row, k)) for k in range(1, n_row)]
    relay = n_row == 2 and n_col == 4
    diag_got = []
    for a in ring_moves(n_row):
        for b in ring_moves(n_col):
            if relay and b == xor_pairs(n_col, 1):
                diag_got.append(lax.ppermute(row_got[0], "col", b))
            else:
                move = pair_product(a, b, n_col)
                diag_got.append(lax.ppermute(col_msg, ("row", "col"), move))

    at = depth * full_x
    got = {("col", i): value for i, value in enumerate(col_got)}
    got.update({("row", k + 1): value for k, value in enumerate(row_got)})
    got.update({("diag", i): value for i, value in enumerate(diag_got)})
    names = [name for name in FIRST_ROUND if name in got]
    names += [name for name in got if name not in names]
    bulk = call(
        functools.partial(half_kernel, depth, wx, n_row), shape((at + whole(section + TOP), wy), BF16),
        flops=1 << 27, moved=1 << 24
    )(row_msg, *row_got, table_x)
    msg, strip, dens, lanes_own = call(
        functools.partial(middle_kernel, n_row, n_col, section, tuple(names)),
        [
            shape((at + whole(section + TOP), wy), BF16),
            shape((whole(TOP), wy), BF16),
            shape((2 * layers, ROWS, wy), F32),
            shape((ROWS, wy), F32),
        ],
        flops=MID,
        moved=MID,
    )(own, row_msg, *[got[name] for name in names], bulk)

    ring = ring_moves(n_sec)
    early = EARLY.get(n_sec, ())
    sec_got, strip_got = [], []
    for k in swap_order(n_sec):
        move = xor_pairs(n_sec, k)
        with_columns = move in ring and k not in early
        sec_got.append(lax.ppermute(msg if with_columns else bulk, "sec", move))
    for move in ring:
        if move[0][1] in early:
            strip_got.append(lax.ppermute(strip, "sec", move))

    cells = call(
        cells_kernel,
        shape((38, depth, wx, wy), F32),
        flops=LBM,
        moved=LBM,
    )(dens)

    hrows, lanes = full_x // 2 + 8, full_y // 2 + 128
    names = ("mult_y", "counts", "put", "lanes_of", "mark_row", "mark_col", "step")
    return call(
        functools.partial(final_kernel, n_sec, section, tables["move"]),
        [shape((38, depth, wx, wy), F32), shape((depth, NSHELL), F32)],
        [
            pltpu.VMEM((depth * full_x, full_y), BF16),
            pltpu.VMEM((whole(section), full_y), BF16),
            pltpu.VMEM((depth, hrows, lanes), F32),
            pltpu.VMEM((38, depth, wx, wy), F32),
            pltpu.VMEM((depth, NSHELL), F32),
            pltpu.SemaphoreType.DMA((len(ENDS) + 1,)),
        ],
        out_specs=[pl.BlockSpec(memory_space=pltpu.HBM)] * 2,
    )(bulk, *sec_got, *strip_got, lanes_own, cells, tables["table_y"], tables["move"].astype(np.int32),
      *[tables[name] for name in names])


def solution(mesh):
    in_specs = (P("col", "row", "sec"), P(None, "col", "row", "sec"), P("row", "sec"))
    out_specs = (P(None, "col", "row", "sec"), P("col", None))
    sizes = [mesh.shape[name] for name in ("sec", "row", "col")]
    return jax.shard_map(
        functools.partial(on_device, *sizes),
        mesh=mesh,
        in_specs=in_specs,
        out_specs=out_specs,
        check_vma=False,
    )
```

```python
import functools
import math

import jax
import jax.numpy as jnp
import ml_dtypes
import numpy as np
from jax import lax
from jax.experimental import pallas as pl
from jax.experimental.pallas import tpu as pltpu
from jax.sharding import PartitionSpec as P

NSHELL = 256
UNUSED = -(1 << 20)
MID = 1 << 24
LBM = 1 << 10
ENDS = (10, 19, 29, 38)
FIRST_ROUND = (("col", 0), ("diag", 0), ("row", 1), ("col", 1), ("diag", 1))
SWAPS = {4: (3, 1, 2)}
EARLY = {4: (1, 2)}
TOP = 40
ROWS = 72
F32 = jnp.float32
BF16 = jnp.bfloat16

LATTICE = (
    (0, 0, 0),
    (1, 0, 0),
    (-1, 0, 0),
    (0, 1, 0),
    (0, -1, 0),
    (0, 0, 1),
    (0, 0, -1),
    (1, 1, 0),
    (-1, -1, 0),
    (1, -1, 0),
    (-1, 1, 0),
    (1, 0, 1),
    (-1, 0, -1),
    (1, 0, -1),
    (-1, 0, 1),
    (0, 1, 1),
    (0, -1, -1),
    (0, 1, -1),
    (0, -1, 1),
)
WEIGHTS = (1.0 / 3.0,) + (1.0 / 18.0,) * 6 + (1.0 / 36.0,) * 12


def xor_pairs(count, bits):
    return [(i, i ^ bits) for i in range(count)]


def shift_pairs(count, step):
    return [(i, (i + step) % count) for i in range(count)]


def ring_moves(count):
    if count == 2:
        return [xor_pairs(2, 1)]
    if count == 4:
        return [xor_pairs(4, 1), xor_pairs(4, 3)]
    return [shift_pairs(count, 1), shift_pairs(count, -1)]


def ring_pick(count, index):
    if count == 2:
        return 0, 0
    if count == 4:
        odd = lax.rem(index, 2)
        return 1 - odd, odd
    return 0, 1


def swap_order(count):
    return SWAPS.get(count, tuple(range(1, count)))


def pair_product(first, second, count_second):
    return [
        (a * count_second + b, c * count_second + d) for a, c in first for b, d in second
    ]


def whole(rows):
    return 16 * (-(-rows // 16))


def choose(items, which):
    if isinstance(which, int):
        return items[which]
    value = items[0]
    for number in range(1, len(items)):
        value = jnp.where(which == number, items[number], value)
    return value


def bf16_table(values):
    return np.asarray(values, np.float32).astype(ml_dtypes.bfloat16)


def angle_table(freq, pos, full):
    step = np.float32(2.0 * math.pi / full)
    return ((freq * pos) % full).astype(np.float32) * step


@functools.lru_cache(maxsize=None)
def make_tables(full_x, full_y, n_row, n_sec, wx, wy):
    half_x, half_y = full_x // 2, full_y // 2
    lanes = half_y + 128
    freq_y = np.arange(lanes)[None, :]
    angles = angle_table(np.arange(full_y)[:, None], freq_y, full_y)
    live = freq_y <= half_y
    table_y = np.concatenate([np.cos(angles) * live, np.sin(angles) * live], 1)
    hrows = half_x + 8
    radius = np.arange(hrows)[:, None] ** 2 + np.arange(lanes)[None, :] ** 2
    base = np.minimum(np.floor(np.sqrt(radius.astype(np.float64))).astype(np.int64), NSHELL - 1)
    valid = (np.arange(hrows)[:, None] <= half_x) & (np.arange(lanes)[None, :] <= half_y)
    move = np.where(valid, base - np.arange(lanes)[None, :], UNUSED)
    mult_y = np.where(freq_y > half_y, 0, np.where((freq_y == 0) | (freq_y == half_y), 1, 2))
    signed_x = np.arange(full_x)
    signed_x = np.where(signed_x < half_x, signed_x, signed_x - full_x)
    signed_y = np.arange(full_y)
    signed_y = np.where(signed_y < half_y, signed_y, signed_y - full_y)
    square = signed_x[:, None] ** 2 + signed_y[None, :] ** 2
    root = np.floor(np.sqrt(square + 1.0) + 1e-9).astype(np.int64)
    special = (root * root == square + 1) & (root < NSHELL) & (square > 0)
    low_label = np.minimum(np.floor(np.sqrt(square.astype(np.float64))), NSHELL - 1)
    counts = np.bincount(low_label.astype(np.int64).ravel(), minlength=NSHELL)
    rank = np.zeros(special.shape, np.int64)
    for r in range(n_row):
        rows = special[r * wx : (r + 1) * wx]
        rank[r * wx : (r + 1) * wx] = np.cumsum(rows, axis=0) - rows
    per = int(rank[special].max()) + 1
    section = 8 * (-(-(n_row * per) // 8))
    total = 128 * (-(-int(special.sum()) // 128))
    put = np.zeros((n_row * per, total))
    lanes_of = np.zeros((total, full_y))
    mark_row = np.zeros((2, hrows, total))
    mark_col = np.zeros((lanes, total))
    step = np.zeros((total, NSHELL))
    for entry, (kx, ky) in enumerate(np.argwhere(special).tolist()):
        ax, ay = abs(int(signed_x[kx])), abs(int(signed_y[ky]))
        same = int(signed_x[kx]) * int(signed_y[ky]) >= 0 or ax == half_x or ay == half_y
        put[kx // wx * per + rank[kx, ky], entry] = 1
        lanes_of[entry, ky] = 1
        mark_row[0 if same else 1, ax, entry] = 1
        mark_col[ay, entry] = 1
        step[entry, root[kx, ky]] += 1
        step[entry, root[kx, ky] - 1] -= 1
    parts = (mult_y, counts[None, :], put, mark_row.reshape(2 * hrows, total), step, move)
    wide = max(p.shape[1] for p in parts)
    small, places = [], []
    for part in parts:
        rows = 8 * (-(-part.shape[0] // 8))
        places.append(sum(p.shape[0] for p in small))
        filled = np.zeros((rows, wide), np.float32)
        filled[: part.shape[0], : part.shape[1]] = part
        small.append(filled)
    columns = np.zeros((full_y, total))
    columns[:lanes] = mark_col
    return dict(
        per=per,
        section=section,
        total=total,
        move=move,
        places=tuple(places),
        small=np.concatenate(small, axis=0),
        large=np.concatenate([table_y, lanes_of.T, columns], axis=1).astype(ml_dtypes.bfloat16),
    )


def turn_table(steps, full):
    quarter = (4 * steps + full // 2) // full
    rest = (steps - quarter * (full // 4)).astype(F32) * F32(2.0 * math.pi / full)
    square = rest * rest
    cos, sin = F32(1.0), F32(1.0)
    for order in (8, 6, 4, 2):
        cos = 1.0 - square * cos * F32(1.0 / (order * (order - 1)))
        sin = 1.0 - square * sin * F32(1.0 / (order * (order + 1)))
    sin = sin * rest
    odd = quarter % 2 == 1
    cos, sin = jnp.where(odd, sin, cos), jnp.where(odd, cos, sin)
    cos = jnp.where((quarter == 1) | (quarter == 2), -cos, cos)
    return cos, jnp.where((quarter == 2) | (quarter == 3), -sin, sin)


def x_table(row, n_row, wx):
    full_x = n_row * wx
    half_x = full_x // 2
    freq = lax.broadcasted_iota(jnp.int32, (full_x, full_x), 0)
    lane = lax.broadcasted_iota(jnp.int32, (full_x, full_x), 1)
    pos = (lane // wx ^ row) * wx + lane % wx
    is_cos = freq <= half_x
    cos, sin = turn_table(jnp.where(is_cos, freq, freq - half_x) * pos % full_x, full_x)
    return jnp.where(is_cos, cos, -sin).astype(BF16)


def planes_kernel(n_row, own_ref, col_ref, table_ref):
    _, depth, wx, _ = own_ref.shape
    for c in range(2):
        for z in range(depth):
            at = (c * depth + z) * wx
            col_ref[at : at + wx] = own_ref[c, z].astype(BF16)
    table_ref[...] = x_table(lax.axis_index("row"), n_row, wx)


def pack_kernel(n_row, n_sec, per, own_ref, row_ref):
    _, depth, wx, wy = own_ref.shape
    edges = []
    densities = [[own_ref[c, z] for z in range(depth)] for c in range(2)]
    for c in range(2):
        for z in range(depth):
            tile = densities[c][z]
            edges += [tile[0:2], tile[wx - 2 : wx]]
    for z in range(depth):
        row_ref[z * wx : (z + 1) * wx] = (densities[0][z] - densities[1][z]).astype(BF16)
    edge = jnp.concatenate(edges, axis=0).astype(BF16)
    at = depth * wx
    count = edge.shape[0]
    row_ref[at : at + count] = edge

    row, sec = lax.axis_index("row"), lax.axis_index("sec")
    square, root = shell_root(row * wx, sec * wy, wx * n_row, wy * n_sec, wx, wy)
    special = (root * root == square + 1.0) & (root < NSHELL) & (square > 0.0)
    nudge = jnp.where(special, own_ref[2, 0] - (root - 1.0), 0.0)
    one = jnp.where(special, F32(1.0), F32(0.0)).astype(BF16)
    down = lax.broadcasted_iota(jnp.int32, (wx, wx), 0)
    above = (lax.broadcasted_iota(jnp.int32, (wx, wx), 1) < down).astype(F32).astype(BF16)
    rank = jnp.dot(above, one, preferred_element_type=F32)
    section = row_ref.shape[0] - at - count
    line = lax.broadcasted_iota(jnp.int32, (section, wy), 0)
    marks = jnp.zeros((section, wy), F32)
    for number in range(per):
        found = jnp.sum(jnp.where(rank == number, nudge, 0.0), axis=0, keepdims=True)
        marks = jnp.where(line == row * per + number, found, marks)
    row_ref[at + count :] = marks.astype(BF16)


def shell_root(first_x, first_y, full_x, full_y, wx, wy):
    kx = first_x + lax.broadcasted_iota(jnp.int32, (wx, wy), 0)
    ky = first_y + lax.broadcasted_iota(jnp.int32, (wx, wy), 1)
    kx = jnp.where(kx < full_x // 2, kx, kx - full_x)
    ky = jnp.where(ky < full_y // 2, ky, ky - full_y)
    square = (kx * kx + ky * ky).astype(F32)
    return square, jnp.floor(jnp.sqrt(square + 1.0) + 0.5)


def half_kernel(depth, wx, n_row, *refs):
    row_refs, table_ref, bulk_ref = refs[:n_row], refs[n_row], refs[n_row + 1]
    full_x = table_ref.shape[0]
    for z in range(depth):
        lines = jnp.concatenate([r[z * wx : (z + 1) * wx] for r in row_refs], axis=0)
        half = jnp.dot(table_ref[...], lines, preferred_element_type=F32)
        bulk_ref[z * full_x : (z + 1) * full_x] = half.astype(BF16)
    at = depth * wx + 8 * depth
    marks = sum(ref[at:].astype(F32) for ref in row_refs)
    bulk_ref[depth * full_x : depth * full_x + marks.shape[0]] = marks.astype(BF16)
    rest = depth * full_x + marks.shape[0]
    if rest < bulk_ref.shape[0]:
        bulk_ref[rest:] = jnp.zeros((bulk_ref.shape[0] - rest, bulk_ref.shape[1]), BF16)


def edges_of(col_ref, wx):
    lines = []
    for start in range(0, col_ref.shape[0], wx):
        lines.append(col_ref[start : start + 16].astype(F32)[:2])
        lines.append(col_ref[start + wx - 16 : start + wx].astype(F32)[14:])
    return jnp.concatenate(lines, axis=0)


def middle_kernel(n_row, n_col, section, names, own_ref, row_ref, *refs):
    _, depth, wx, wy = own_ref.shape
    col_moves, row_moves = len(ring_moves(n_col)), len(ring_moves(n_row))
    by_name, refs = dict(zip(names, refs)), refs[len(names) :]
    bulk_ref, msg_ref, strip_ref, dens_ref, lanes_ref = refs
    col_refs = [by_name["col", i] for i in range(col_moves)]
    row_refs = [row_ref] + [by_name["row", k] for k in range(1, n_row)]
    diag_refs = [by_name["diag", i] for i in range(col_moves * row_moves)]
    row, col = lax.axis_index("row"), lax.axis_index("col")
    at = depth * wx
    count = 8 * depth
    col_prev, col_next = ring_pick(n_col, col)
    before = choose([r[...].astype(F32) for r in col_refs], col_prev)
    after = choose([r[...].astype(F32) for r in col_refs], col_next)
    edge_list = [r[at : at + count].astype(F32) for r in row_refs]
    edge_prev = choose(edge_list, row ^ lax.rem(row + n_row - 1, n_row)) if n_row > 2 else edge_list[1]
    edge_next = choose(edge_list, row ^ lax.rem(row + 1, n_row)) if n_row > 2 else edge_list[1]
    row_prev, row_next = ring_pick(n_row, row)
    diag = [
        r[at : at + count].astype(F32) if r.shape == row_ref.shape else edges_of(r, wx)
        for r in diag_refs
    ]

    def diag_of(row_which, col_which):
        lines = [
            choose(diag[m * col_moves : (m + 1) * col_moves], col_which) for m in range(row_moves)
        ]
        return choose(lines, row_which)

    corner = {
        (0, -1): diag_of(row_prev, col_prev),
        (0, 1): diag_of(row_prev, col_next),
        (1, -1): diag_of(row_next, col_prev),
        (1, 1): diag_of(row_next, col_next),
    }
    lane = lax.broadcasted_iota(jnp.int32, (ROWS, wy), 1)
    gap = jnp.zeros((ROWS - wx - 4, wy), F32)
    strips = jnp.zeros((ROWS, wy), F32)
    layers = depth + 4
    for c in range(2):
        for layer in range(layers):
            z = layer - 2
            if z < 0:
                source, plane, low, high = before, depth + z, corner[0, -1], corner[1, -1]
            elif z >= depth:
                source, plane, low, high = after, z - depth, corner[0, 1], corner[1, 1]
            else:
                source, plane, low, high = None, z, edge_prev, edge_next
            where = c * depth + plane
            if source is None:
                body = own_ref[c, plane]
            else:
                body = source[where * wx : (where + 1) * wx]
            tail = jnp.concatenate(
                [high[where * 4 : where * 4 + 2], gap, low[where * 4 + 2 : where * 4 + 4]], axis=0
            )
            tile = jnp.concatenate([body, tail], axis=0)
            group = c * layers + layer
            dens_ref[group] = tile
            at_lane = 8 * group
            moved = pltpu.roll(tile, (at_lane + 2) % wy, 1)
            strips = jnp.where((lane >= at_lane) & (lane < at_lane + 4), moved, strips)
    lanes_ref[...] = strips + pltpu.roll(strips, 4, 1)
    lower = jnp.concatenate([strips[TOP:], jnp.zeros((2 * TOP - ROWS, wy), F32)], axis=0)
    folded = strips[:TOP] + pltpu.roll(lower, 4, 1)
    gap = jnp.zeros((strip_ref.shape[0] - TOP, wy), F32)
    strip_ref[...] = jnp.concatenate([folded, gap], axis=0).astype(BF16)
    at = msg_ref.shape[0] - whole(section + TOP)
    msg_ref[:at] = bulk_ref[:at]
    parts = [bulk_ref[at : at + whole(section)].astype(F32)[:section], folded]
    missing = msg_ref.shape[0] - at - section - TOP
    if missing:
        parts.append(jnp.zeros((missing, wy), F32))
    msg_ref[at:] = jnp.concatenate(parts, axis=0).astype(BF16)


def turn(tile, shift, axis):
    shift = shift % tile.shape[axis]
    return tile if shift == 0 else pltpu.roll(tile, shift, axis)


def pull_of(below, here, above):
    around = below + above
    line_y = turn(here, -1, 1) + turn(here, 1, 1)
    line_x = turn(here, -1, 0) + turn(here, 1, 0)
    flat = 2.0 * here + around
    mix = flat + line_y
    pull_x = turn(mix, -1, 0) - turn(mix, 1, 0)
    mix = flat + line_x
    pull_y = turn(mix, -1, 1) - turn(mix, 1, 1)
    gap = above - below
    pull_z = 2.0 * gap + turn(gap, -1, 0) + turn(gap, 1, 0) + turn(gap, -1, 1) + turn(gap, 1, 1)
    return pull_x, pull_y, pull_z


def relax_terms(density, velocity):
    vx, vy, vz = velocity
    squared = vx * vx + vy * vy + vz * vz
    rest = density * (1.0 - 1.875 * squared)
    terms = [WEIGHTS[0] * rest]
    for number in range(1, 19, 2):
        offsets = LATTICE[number]
        projected = None
        for axis in range(3):
            if offsets[axis]:
                part = velocity[axis] if offsets[axis] > 0 else -velocity[axis]
                projected = part if projected is None else projected + part
        weighted = density * projected
        even = WEIGHTS[number] * (rest + 5.625 * (weighted * projected))
        odd = (WEIGHTS[number] * 3.75) * weighted
        terms += [even + odd, even - odd]
    return terms


def cells_kernel(dens_ref, out_ref):
    _, depth, wx, _ = out_ref.shape
    layers = depth + 4
    scale = -1.6 / 36.0
    for layer in range(1, layers - 1):
        for c in range(2):
            other = (1 - c) * layers + layer
            pulls = pull_of(dens_ref[other - 1], dens_ref[other], dens_ref[other + 1])
            velocity = [scale * p for p in pulls]
            terms = relax_terms(dens_ref[c * layers + layer], velocity)
            for number in range(19):
                cx, cy, cz = LATTICE[number]
                z = layer - 2 + cz
                if 0 <= z < depth:
                    tile = turn(turn(terms[number], cx, 0), cy, 1)
                    out_ref[c * 19 + number, z] = tile[:wx]


def set_ends(n_sec, start, at, msg_refs, lanes_ref, cells_ref, out_hbm, out_ref, sems):
    _, depth, wx, wy = out_ref.shape
    layers = depth + 4
    strips = [
        r[:].astype(F32)[:TOP] if r.shape[0] < start else r[start:].astype(F32)[at - start :][:TOP]
        for r in msg_refs
    ]
    index = lax.axis_index("sec")
    prev_which, next_which = ring_pick(n_sec, index)
    before, after = choose(strips, prev_which), choose(strips, next_which)
    rest = ROWS - TOP
    before = jnp.concatenate([before, turn(before, -4, 1)[:rest]], axis=0)
    after = jnp.concatenate([turn(after, 4, 1), after[:rest]], axis=0)
    place = lax.rem(lax.broadcasted_iota(jnp.int32, (ROWS, wy), 1), 8)
    tile = jnp.where(place < 2, before, jnp.where(place >= 6, after, lanes_ref[...]))
    pulls = pull_of(turn(tile, 8, 1), tile, turn(tile, -8, 1))
    span = 8 * layers
    first = lax.broadcasted_iota(jnp.int32, (ROWS, wy), 1) < span
    scale = -1.6 / 36.0
    velocity = [scale * jnp.where(first, turn(p, -span, 1), turn(p, span, 1)) for p in pulls]
    terms = relax_terms(tile, velocity)
    lane = lax.broadcasted_iota(jnp.int32, (wx, wy), 1)
    copies = []
    moved = []
    for number in range(19):
        cx, cy, cz = LATTICE[number]
        term = turn(terms[number], cx, 0)[:wx]
        if cy == 0:
            term = jnp.where(place[:wx] == 1, turn(term, -4, 1), term)
        moved.append(term)
    masks = {1: lane < 2, -1: lane >= wy - 2, 0: (lane == 0) | (lane == wy - 1)}
    begin = 0
    for q in range(38):
        c, number = divmod(q, 19)
        _, cy, cz = LATTICE[number]
        for z in range(depth):
            group = 8 * (c * layers + 2 + z - cz)
            back = {1: group + 1, -1: group + 5 - (wy - 2), 0: group + 2}[cy]
            out_ref[q, z] = jnp.where(masks[cy], turn(moved[number], -back, 1), cells_ref[q, z])
        if q + 1 in ENDS:
            span = pl.ds(begin, q + 1 - begin)
            copy = pltpu.make_async_copy(
                out_ref.at[span], out_hbm.at[span], sems.at[len(copies)]
            )
            copy.start()
            copies.append(copy)
            begin = q + 1
    return copies


def final_kernel(n_sec, section, places, total, move, msg_own_ref, *refs):
    msg_refs = [msg_own_ref] + [refs[swap_order(n_sec).index(k)] for k in range(1, n_sec)]
    refs = refs[n_sec - 1 :]
    ring = []
    for move_ in ring_moves(n_sec):
        k = move_[0][1]
        if k in EARLY.get(n_sec, ()):
            ring.append(refs[0])
            refs = refs[1:]
        else:
            ring.append(msg_refs[k])
    (strips_ref, cells_ref), refs = refs[:2], refs[2:]
    (large_ref, small_ref,
     out_hbm, spec_hbm, lhs_ref, mark_ref, part_ref, out_ref, spec_ref, sems) = refs
    depth = spec_ref.shape[0]
    sec = lax.axis_index("sec")
    full_y, lanes = large_ref.shape[0], move.shape[1]
    wy = full_y // n_sec
    full_x = lhs_ref.shape[0] // depth
    half_x = full_x // 2
    hrows = half_x + 8
    at = depth * full_x
    at_mult, at_counts, at_put, at_row, at_step, at_move = places
    copies = set_ends(n_sec, at, at + section, ring, strips_ref, cells_ref, out_hbm, out_ref, sems)

    for k in range(n_sec):
        start = pl.multiple_of((sec ^ k) * wy, wy)
        lhs_ref[:, pl.ds(start, wy)] = msg_refs[k][:at]
        mark_ref[:, pl.ds(start, wy)] = msg_refs[k][at : at + mark_ref.shape[0]]
    transform = jnp.dot(lhs_ref[...], large_ref[:, : 2 * lanes], preferred_element_type=F32)

    find = large_ref[:, 2 * lanes : 2 * lanes + total]
    found = jnp.dot(mark_ref[...], find, preferred_element_type=F32)[:section]
    nudge = jnp.sum(found * small_ref[at_put:at_row, :total], axis=0, keepdims=True)

    mult = small_ref[at_mult : at_mult + 1, :lanes]
    columns = large_ref[:lanes, 2 * lanes + total :]
    row_zero = lax.broadcasted_iota(jnp.int32, (half_x, lanes), 0) == 0
    rest = jnp.zeros((7, lanes), F32)
    picks = []
    for z in range(depth):
        real = transform[z * full_x : z * full_x + half_x]
        imag = transform[z * full_x + half_x : (z + 1) * full_x]
        rc, rs = real[:, :lanes], real[:, lanes:]
        ic, is_ = imag[:, :lanes], imag[:, lanes:]
        top = rc * rc + rs * rs
        low = ic * ic + is_ * is_
        both = top + low
        cross = 2.0 * (rc * is_ - ic * rs)
        part_ref[z, :half_x] = mult * jnp.where(row_zero, top, 2.0 * both)
        part_ref[z, half_x:] = jnp.concatenate([mult * low[0:1], rest], axis=0)
        plus = jnp.concatenate([jnp.where(row_zero, top, both + cross), low[0:1], rest], axis=0)
        minus = jnp.concatenate([both - cross, low[0:1], rest], axis=0)
        value = 0.0
        for number, power in enumerate((plus, minus)):
            head = power.astype(BF16)
            tail = (power - head.astype(F32)).astype(BF16)
            found = jnp.dot(head, columns, preferred_element_type=F32) + jnp.dot(
                tail, columns, preferred_element_type=F32
            )
            start = at_row + number * hrows
            rows = small_ref[start : start + hrows, :total]
            value = value + jnp.sum(found * rows, axis=0, keepdims=True)
        picks.append(value)
    picks.append(jnp.ones_like(picks[0]))
    picks.append(jnp.zeros((8 - len(picks), picks[0].shape[1]), F32))
    moved = lax.dot_general(
        jnp.concatenate(picks, axis=0) * nudge,
        small_ref[at_step : at_step + total, :NSHELL],
        (((1,), (0,)), ((), ())),
        precision=lax.Precision.HIGHEST, preferred_element_type=F32,
    )

    tiles = NSHELL // 128
    lane = lax.broadcasted_iota(jnp.int32, (8, 128), 1)
    sums = [[jnp.zeros((8, 128), F32) for _ in range(tiles)] for _ in range(depth)]
    for tile in range(lanes // 128):
        block = move[:, tile * 128 : (tile + 1) * 128]
        at_lanes = slice(tile * 128, (tile + 1) * 128)
        for value in np.unique(block):
            if value == UNUSED:
                continue
            value = int(value)
            totals = [None] * depth
            for group in range(hrows // 8):
                if not (block[group * 8 : group * 8 + 8] == value).any():
                    continue
                rows = slice(group * 8, group * 8 + 8)
                line = slice(at_move + group * 8, at_move + group * 8 + 8)
                same = small_ref[line, at_lanes] == F32(value)
                for z in range(depth):
                    term = jnp.where(same, part_ref[z, rows, at_lanes], 0.0)
                    totals[z] = term if totals[z] is None else totals[z] + term
            shift = value % 128
            goal = tile + value // 128
            for z in range(depth):
                total = turn(totals[z], shift, 1)
                if 0 <= goal < tiles:
                    sums[z][goal] += jnp.where(lane >= shift, total, 0.0)
                if shift and 0 <= goal + 1 < tiles:
                    sums[z][goal + 1] += jnp.where(lane < shift, total, 0.0)
    counts = small_ref[at_counts : at_counts + 1, :NSHELL]
    norm = (counts + moved[depth : depth + 1]) * float(full_x * full_y)
    lines = []
    for z in range(depth):
        line = jnp.sum(jnp.concatenate(sums[z], axis=1), axis=0, keepdims=True)
        lines.append((line + moved[z : z + 1]) / norm)
    spec_ref[...] = jnp.concatenate(lines, axis=0)
    copies.append(pltpu.make_async_copy(spec_ref, spec_hbm, sems.at[len(ENDS)]))
    copies[-1].start()
    for copy in copies:
        copy.wait()


def call(kernel, outs, scratch=(), flops=0, moved=0, limit=48 << 20, **specs):
    return pl.pallas_call(
        kernel,
        out_shape=outs,
        scratch_shapes=list(scratch),
        compiler_params=pltpu.CompilerParams(vmem_limit_bytes=limit),
        cost_estimate=pl.CostEstimate(flops=flops, bytes_accessed=moved, transcendentals=0),
        **specs,
    )


def on_device(n_sec, n_row, n_col, labels, jitter, shells):
    depth, wx, wy = labels.shape
    full_x, full_y = wx * n_row, wy * n_sec
    tables = make_tables(full_x, full_y, n_row, n_sec, wx, wy)
    per, section = tables["per"], tables["section"]
    layers = depth + 4
    count = 8 * depth
    shape = jax.ShapeDtypeStruct

    part = lax.broadcasted_iota(jnp.int32, (3, depth, wx, wy), 0)
    none = (0, 0, 0)
    factor = lax.pad(jitter, F32(0.0), ((0, 1, 0), none, none, none))
    whole_numbers = jnp.where(part == 2, shells[None, None], labels[None] ^ part)
    density = jnp.where(whole_numbers == 1, F32(1.0), F32(0.2)) * factor
    own = jnp.where(part == 2, whole_numbers.astype(F32), density)
    row_msg = call(
        functools.partial(pack_kernel, n_row, n_sec, per),
        shape((depth * wx + count + whole(section), wy), BF16),
    )(own)
    col_msg, table_x = call(
        functools.partial(planes_kernel, n_row),
        [shape((2 * depth * wx, wy), BF16), shape((full_x, full_x), BF16)],
    )(own)

    col_got = [lax.ppermute(col_msg, "col", m) for m in ring_moves(n_col)]
    row_got = [lax.ppermute(row_msg, "row", xor_pairs(n_row, k)) for k in range(1, n_row)]
    relay = n_row == 2 and n_col == 4
    diag_got = []
    for a in ring_moves(n_row):
        for b in ring_moves(n_col):
            if relay and b == xor_pairs(n_col, 1):
                diag_got.append(lax.ppermute(row_got[0], "col", b))
            else:
                move = pair_product(a, b, n_col)
                diag_got.append(lax.ppermute(col_msg, ("row", "col"), move))

    at = depth * full_x
    got = {("col", i): value for i, value in enumerate(col_got)}
    got.update({("row", k + 1): value for k, value in enumerate(row_got)})
    got.update({("diag", i): value for i, value in enumerate(diag_got)})
    names = [name for name in FIRST_ROUND if name in got]
    names += [name for name in got if name not in names]
    bulk = call(
        functools.partial(half_kernel, depth, wx, n_row), shape((at + whole(section + TOP), wy), BF16),
        flops=1 << 27, moved=1 << 24
    )(row_msg, *row_got, table_x)
    msg, strip, dens, lanes_own = call(
        functools.partial(middle_kernel, n_row, n_col, section, tuple(names)),
        [
            shape((at + whole(section + TOP), wy), BF16),
            shape((whole(TOP), wy), BF16),
            shape((2 * layers, ROWS, wy), F32),
            shape((ROWS, wy), F32),
        ],
        flops=MID,
        moved=MID,
    )(own, row_msg, *[got[name] for name in names], bulk)

    ring = ring_moves(n_sec)
    early = EARLY.get(n_sec, ())
    sec_got, strip_got = [], []
    for k in swap_order(n_sec):
        move = xor_pairs(n_sec, k)
        with_columns = move in ring and k not in early
        sec_got.append(lax.ppermute(msg if with_columns else bulk, "sec", move))
    for move in ring:
        if move[0][1] in early:
            strip_got.append(lax.ppermute(strip, "sec", move))

    cells = call(
        cells_kernel,
        shape((38, depth, wx, wy), F32),
        flops=LBM,
        moved=LBM,
    )(dens)

    hrows, lanes = full_x // 2 + 8, full_y // 2 + 128
    return call(
        functools.partial(
            final_kernel, n_sec, section, tables["places"], tables["total"], tables["move"]
        ),
        [shape((38, depth, wx, wy), F32), shape((depth, NSHELL), F32)],
        [
            pltpu.VMEM((depth * full_x, full_y), BF16),
            pltpu.VMEM((whole(section), full_y), BF16),
            pltpu.VMEM((depth, hrows, lanes), F32),
            pltpu.VMEM((38, depth, wx, wy), F32),
            pltpu.VMEM((depth, NSHELL), F32),
            pltpu.SemaphoreType.DMA((len(ENDS) + 1,)),
        ],
        out_specs=[pl.BlockSpec(memory_space=pltpu.HBM)] * 2,
    )(bulk, *sec_got, *strip_got, lanes_own, cells, tables["large"], tables["small"])


def solution(mesh):
    in_specs = (P("col", "row", "sec"), P(None, "col", "row", "sec"), P("row", "sec"))
    out_specs = (P(None, "col", "row", "sec"), P("col", None))
    sizes = [mesh.shape[name] for name in ("sec", "row", "col")]
    return jax.shard_map(
        functools.partial(on_device, *sizes),
        mesh=mesh,
        in_specs=in_specs,
        out_specs=out_specs,
        check_vma=False,
    )
```

```python
import functools
import math

import jax
import jax.numpy as jnp
import ml_dtypes
import numpy as np
from jax import lax
from jax.experimental import pallas as pl
from jax.experimental.pallas import tpu as pltpu
from jax.sharding import PartitionSpec as P

NSHELL = 256
UNUSED = -(1 << 20)
MID = 1 << 24
LBM = 1 << 10
ENDS = (10, 19, 29, 38)
FIRST_ROUND = (("col", 0), ("diag", 0), ("row", 1), ("col", 1), ("diag", 1))
SWAPS = {4: (3, 1, 2)}
EARLY = {4: (1, 2)}
TOP = 40
ROWS = 72
F32 = jnp.float32
BF16 = jnp.bfloat16

LATTICE = (
    (0, 0, 0),
    (1, 0, 0),
    (-1, 0, 0),
    (0, 1, 0),
    (0, -1, 0),
    (0, 0, 1),
    (0, 0, -1),
    (1, 1, 0),
    (-1, -1, 0),
    (1, -1, 0),
    (-1, 1, 0),
    (1, 0, 1),
    (-1, 0, -1),
    (1, 0, -1),
    (-1, 0, 1),
    (0, 1, 1),
    (0, -1, -1),
    (0, 1, -1),
    (0, -1, 1),
)
WEIGHTS = (1.0 / 3.0,) + (1.0 / 18.0,) * 6 + (1.0 / 36.0,) * 12


def xor_pairs(count, bits):
    return [(i, i ^ bits) for i in range(count)]


def shift_pairs(count, step):
    return [(i, (i + step) % count) for i in range(count)]


def ring_moves(count):
    if count == 2:
        return [xor_pairs(2, 1)]
    if count == 4:
        return [xor_pairs(4, 1), xor_pairs(4, 3)]
    return [shift_pairs(count, 1), shift_pairs(count, -1)]


def ring_pick(count, index):
    if count == 2:
        return 0, 0
    if count == 4:
        odd = lax.rem(index, 2)
        return 1 - odd, odd
    return 0, 1


def swap_order(count):
    return SWAPS.get(count, tuple(range(1, count)))


def late_swaps(count):
    return tuple(k for k in range(1, count) if k not in EARLY.get(count, ()))


def pair_product(first, second, count_second):
    return [
        (a * count_second + b, c * count_second + d) for a, c in first for b, d in second
    ]


def whole(rows):
    return 16 * (-(-rows // 16))


def choose(items, which):
    if isinstance(which, int):
        return items[which]
    value = items[0]
    for number in range(1, len(items)):
        value = jnp.where(which == number, items[number], value)
    return value


def bf16_table(values):
    return np.asarray(values, np.float32).astype(ml_dtypes.bfloat16)


def angle_table(freq, pos, full):
    step = np.float32(2.0 * math.pi / full)
    return ((freq * pos) % full).astype(np.float32) * step


@functools.lru_cache(maxsize=None)
def make_tables(full_x, full_y, n_row, n_sec, wx, wy):
    half_x, half_y = full_x // 2, full_y // 2
    lanes = half_y + 128
    freq_y = np.arange(lanes)[None, :]
    angles = angle_table(np.arange(full_y)[:, None], freq_y, full_y)
    live = freq_y <= half_y
    table_y = np.concatenate([np.cos(angles) * live, np.sin(angles) * live], 1)
    hrows = half_x + 8
    radius = np.arange(hrows)[:, None] ** 2 + np.arange(lanes)[None, :] ** 2
    base = np.minimum(np.floor(np.sqrt(radius.astype(np.float64))).astype(np.int64), NSHELL - 1)
    valid = (np.arange(hrows)[:, None] <= half_x) & (np.arange(lanes)[None, :] <= half_y)
    move = np.where(valid, base - np.arange(lanes)[None, :], UNUSED)
    mult_y = np.where(freq_y > half_y, 0, np.where((freq_y == 0) | (freq_y == half_y), 1, 2))
    signed_x = np.arange(full_x)
    signed_x = np.where(signed_x < half_x, signed_x, signed_x - full_x)
    signed_y = np.arange(full_y)
    signed_y = np.where(signed_y < half_y, signed_y, signed_y - full_y)
    square = signed_x[:, None] ** 2 + signed_y[None, :] ** 2
    root = np.floor(np.sqrt(square + 1.0) + 1e-9).astype(np.int64)
    special = (root * root == square + 1) & (root < NSHELL) & (square > 0)
    low_label = np.minimum(np.floor(np.sqrt(square.astype(np.float64))), NSHELL - 1)
    counts = np.bincount(low_label.astype(np.int64).ravel(), minlength=NSHELL)
    rank = np.zeros(special.shape, np.int64)
    for r in range(n_row):
        rows = special[r * wx : (r + 1) * wx]
        rank[r * wx : (r + 1) * wx] = np.cumsum(rows, axis=0) - rows
    per = int(rank[special].max()) + 1
    section = 8 * (-(-(n_row * per) // 8))
    total = 128 * (-(-int(special.sum()) // 128))
    put = np.zeros((n_row * per, total))
    lanes_of = np.zeros((total, full_y))
    mark_row = np.zeros((2, hrows, total))
    mark_col = np.zeros((lanes, total))
    step = np.zeros((total, NSHELL))
    for entry, (kx, ky) in enumerate(np.argwhere(special).tolist()):
        ax, ay = abs(int(signed_x[kx])), abs(int(signed_y[ky]))
        same = int(signed_x[kx]) * int(signed_y[ky]) >= 0 or ax == half_x or ay == half_y
        put[kx // wx * per + rank[kx, ky], entry] = 1
        lanes_of[entry, ky] = 1
        mark_row[0 if same else 1, ax, entry] = 1
        mark_col[ay, entry] = 1
        step[entry, root[kx, ky]] += 1
        step[entry, root[kx, ky] - 1] -= 1
    parts = (mult_y, counts[None, :], put, mark_row.reshape(2 * hrows, total), step, move)
    wide = max(p.shape[1] for p in parts)
    small, places = [], []
    for part in parts:
        rows = 8 * (-(-part.shape[0] // 8))
        places.append(sum(p.shape[0] for p in small))
        filled = np.zeros((rows, wide), np.float32)
        filled[: part.shape[0], : part.shape[1]] = part
        small.append(filled)
    columns = np.zeros((full_y, total))
    columns[:lanes] = mark_col
    return dict(
        per=per,
        section=section,
        total=total,
        move=move,
        places=tuple(places),
        small=np.concatenate(small, axis=0),
        large=np.concatenate([table_y, lanes_of.T, columns], axis=1).astype(ml_dtypes.bfloat16),
    )


def turn_table(steps, full):
    quarter = (4 * steps + full // 2) // full
    rest = (steps - quarter * (full // 4)).astype(F32) * F32(2.0 * math.pi / full)
    square = rest * rest
    cos, sin = F32(1.0), F32(1.0)
    for order in (8, 6, 4, 2):
        cos = 1.0 - square * cos * F32(1.0 / (order * (order - 1)))
        sin = 1.0 - square * sin * F32(1.0 / (order * (order + 1)))
    sin = sin * rest
    odd = quarter % 2 == 1
    cos, sin = jnp.where(odd, sin, cos), jnp.where(odd, cos, sin)
    cos = jnp.where((quarter == 1) | (quarter == 2), -cos, cos)
    return cos, jnp.where((quarter == 2) | (quarter == 3), -sin, sin)


def x_table(row, n_row, wx):
    full_x = n_row * wx
    half_x = full_x // 2
    freq = lax.broadcasted_iota(jnp.int32, (full_x, full_x), 0)
    lane = lax.broadcasted_iota(jnp.int32, (full_x, full_x), 1)
    pos = (lane // wx ^ row) * wx + lane % wx
    is_cos = freq <= half_x
    cos, sin = turn_table(jnp.where(is_cos, freq, freq - half_x) * pos % full_x, full_x)
    return jnp.where(is_cos, cos, -sin).astype(BF16)


def planes_kernel(n_row, own_ref, col_ref, table_ref):
    _, depth, wx, _ = own_ref.shape
    for c in range(2):
        for z in range(depth):
            at = (c * depth + z) * wx
            col_ref[at : at + wx] = own_ref[c, z].astype(BF16)
    table_ref[...] = x_table(lax.axis_index("row"), n_row, wx)


def pack_kernel(n_row, n_sec, per, own_ref, row_ref):
    _, depth, wx, wy = own_ref.shape
    edges = []
    densities = [[own_ref[c, z] for z in range(depth)] for c in range(2)]
    for c in range(2):
        for z in range(depth):
            tile = densities[c][z]
            edges += [tile[0:2], tile[wx - 2 : wx]]
    for z in range(depth):
        row_ref[z * wx : (z + 1) * wx] = (densities[0][z] - densities[1][z]).astype(BF16)
    edge = jnp.concatenate(edges, axis=0).astype(BF16)
    at = depth * wx
    count = edge.shape[0]
    row_ref[at : at + count] = edge

    row, sec = lax.axis_index("row"), lax.axis_index("sec")
    square, root = shell_root(row * wx, sec * wy, wx * n_row, wy * n_sec, wx, wy)
    special = (root * root == square + 1.0) & (root < NSHELL) & (square > 0.0)
    nudge = jnp.where(special, own_ref[2, 0] - (root - 1.0), 0.0)
    one = jnp.where(special, F32(1.0), F32(0.0)).astype(BF16)
    down = lax.broadcasted_iota(jnp.int32, (wx, wx), 0)
    above = (lax.broadcasted_iota(jnp.int32, (wx, wx), 1) < down).astype(F32).astype(BF16)
    rank = jnp.dot(above, one, preferred_element_type=F32)
    section = row_ref.shape[0] - at - count
    line = lax.broadcasted_iota(jnp.int32, (section, wy), 0)
    marks = jnp.zeros((section, wy), F32)
    for number in range(per):
        found = jnp.sum(jnp.where(rank == number, nudge, 0.0), axis=0, keepdims=True)
        marks = jnp.where(line == row * per + number, found, marks)
    row_ref[at + count :] = marks.astype(BF16)


def shell_root(first_x, first_y, full_x, full_y, wx, wy):
    kx = first_x + lax.broadcasted_iota(jnp.int32, (wx, wy), 0)
    ky = first_y + lax.broadcasted_iota(jnp.int32, (wx, wy), 1)
    kx = jnp.where(kx < full_x // 2, kx, kx - full_x)
    ky = jnp.where(ky < full_y // 2, ky, ky - full_y)
    square = (kx * kx + ky * ky).astype(F32)
    return square, jnp.floor(jnp.sqrt(square + 1.0) + 0.5)


def half_kernel(depth, wx, n_row, *refs):
    row_refs, table_ref, bulk_ref = refs[:n_row], refs[n_row], refs[n_row + 1]
    full_x = table_ref.shape[0]
    for z in range(depth):
        lines = jnp.concatenate([r[z * wx : (z + 1) * wx] for r in row_refs], axis=0)
        half = jnp.dot(table_ref[...], lines, preferred_element_type=F32)
        bulk_ref[z * full_x : (z + 1) * full_x] = half.astype(BF16)
    at = depth * wx + 8 * depth
    marks = sum(ref[at:].astype(F32) for ref in row_refs)
    bulk_ref[depth * full_x : depth * full_x + marks.shape[0]] = marks.astype(BF16)
    rest = depth * full_x + marks.shape[0]
    if rest < bulk_ref.shape[0]:
        bulk_ref[rest:] = jnp.zeros((bulk_ref.shape[0] - rest, bulk_ref.shape[1]), BF16)


def edges_of(col_ref, wx):
    lines = []
    for start in range(0, col_ref.shape[0], wx):
        lines.append(col_ref[start : start + 16].astype(F32)[:2])
        lines.append(col_ref[start + wx - 16 : start + wx].astype(F32)[14:])
    return jnp.concatenate(lines, axis=0)


def middle_kernel(n_row, n_col, section, names, own_ref, row_ref, *refs):
    _, depth, wx, wy = own_ref.shape
    col_moves, row_moves = len(ring_moves(n_col)), len(ring_moves(n_row))
    by_name, refs = dict(zip(names, refs)), refs[len(names) :]
    bulk_ref, msg_ref, strip_ref, dens_ref, lanes_ref = refs
    col_refs = [by_name["col", i] for i in range(col_moves)]
    row_refs = [row_ref] + [by_name["row", k] for k in range(1, n_row)]
    diag_refs = [by_name["diag", i] for i in range(col_moves * row_moves)]
    row, col = lax.axis_index("row"), lax.axis_index("col")
    at = depth * wx
    count = 8 * depth
    col_prev, col_next = ring_pick(n_col, col)
    before = choose([r[...].astype(F32) for r in col_refs], col_prev)
    after = choose([r[...].astype(F32) for r in col_refs], col_next)
    edge_list = [r[at : at + count].astype(F32) for r in row_refs]
    edge_prev = choose(edge_list, row ^ lax.rem(row + n_row - 1, n_row)) if n_row > 2 else edge_list[1]
    edge_next = choose(edge_list, row ^ lax.rem(row + 1, n_row)) if n_row > 2 else edge_list[1]
    row_prev, row_next = ring_pick(n_row, row)
    diag = [
        r[at : at + count].astype(F32) if r.shape == row_ref.shape else edges_of(r, wx)
        for r in diag_refs
    ]

    def diag_of(row_which, col_which):
        lines = [
            choose(diag[m * col_moves : (m + 1) * col_moves], col_which) for m in range(row_moves)
        ]
        return choose(lines, row_which)

    corner = {
        (0, -1): diag_of(row_prev, col_prev),
        (0, 1): diag_of(row_prev, col_next),
        (1, -1): diag_of(row_next, col_prev),
        (1, 1): diag_of(row_next, col_next),
    }
    lane = lax.broadcasted_iota(jnp.int32, (ROWS, wy), 1)
    gap = jnp.zeros((ROWS - wx - 4, wy), F32)
    strips = jnp.zeros((ROWS, wy), F32)
    layers = depth + 4
    for c in range(2):
        for layer in range(layers):
            z = layer - 2
            if z < 0:
                source, plane, low, high = before, depth + z, corner[0, -1], corner[1, -1]
            elif z >= depth:
                source, plane, low, high = after, z - depth, corner[0, 1], corner[1, 1]
            else:
                source, plane, low, high = None, z, edge_prev, edge_next
            where = c * depth + plane
            if source is None:
                body = own_ref[c, plane]
            else:
                body = source[where * wx : (where + 1) * wx]
            tail = jnp.concatenate(
                [high[where * 4 : where * 4 + 2], gap, low[where * 4 + 2 : where * 4 + 4]], axis=0
            )
            tile = jnp.concatenate([body, tail], axis=0)
            group = c * layers + layer
            dens_ref[group] = tile
            at_lane = 8 * group
            moved = pltpu.roll(tile, (at_lane + 2) % wy, 1)
            strips = jnp.where((lane >= at_lane) & (lane < at_lane + 4), moved, strips)
    lanes_ref[...] = strips + pltpu.roll(strips, 4, 1)
    lower = jnp.concatenate([strips[TOP:], jnp.zeros((2 * TOP - ROWS, wy), F32)], axis=0)
    folded = strips[:TOP] + pltpu.roll(lower, 4, 1)
    gap = jnp.zeros((strip_ref.shape[0] - TOP, wy), F32)
    strip_ref[...] = jnp.concatenate([folded, gap], axis=0).astype(BF16)
    at = msg_ref.shape[0] - whole(section + TOP)
    msg_ref[:at] = bulk_ref[:at]
    parts = [bulk_ref[at : at + whole(section)].astype(F32)[:section], folded]
    missing = msg_ref.shape[0] - at - section - TOP
    if missing:
        parts.append(jnp.zeros((missing, wy), F32))
    msg_ref[at:] = jnp.concatenate(parts, axis=0).astype(BF16)


def turn(tile, shift, axis):
    shift = shift % tile.shape[axis]
    return tile if shift == 0 else pltpu.roll(tile, shift, axis)


def pull_of(below, here, above):
    around = below + above
    line_y = turn(here, -1, 1) + turn(here, 1, 1)
    line_x = turn(here, -1, 0) + turn(here, 1, 0)
    flat = 2.0 * here + around
    mix = flat + line_y
    pull_x = turn(mix, -1, 0) - turn(mix, 1, 0)
    mix = flat + line_x
    pull_y = turn(mix, -1, 1) - turn(mix, 1, 1)
    gap = above - below
    pull_z = 2.0 * gap + turn(gap, -1, 0) + turn(gap, 1, 0) + turn(gap, -1, 1) + turn(gap, 1, 1)
    return pull_x, pull_y, pull_z


def relax_terms(density, velocity):
    vx, vy, vz = velocity
    squared = vx * vx + vy * vy + vz * vz
    rest = density * (1.0 - 1.875 * squared)
    terms = [WEIGHTS[0] * rest]
    for number in range(1, 19, 2):
        offsets = LATTICE[number]
        projected = None
        for axis in range(3):
            if offsets[axis]:
                part = velocity[axis] if offsets[axis] > 0 else -velocity[axis]
                projected = part if projected is None else projected + part
        weighted = density * projected
        even = WEIGHTS[number] * (rest + 5.625 * (weighted * projected))
        odd = (WEIGHTS[number] * 3.75) * weighted
        terms += [even + odd, even - odd]
    return terms


def cells_kernel(dens_ref, out_ref):
    _, depth, wx, _ = out_ref.shape
    layers = depth + 4
    scale = -1.6 / 36.0
    for layer in range(1, layers - 1):
        for c in range(2):
            other = (1 - c) * layers + layer
            pulls = pull_of(dens_ref[other - 1], dens_ref[other], dens_ref[other + 1])
            velocity = [scale * p for p in pulls]
            terms = relax_terms(dens_ref[c * layers + layer], velocity)
            for number in range(19):
                cx, cy, cz = LATTICE[number]
                z = layer - 2 + cz
                if 0 <= z < depth:
                    tile = turn(turn(terms[number], cx, 0), cy, 1)
                    out_ref[c * 19 + number, z] = tile[:wx]


def set_ends(n_sec, start, at, msg_refs, lanes_ref, cells_ref, out_hbm, out_ref, sems):
    _, depth, wx, wy = out_ref.shape
    layers = depth + 4
    strips = [
        r[:].astype(F32)[:TOP] if r.shape[0] < start else r[start:].astype(F32)[at - start :][:TOP]
        for r in msg_refs
    ]
    index = lax.axis_index("sec")
    prev_which, next_which = ring_pick(n_sec, index)
    before, after = choose(strips, prev_which), choose(strips, next_which)
    rest = ROWS - TOP
    before = jnp.concatenate([before, turn(before, -4, 1)[:rest]], axis=0)
    after = jnp.concatenate([turn(after, 4, 1), after[:rest]], axis=0)
    place = lax.rem(lax.broadcasted_iota(jnp.int32, (ROWS, wy), 1), 8)
    tile = jnp.where(place < 2, before, jnp.where(place >= 6, after, lanes_ref[...]))
    pulls = pull_of(turn(tile, 8, 1), tile, turn(tile, -8, 1))
    span = 8 * layers
    first = lax.broadcasted_iota(jnp.int32, (ROWS, wy), 1) < span
    scale = -1.6 / 36.0
    velocity = [scale * jnp.where(first, turn(p, -span, 1), turn(p, span, 1)) for p in pulls]
    terms = relax_terms(tile, velocity)
    lane = lax.broadcasted_iota(jnp.int32, (wx, wy), 1)
    copies = []
    moved = []
    for number in range(19):
        cx, cy, cz = LATTICE[number]
        term = turn(terms[number], cx, 0)[:wx]
        if cy == 0:
            term = jnp.where(place[:wx] == 1, turn(term, -4, 1), term)
        moved.append(term)
    masks = {1: lane < 2, -1: lane >= wy - 2, 0: (lane == 0) | (lane == wy - 1)}
    begin = 0
    for q in range(38):
        c, number = divmod(q, 19)
        _, cy, cz = LATTICE[number]
        for z in range(depth):
            group = 8 * (c * layers + 2 + z - cz)
            back = {1: group + 1, -1: group + 5 - (wy - 2), 0: group + 2}[cy]
            out_ref[q, z] = jnp.where(masks[cy], turn(moved[number], -back, 1), cells_ref[q, z])
        if q + 1 in ENDS:
            span = pl.ds(begin, q + 1 - begin)
            copy = pltpu.make_async_copy(
                out_ref.at[span], out_hbm.at[span], sems.at[len(copies)]
            )
            copy.start()
            copies.append(copy)
            begin = q + 1
    return copies


def early_kernel(n_sec, lanes, taken, *refs):
    msg_refs, (large_ref, out_ref) = refs[:-2], refs[-2:]
    wy = large_ref.shape[0] // n_sec
    sec = lax.axis_index("sec")
    total = None
    for k, ref in zip(taken, msg_refs):
        start = pl.multiple_of((sec ^ k) * wy, wy)
        part = jnp.dot(
            ref[: out_ref.shape[0]],
            large_ref[pl.ds(start, wy), : 2 * lanes],
            preferred_element_type=F32,
        )
        total = part if total is None else total + part
    out_ref[...] = total


def final_kernel(n_sec, section, places, total, move, msg_own_ref, *refs):
    msg_refs = [msg_own_ref] + [refs[swap_order(n_sec).index(k)] for k in range(1, n_sec)]
    refs = refs[n_sec - 1 :]
    ring = []
    for move_ in ring_moves(n_sec):
        k = move_[0][1]
        if k in EARLY.get(n_sec, ()):
            ring.append(refs[0])
            refs = refs[1:]
        else:
            ring.append(msg_refs[k])
    (strips_ref, cells_ref), refs = refs[:2], refs[2:]
    (early_ref, large_ref, small_ref,
     out_hbm, spec_hbm, mark_ref, part_ref, out_ref, spec_ref, sems) = refs
    depth = spec_ref.shape[0]
    sec = lax.axis_index("sec")
    full_y, lanes = large_ref.shape[0], move.shape[1]
    wy = full_y // n_sec
    full_x = early_ref.shape[0] // depth
    half_x = full_x // 2
    hrows = half_x + 8
    at = depth * full_x
    at_mult, at_counts, at_put, at_row, at_step, at_move = places
    copies = set_ends(n_sec, at, at + section, ring, strips_ref, cells_ref, out_hbm, out_ref, sems)

    for k in range(n_sec):
        start = pl.multiple_of((sec ^ k) * wy, wy)
        mark_ref[:, pl.ds(start, wy)] = msg_refs[k][at : at + mark_ref.shape[0]]
    transform = early_ref[...]
    for k in late_swaps(n_sec):
        start = pl.multiple_of((sec ^ k) * wy, wy)
        transform = transform + jnp.dot(
            msg_refs[k][:at],
            large_ref[pl.ds(start, wy), : 2 * lanes],
            preferred_element_type=F32,
        )

    find = large_ref[:, 2 * lanes : 2 * lanes + total]
    found = jnp.dot(mark_ref[...], find, preferred_element_type=F32)[:section]
    nudge = jnp.sum(found * small_ref[at_put:at_row, :total], axis=0, keepdims=True)

    mult = small_ref[at_mult : at_mult + 1, :lanes]
    columns = large_ref[:lanes, 2 * lanes + total :]
    row_zero = lax.broadcasted_iota(jnp.int32, (half_x, lanes), 0) == 0
    rest = jnp.zeros((7, lanes), F32)
    picks = []
    for z in range(depth):
        real = transform[z * full_x : z * full_x + half_x]
        imag = transform[z * full_x + half_x : (z + 1) * full_x]
        rc, rs = real[:, :lanes], real[:, lanes:]
        ic, is_ = imag[:, :lanes], imag[:, lanes:]
        top = rc * rc + rs * rs
        low = ic * ic + is_ * is_
        both = top + low
        cross = 2.0 * (rc * is_ - ic * rs)
        part_ref[z, :half_x] = mult * jnp.where(row_zero, top, 2.0 * both)
        part_ref[z, half_x:] = jnp.concatenate([mult * low[0:1], rest], axis=0)
        plus = jnp.concatenate([jnp.where(row_zero, top, both + cross), low[0:1], rest], axis=0)
        minus = jnp.concatenate([both - cross, low[0:1], rest], axis=0)
        value = 0.0
        for number, power in enumerate((plus, minus)):
            head = power.astype(BF16)
            tail = (power - head.astype(F32)).astype(BF16)
            found = jnp.dot(head, columns, preferred_element_type=F32) + jnp.dot(
                tail, columns, preferred_element_type=F32
            )
            start = at_row + number * hrows
            rows = small_ref[start : start + hrows, :total]
            value = value + jnp.sum(found * rows, axis=0, keepdims=True)
        picks.append(value)
    picks.append(jnp.ones_like(picks[0]))
    picks.append(jnp.zeros((8 - len(picks), picks[0].shape[1]), F32))
    moved = lax.dot_general(
        jnp.concatenate(picks, axis=0) * nudge,
        small_ref[at_step : at_step + total, :NSHELL],
        (((1,), (0,)), ((), ())),
        precision=lax.Precision.HIGHEST, preferred_element_type=F32,
    )

    tiles = NSHELL // 128
    lane = lax.broadcasted_iota(jnp.int32, (8, 128), 1)
    sums = [[jnp.zeros((8, 128), F32) for _ in range(tiles)] for _ in range(depth)]
    for tile in range(lanes // 128):
        block = move[:, tile * 128 : (tile + 1) * 128]
        at_lanes = slice(tile * 128, (tile + 1) * 128)
        for value in np.unique(block):
            if value == UNUSED:
                continue
            value = int(value)
            totals = [None] * depth
            for group in range(hrows // 8):
                if not (block[group * 8 : group * 8 + 8] == value).any():
                    continue
                rows = slice(group * 8, group * 8 + 8)
                line = slice(at_move + group * 8, at_move + group * 8 + 8)
                same = small_ref[line, at_lanes] == F32(value)
                for z in range(depth):
                    term = jnp.where(same, part_ref[z, rows, at_lanes], 0.0)
                    totals[z] = term if totals[z] is None else totals[z] + term
            shift = value % 128
            goal = tile + value // 128
            for z in range(depth):
                total = turn(totals[z], shift, 1)
                if 0 <= goal < tiles:
                    sums[z][goal] += jnp.where(lane >= shift, total, 0.0)
                if shift and 0 <= goal + 1 < tiles:
                    sums[z][goal + 1] += jnp.where(lane < shift, total, 0.0)
    counts = small_ref[at_counts : at_counts + 1, :NSHELL]
    norm = (counts + moved[depth : depth + 1]) * float(full_x * full_y)
    lines = []
    for z in range(depth):
        line = jnp.sum(jnp.concatenate(sums[z], axis=1), axis=0, keepdims=True)
        lines.append((line + moved[z : z + 1]) / norm)
    spec_ref[...] = jnp.concatenate(lines, axis=0)
    copies.append(pltpu.make_async_copy(spec_ref, spec_hbm, sems.at[len(ENDS)]))
    copies[-1].start()
    for copy in copies:
        copy.wait()


def call(kernel, outs, scratch=(), flops=0, moved=0, limit=48 << 20, **specs):
    return pl.pallas_call(
        kernel,
        out_shape=outs,
        scratch_shapes=list(scratch),
        compiler_params=pltpu.CompilerParams(vmem_limit_bytes=limit),
        cost_estimate=pl.CostEstimate(flops=flops, bytes_accessed=moved, transcendentals=0),
        **specs,
    )


def on_device(n_sec, n_row, n_col, labels, jitter, shells):
    depth, wx, wy = labels.shape
    full_x, full_y = wx * n_row, wy * n_sec
    tables = make_tables(full_x, full_y, n_row, n_sec, wx, wy)
    per, section = tables["per"], tables["section"]
    layers = depth + 4
    count = 8 * depth
    shape = jax.ShapeDtypeStruct

    part = lax.broadcasted_iota(jnp.int32, (3, depth, wx, wy), 0)
    none = (0, 0, 0)
    factor = lax.pad(jitter, F32(0.0), ((0, 1, 0), none, none, none))
    whole_numbers = jnp.where(part == 2, shells[None, None], labels[None] ^ part)
    density = jnp.where(whole_numbers == 1, F32(1.0), F32(0.2)) * factor
    own = jnp.where(part == 2, whole_numbers.astype(F32), density)
    row_msg = call(
        functools.partial(pack_kernel, n_row, n_sec, per),
        shape((depth * wx + count + whole(section), wy), BF16),
    )(own)
    col_msg, table_x = call(
        functools.partial(planes_kernel, n_row),
        [shape((2 * depth * wx, wy), BF16), shape((full_x, full_x), BF16)],
    )(own)

    col_got = [lax.ppermute(col_msg, "col", m) for m in ring_moves(n_col)]
    row_got = [lax.ppermute(row_msg, "row", xor_pairs(n_row, k)) for k in range(1, n_row)]
    relay = n_row == 2 and n_col == 4
    diag_got = []
    for a in ring_moves(n_row):
        for b in ring_moves(n_col):
            if relay and b == xor_pairs(n_col, 1):
                diag_got.append(lax.ppermute(row_got[0], "col", b))
            else:
                move = pair_product(a, b, n_col)
                diag_got.append(lax.ppermute(col_msg, ("row", "col"), move))

    at = depth * full_x
    got = {("col", i): value for i, value in enumerate(col_got)}
    got.update({("row", k + 1): value for k, value in enumerate(row_got)})
    got.update({("diag", i): value for i, value in enumerate(diag_got)})
    names = [name for name in FIRST_ROUND if name in got]
    names += [name for name in got if name not in names]
    bulk = call(
        functools.partial(half_kernel, depth, wx, n_row), shape((at + whole(section + TOP), wy), BF16),
        flops=1 << 27, moved=1 << 24
    )(row_msg, *row_got, table_x)
    msg, strip, dens, lanes_own = call(
        functools.partial(middle_kernel, n_row, n_col, section, tuple(names)),
        [
            shape((at + whole(section + TOP), wy), BF16),
            shape((whole(TOP), wy), BF16),
            shape((2 * layers, ROWS, wy), F32),
            shape((ROWS, wy), F32),
        ],
        flops=MID,
        moved=MID,
    )(own, row_msg, *[got[name] for name in names], bulk)

    ring = ring_moves(n_sec)
    early = EARLY.get(n_sec, ())
    sec_got, strip_got = [], []
    for k in swap_order(n_sec):
        move = xor_pairs(n_sec, k)
        with_columns = move in ring and k not in early
        sec_got.append(lax.ppermute(msg if with_columns else bulk, "sec", move))
    for move in ring:
        if move[0][1] in early:
            strip_got.append(lax.ppermute(strip, "sec", move))

    cells = call(
        cells_kernel,
        shape((38, depth, wx, wy), F32),
        flops=LBM,
        moved=LBM,
    )(dens)

    hrows, lanes = full_x // 2 + 8, full_y // 2 + 128
    taken = (0,) + EARLY.get(n_sec, ())
    blocks = [bulk if k == 0 else sec_got[swap_order(n_sec).index(k)] for k in taken]
    early_part = call(
        functools.partial(early_kernel, n_sec, lanes, taken),
        shape((depth * full_x, 2 * lanes), F32),
    )(*blocks, tables["large"])
    return call(
        functools.partial(
            final_kernel, n_sec, section, tables["places"], tables["total"], tables["move"]
        ),
        [shape((38, depth, wx, wy), F32), shape((depth, NSHELL), F32)],
        [
            pltpu.VMEM((whole(section), full_y), BF16),
            pltpu.VMEM((depth, hrows, lanes), F32),
            pltpu.VMEM((38, depth, wx, wy), F32),
            pltpu.VMEM((depth, NSHELL), F32),
            pltpu.SemaphoreType.DMA((len(ENDS) + 1,)),
        ],
        out_specs=[pl.BlockSpec(memory_space=pltpu.HBM)] * 2,
    )(bulk, *sec_got, *strip_got, lanes_own, cells, early_part, tables["large"], tables["small"])


def solution(mesh):
    in_specs = (P("col", "row", "sec"), P(None, "col", "row", "sec"), P("row", "sec"))
    out_specs = (P(None, "col", "row", "sec"), P("col", None))
    sizes = [mesh.shape[name] for name in ("sec", "row", "col")]
    return jax.shard_map(
        functools.partial(on_device, *sizes),
        mesh=mesh,
        in_specs=in_specs,
        out_specs=out_specs,
        check_vma=False,
    )
```

```python
import functools
import math

import jax
import jax.numpy as jnp
import ml_dtypes
import numpy as np
from jax import lax
from jax.experimental import pallas as pl
from jax.experimental.pallas import tpu as pltpu
from jax.sharding import PartitionSpec as P

NSHELL = 256
UNUSED = -(1 << 20)
MID = 1 << 24
LBM = 1 << 10
ENDS = (10, 19, 29, 38)
FIRST_ROUND = (("col", 0), ("diag", 0), ("row", 1), ("col", 1), ("diag", 1))
SWAPS = {4: (3, 1, 2)}
EARLY = {4: (1, 2)}
TOP = 40
ROWS = 72
F32 = jnp.float32
BF16 = jnp.bfloat16

LATTICE = (
    (0, 0, 0),
    (1, 0, 0),
    (-1, 0, 0),
    (0, 1, 0),
    (0, -1, 0),
    (0, 0, 1),
    (0, 0, -1),
    (1, 1, 0),
    (-1, -1, 0),
    (1, -1, 0),
    (-1, 1, 0),
    (1, 0, 1),
    (-1, 0, -1),
    (1, 0, -1),
    (-1, 0, 1),
    (0, 1, 1),
    (0, -1, -1),
    (0, 1, -1),
    (0, -1, 1),
)
WEIGHTS = (1.0 / 3.0,) + (1.0 / 18.0,) * 6 + (1.0 / 36.0,) * 12


def xor_pairs(count, bits):
    return [(i, i ^ bits) for i in range(count)]


def shift_pairs(count, step):
    return [(i, (i + step) % count) for i in range(count)]


def ring_moves(count):
    if count == 2:
        return [xor_pairs(2, 1)]
    if count == 4:
        return [xor_pairs(4, 1), xor_pairs(4, 3)]
    return [shift_pairs(count, 1), shift_pairs(count, -1)]


def ring_pick(count, index):
    if count == 2:
        return 0, 0
    if count == 4:
        odd = lax.rem(index, 2)
        return 1 - odd, odd
    return 0, 1


def swap_order(count):
    return SWAPS.get(count, tuple(range(1, count)))


def late_swaps(count):
    return tuple(k for k in range(1, count) if k not in EARLY.get(count, ()))


def pair_product(first, second, count_second):
    return [
        (a * count_second + b, c * count_second + d) for a, c in first for b, d in second
    ]


def whole(rows):
    return 16 * (-(-rows // 16))


def choose(items, which):
    if isinstance(which, int):
        return items[which]
    value = items[0]
    for number in range(1, len(items)):
        value = jnp.where(which == number, items[number], value)
    return value


def bf16_table(values):
    return np.asarray(values, np.float32).astype(ml_dtypes.bfloat16)


def angle_table(freq, pos, full):
    step = np.float32(2.0 * math.pi / full)
    return ((freq * pos) % full).astype(np.float32) * step


@functools.lru_cache(maxsize=None)
def make_tables(full_x, full_y, n_row, n_sec, wx, wy):
    half_x, half_y = full_x // 2, full_y // 2
    lanes = half_y + 128
    freq_y = np.arange(lanes)[None, :]
    angles = angle_table(np.arange(full_y)[:, None], freq_y, full_y)
    live = freq_y <= half_y
    table_y = np.concatenate([np.cos(angles) * live, np.sin(angles) * live], 1)
    hrows = half_x + 8
    radius = np.arange(hrows)[:, None] ** 2 + np.arange(lanes)[None, :] ** 2
    base = np.minimum(np.floor(np.sqrt(radius.astype(np.float64))).astype(np.int64), NSHELL - 1)
    valid = (np.arange(hrows)[:, None] <= half_x) & (np.arange(lanes)[None, :] <= half_y)
    move = np.where(valid, base - np.arange(lanes)[None, :], UNUSED)
    mult_y = np.where(freq_y > half_y, 0, np.where((freq_y == 0) | (freq_y == half_y), 1, 2))
    signed_x = np.arange(full_x)
    signed_x = np.where(signed_x < half_x, signed_x, signed_x - full_x)
    signed_y = np.arange(full_y)
    signed_y = np.where(signed_y < half_y, signed_y, signed_y - full_y)
    square = signed_x[:, None] ** 2 + signed_y[None, :] ** 2
    root = np.floor(np.sqrt(square + 1.0) + 1e-9).astype(np.int64)
    special = (root * root == square + 1) & (root < NSHELL) & (square > 0)
    low_label = np.minimum(np.floor(np.sqrt(square.astype(np.float64))), NSHELL - 1)
    counts = np.bincount(low_label.astype(np.int64).ravel(), minlength=NSHELL)
    rank = np.zeros(special.shape, np.int64)
    for r in range(n_row):
        rows = special[r * wx : (r + 1) * wx]
        rank[r * wx : (r + 1) * wx] = np.cumsum(rows, axis=0) - rows
    per = int(rank[special].max()) + 1
    section = 8 * (-(-(n_row * per) // 8))
    total = 128 * (-(-int(special.sum()) // 128))
    put = np.zeros((n_row * per, total))
    lanes_of = np.zeros((total, full_y))
    mark_row = np.zeros((2, hrows, total))
    mark_col = np.zeros((lanes, total))
    step = np.zeros((total, NSHELL))
    for entry, (kx, ky) in enumerate(np.argwhere(special).tolist()):
        ax, ay = abs(int(signed_x[kx])), abs(int(signed_y[ky]))
        same = int(signed_x[kx]) * int(signed_y[ky]) >= 0 or ax == half_x or ay == half_y
        put[kx // wx * per + rank[kx, ky], entry] = 1
        lanes_of[entry, ky] = 1
        mark_row[0 if same else 1, ax, entry] = 1
        mark_col[ay, entry] = 1
        step[entry, root[kx, ky]] += 1
        step[entry, root[kx, ky] - 1] -= 1
    parts = (mult_y, counts[None, :], put, mark_row.reshape(2 * hrows, total), step, move)
    wide = max(p.shape[1] for p in parts)
    small, places = [], []
    for part in parts:
        rows = 8 * (-(-part.shape[0] // 8))
        places.append(sum(p.shape[0] for p in small))
        filled = np.zeros((rows, wide), np.float32)
        filled[: part.shape[0], : part.shape[1]] = part
        small.append(filled)
    columns = np.zeros((full_y, total))
    columns[:lanes] = mark_col
    return dict(
        per=per,
        section=section,
        total=total,
        move=move,
        places=tuple(places),
        small=np.concatenate(small, axis=0),
        large=np.concatenate([table_y, lanes_of.T, columns], axis=1).astype(ml_dtypes.bfloat16),
    )


def turn_table(steps, full):
    quarter = (4 * steps + full // 2) // full
    rest = (steps - quarter * (full // 4)).astype(F32) * F32(2.0 * math.pi / full)
    square = rest * rest
    cos, sin = F32(1.0), F32(1.0)
    for order in (8, 6, 4, 2):
        cos = 1.0 - square * cos * F32(1.0 / (order * (order - 1)))
        sin = 1.0 - square * sin * F32(1.0 / (order * (order + 1)))
    sin = sin * rest
    odd = quarter % 2 == 1
    cos, sin = jnp.where(odd, sin, cos), jnp.where(odd, cos, sin)
    cos = jnp.where((quarter == 1) | (quarter == 2), -cos, cos)
    return cos, jnp.where((quarter == 2) | (quarter == 3), -sin, sin)


def x_table(row, n_row, wx):
    full_x = n_row * wx
    half_x = full_x // 2
    freq = lax.broadcasted_iota(jnp.int32, (full_x, full_x), 0)
    lane = lax.broadcasted_iota(jnp.int32, (full_x, full_x), 1)
    pos = (lane // wx ^ row) * wx + lane % wx
    is_cos = freq <= half_x
    cos, sin = turn_table(jnp.where(is_cos, freq, freq - half_x) * pos % full_x, full_x)
    return jnp.where(is_cos, cos, -sin).astype(BF16)


def planes_kernel(n_row, own_ref, col_ref, table_ref):
    _, depth, wx, _ = own_ref.shape
    for c in range(2):
        for z in range(depth):
            at = (c * depth + z) * wx
            col_ref[at : at + wx] = own_ref[c, z].astype(BF16)
    table_ref[...] = x_table(lax.axis_index("row"), n_row, wx)


def pack_kernel(n_row, n_sec, per, own_ref, row_ref):
    _, depth, wx, wy = own_ref.shape
    edges = []
    densities = [[own_ref[c, z] for z in range(depth)] for c in range(2)]
    for c in range(2):
        for z in range(depth):
            tile = densities[c][z]
            edges += [tile[0:2], tile[wx - 2 : wx]]
    for z in range(depth):
        row_ref[z * wx : (z + 1) * wx] = (densities[0][z] - densities[1][z]).astype(BF16)
    edge = jnp.concatenate(edges, axis=0).astype(BF16)
    at = depth * wx
    count = edge.shape[0]
    row_ref[at : at + count] = edge

    row, sec = lax.axis_index("row"), lax.axis_index("sec")
    square, root = shell_root(row * wx, sec * wy, wx * n_row, wy * n_sec, wx, wy)
    special = (root * root == square + 1.0) & (root < NSHELL) & (square > 0.0)
    nudge = jnp.where(special, own_ref[2, 0] - (root - 1.0), 0.0)
    one = jnp.where(special, F32(1.0), F32(0.0)).astype(BF16)
    down = lax.broadcasted_iota(jnp.int32, (wx, wx), 0)
    above = (lax.broadcasted_iota(jnp.int32, (wx, wx), 1) < down).astype(F32).astype(BF16)
    rank = jnp.dot(above, one, preferred_element_type=F32)
    section = row_ref.shape[0] - at - count
    line = lax.broadcasted_iota(jnp.int32, (section, wy), 0)
    marks = jnp.zeros((section, wy), F32)
    for number in range(per):
        found = jnp.sum(jnp.where(rank == number, nudge, 0.0), axis=0, keepdims=True)
        marks = jnp.where(line == row * per + number, found, marks)
    row_ref[at + count :] = marks.astype(BF16)


def shell_root(first_x, first_y, full_x, full_y, wx, wy):
    kx = first_x + lax.broadcasted_iota(jnp.int32, (wx, wy), 0)
    ky = first_y + lax.broadcasted_iota(jnp.int32, (wx, wy), 1)
    kx = jnp.where(kx < full_x // 2, kx, kx - full_x)
    ky = jnp.where(ky < full_y // 2, ky, ky - full_y)
    square = (kx * kx + ky * ky).astype(F32)
    return square, jnp.floor(jnp.sqrt(square + 1.0) + 0.5)


def half_kernel(depth, wx, n_row, *refs):
    row_refs, table_ref, bulk_ref = refs[:n_row], refs[n_row], refs[n_row + 1]
    full_x = table_ref.shape[0]
    lines = jnp.concatenate(
        [
            jnp.concatenate([r[z * wx : (z + 1) * wx] for r in row_refs], axis=0)
            for z in range(depth)
        ],
        axis=1,
    )
    half = jnp.dot(table_ref[...], lines, preferred_element_type=F32).astype(BF16)
    wy = bulk_ref.shape[1]
    for z in range(depth):
        bulk_ref[z * full_x : (z + 1) * full_x] = half[:, z * wy : (z + 1) * wy]
    at = depth * wx + 8 * depth
    marks = sum(ref[at:].astype(F32) for ref in row_refs)
    bulk_ref[depth * full_x : depth * full_x + marks.shape[0]] = marks.astype(BF16)
    rest = depth * full_x + marks.shape[0]
    if rest < bulk_ref.shape[0]:
        bulk_ref[rest:] = jnp.zeros((bulk_ref.shape[0] - rest, bulk_ref.shape[1]), BF16)


def edges_of(col_ref, wx):
    lines = []
    for start in range(0, col_ref.shape[0], wx):
        lines.append(col_ref[start : start + 16].astype(F32)[:2])
        lines.append(col_ref[start + wx - 16 : start + wx].astype(F32)[14:])
    return jnp.concatenate(lines, axis=0)


def middle_kernel(n_row, n_col, section, names, own_ref, row_ref, *refs):
    _, depth, wx, wy = own_ref.shape
    col_moves, row_moves = len(ring_moves(n_col)), len(ring_moves(n_row))
    by_name, refs = dict(zip(names, refs)), refs[len(names) :]
    bulk_ref, msg_ref, strip_ref, dens_ref, lanes_ref = refs
    col_refs = [by_name["col", i] for i in range(col_moves)]
    row_refs = [row_ref] + [by_name["row", k] for k in range(1, n_row)]
    diag_refs = [by_name["diag", i] for i in range(col_moves * row_moves)]
    row, col = lax.axis_index("row"), lax.axis_index("col")
    at = depth * wx
    count = 8 * depth
    col_prev, col_next = ring_pick(n_col, col)
    before = choose([r[...].astype(F32) for r in col_refs], col_prev)
    after = choose([r[...].astype(F32) for r in col_refs], col_next)
    edge_list = [r[at : at + count].astype(F32) for r in row_refs]
    edge_prev = choose(edge_list, row ^ lax.rem(row + n_row - 1, n_row)) if n_row > 2 else edge_list[1]
    edge_next = choose(edge_list, row ^ lax.rem(row + 1, n_row)) if n_row > 2 else edge_list[1]
    row_prev, row_next = ring_pick(n_row, row)
    diag = [
        r[at : at + count].astype(F32) if r.shape == row_ref.shape else edges_of(r, wx)
        for r in diag_refs
    ]

    def diag_of(row_which, col_which):
        lines = [
            choose(diag[m * col_moves : (m + 1) * col_moves], col_which) for m in range(row_moves)
        ]
        return choose(lines, row_which)

    corner = {
        (0, -1): diag_of(row_prev, col_prev),
        (0, 1): diag_of(row_prev, col_next),
        (1, -1): diag_of(row_next, col_prev),
        (1, 1): diag_of(row_next, col_next),
    }
    lane = lax.broadcasted_iota(jnp.int32, (ROWS, wy), 1)
    gap = jnp.zeros((ROWS - wx - 4, wy), F32)
    strips = jnp.zeros((ROWS, wy), F32)
    layers = depth + 4
    for c in range(2):
        for layer in range(layers):
            z = layer - 2
            if z < 0:
                source, plane, low, high = before, depth + z, corner[0, -1], corner[1, -1]
            elif z >= depth:
                source, plane, low, high = after, z - depth, corner[0, 1], corner[1, 1]
            else:
                source, plane, low, high = None, z, edge_prev, edge_next
            where = c * depth + plane
            if source is None:
                body = own_ref[c, plane]
            else:
                body = source[where * wx : (where + 1) * wx]
            tail = jnp.concatenate(
                [high[where * 4 : where * 4 + 2], gap, low[where * 4 + 2 : where * 4 + 4]], axis=0
            )
            tile = jnp.concatenate([body, tail], axis=0)
            group = c * layers + layer
            dens_ref[group] = tile
            at_lane = 8 * group
            moved = pltpu.roll(tile, (at_lane + 2) % wy, 1)
            strips = jnp.where((lane >= at_lane) & (lane < at_lane + 4), moved, strips)
    lanes_ref[...] = strips + pltpu.roll(strips, 4, 1)
    lower = jnp.concatenate([strips[TOP:], jnp.zeros((2 * TOP - ROWS, wy), F32)], axis=0)
    folded = strips[:TOP] + pltpu.roll(lower, 4, 1)
    gap = jnp.zeros((strip_ref.shape[0] - TOP, wy), F32)
    strip_ref[...] = jnp.concatenate([folded, gap], axis=0).astype(BF16)
    at = msg_ref.shape[0] - whole(section + TOP)
    msg_ref[:at] = bulk_ref[:at]
    parts = [bulk_ref[at : at + whole(section)].astype(F32)[:section], folded]
    missing = msg_ref.shape[0] - at - section - TOP
    if missing:
        parts.append(jnp.zeros((missing, wy), F32))
    msg_ref[at:] = jnp.concatenate(parts, axis=0).astype(BF16)


def turn(tile, shift, axis):
    shift = shift % tile.shape[axis]
    return tile if shift == 0 else pltpu.roll(tile, shift, axis)


def pull_of(below, here, above):
    around = below + above
    line_y = turn(here, -1, 1) + turn(here, 1, 1)
    line_x = turn(here, -1, 0) + turn(here, 1, 0)
    flat = 2.0 * here + around
    mix = flat + line_y
    pull_x = turn(mix, -1, 0) - turn(mix, 1, 0)
    mix = flat + line_x
    pull_y = turn(mix, -1, 1) - turn(mix, 1, 1)
    gap = above - below
    pull_z = 2.0 * gap + turn(gap, -1, 0) + turn(gap, 1, 0) + turn(gap, -1, 1) + turn(gap, 1, 1)
    return pull_x, pull_y, pull_z


def relax_terms(density, velocity):
    vx, vy, vz = velocity
    squared = vx * vx + vy * vy + vz * vz
    rest = density * (1.0 - 1.875 * squared)
    terms = [WEIGHTS[0] * rest]
    for number in range(1, 19, 2):
        offsets = LATTICE[number]
        projected = None
        for axis in range(3):
            if offsets[axis]:
                part = velocity[axis] if offsets[axis] > 0 else -velocity[axis]
                projected = part if projected is None else projected + part
        weighted = density * projected
        even = WEIGHTS[number] * (rest + 5.625 * (weighted * projected))
        odd = (WEIGHTS[number] * 3.75) * weighted
        terms += [even + odd, even - odd]
    return terms


def cells_kernel(dens_ref, out_ref):
    _, depth, wx, _ = out_ref.shape
    layers = depth + 4
    scale = -1.6 / 36.0
    for layer in range(1, layers - 1):
        for c in range(2):
            other = (1 - c) * layers + layer
            pulls = pull_of(dens_ref[other - 1], dens_ref[other], dens_ref[other + 1])
            velocity = [scale * p for p in pulls]
            terms = relax_terms(dens_ref[c * layers + layer], velocity)
            for number in range(19):
                cx, cy, cz = LATTICE[number]
                z = layer - 2 + cz
                if 0 <= z < depth:
                    tile = turn(turn(terms[number], cx, 0), cy, 1)
                    out_ref[c * 19 + number, z] = tile[:wx]


def set_ends(n_sec, start, at, msg_refs, lanes_ref, cells_ref, out_hbm, out_ref, sems):
    _, depth, wx, wy = out_ref.shape
    layers = depth + 4
    strips = [
        r[:].astype(F32)[:TOP] if r.shape[0] < start else r[start:].astype(F32)[at - start :][:TOP]
        for r in msg_refs
    ]
    index = lax.axis_index("sec")
    prev_which, next_which = ring_pick(n_sec, index)
    before, after = choose(strips, prev_which), choose(strips, next_which)
    rest = ROWS - TOP
    before = jnp.concatenate([before, turn(before, -4, 1)[:rest]], axis=0)
    after = jnp.concatenate([turn(after, 4, 1), after[:rest]], axis=0)
    place = lax.rem(lax.broadcasted_iota(jnp.int32, (ROWS, wy), 1), 8)
    tile = jnp.where(place < 2, before, jnp.where(place >= 6, after, lanes_ref[...]))
    pulls = pull_of(turn(tile, 8, 1), tile, turn(tile, -8, 1))
    span = 8 * layers
    first = lax.broadcasted_iota(jnp.int32, (ROWS, wy), 1) < span
    scale = -1.6 / 36.0
    velocity = [scale * jnp.where(first, turn(p, -span, 1), turn(p, span, 1)) for p in pulls]
    terms = relax_terms(tile, velocity)
    lane = lax.broadcasted_iota(jnp.int32, (wx, wy), 1)
    copies = []
    moved = []
    for number in range(19):
        cx, cy, cz = LATTICE[number]
        term = turn(terms[number], cx, 0)[:wx]
        if cy == 0:
            term = jnp.where(place[:wx] == 1, turn(term, -4, 1), term)
        moved.append(term)
    masks = {1: lane < 2, -1: lane >= wy - 2, 0: (lane == 0) | (lane == wy - 1)}
    begin = 0
    for q in range(38):
        c, number = divmod(q, 19)
        _, cy, cz = LATTICE[number]
        for z in range(depth):
            group = 8 * (c * layers + 2 + z - cz)
            back = {1: group + 1, -1: group + 5 - (wy - 2), 0: group + 2}[cy]
            out_ref[q, z] = jnp.where(masks[cy], turn(moved[number], -back, 1), cells_ref[q, z])
        if q + 1 in ENDS:
            span = pl.ds(begin, q + 1 - begin)
            copy = pltpu.make_async_copy(
                out_ref.at[span], out_hbm.at[span], sems.at[len(copies)]
            )
            copy.start()
            copies.append(copy)
            begin = q + 1
    return copies


def early_kernel(n_sec, lanes, taken, *refs):
    msg_refs, (large_ref, out_ref) = refs[:-2], refs[-2:]
    wy = large_ref.shape[0] // n_sec
    sec = lax.axis_index("sec")
    total = None
    for k, ref in zip(taken, msg_refs):
        start = pl.multiple_of((sec ^ k) * wy, wy)
        part = jnp.dot(
            ref[: out_ref.shape[0]],
            large_ref[pl.ds(start, wy), : 2 * lanes],
            preferred_element_type=F32,
        )
        total = part if total is None else total + part
    out_ref[...] = total


def final_kernel(n_sec, section, places, total, move, msg_own_ref, *refs):
    msg_refs = [msg_own_ref] + [refs[swap_order(n_sec).index(k)] for k in range(1, n_sec)]
    refs = refs[n_sec - 1 :]
    ring = []
    for move_ in ring_moves(n_sec):
        k = move_[0][1]
        if k in EARLY.get(n_sec, ()):
            ring.append(refs[0])
            refs = refs[1:]
        else:
            ring.append(msg_refs[k])
    (strips_ref, cells_ref), refs = refs[:2], refs[2:]
    (early_ref, large_ref, small_ref,
     out_hbm, spec_hbm, mark_ref, part_ref, out_ref, spec_ref, sems) = refs
    depth = spec_ref.shape[0]
    sec = lax.axis_index("sec")
    full_y, lanes = large_ref.shape[0], move.shape[1]
    wy = full_y // n_sec
    full_x = early_ref.shape[0] // depth
    half_x = full_x // 2
    hrows = half_x + 8
    at = depth * full_x
    at_mult, at_counts, at_put, at_row, at_step, at_move = places
    copies = set_ends(n_sec, at, at + section, ring, strips_ref, cells_ref, out_hbm, out_ref, sems)

    for k in range(n_sec):
        start = pl.multiple_of((sec ^ k) * wy, wy)
        mark_ref[:, pl.ds(start, wy)] = msg_refs[k][at : at + mark_ref.shape[0]]
    transform = early_ref[...]
    for k in late_swaps(n_sec):
        start = pl.multiple_of((sec ^ k) * wy, wy)
        transform = transform + jnp.dot(
            msg_refs[k][:at],
            large_ref[pl.ds(start, wy), : 2 * lanes],
            preferred_element_type=F32,
        )

    find = large_ref[:, 2 * lanes : 2 * lanes + total]
    found = jnp.dot(mark_ref[...], find, preferred_element_type=F32)[:section]
    nudge = jnp.sum(found * small_ref[at_put:at_row, :total], axis=0, keepdims=True)

    mult = small_ref[at_mult : at_mult + 1, :lanes]
    columns = large_ref[:lanes, 2 * lanes + total :]
    row_zero = lax.broadcasted_iota(jnp.int32, (half_x, lanes), 0) == 0
    rest = jnp.zeros((7, lanes), F32)
    picks = []
    for z in range(depth):
        real = transform[z * full_x : z * full_x + half_x]
        imag = transform[z * full_x + half_x : (z + 1) * full_x]
        rc, rs = real[:, :lanes], real[:, lanes:]
        ic, is_ = imag[:, :lanes], imag[:, lanes:]
        top = rc * rc + rs * rs
        low = ic * ic + is_ * is_
        both = top + low
        cross = 2.0 * (rc * is_ - ic * rs)
        part_ref[z, :half_x] = mult * jnp.where(row_zero, top, 2.0 * both)
        part_ref[z, half_x:] = jnp.concatenate([mult * low[0:1], rest], axis=0)
        plus = jnp.concatenate([jnp.where(row_zero, top, both + cross), low[0:1], rest], axis=0)
        minus = jnp.concatenate([both - cross, low[0:1], rest], axis=0)
        value = 0.0
        for number, power in enumerate((plus, minus)):
            head = power.astype(BF16)
            tail = (power - head.astype(F32)).astype(BF16)
            found = jnp.dot(head, columns, preferred_element_type=F32) + jnp.dot(
                tail, columns, preferred_element_type=F32
            )
            start = at_row + number * hrows
            rows = small_ref[start : start + hrows, :total]
            value = value + jnp.sum(found * rows, axis=0, keepdims=True)
        picks.append(value)
    picks.append(jnp.ones_like(picks[0]))
    picks.append(jnp.zeros((8 - len(picks), picks[0].shape[1]), F32))
    moved = lax.dot_general(
        jnp.concatenate(picks, axis=0) * nudge,
        small_ref[at_step : at_step + total, :NSHELL],
        (((1,), (0,)), ((), ())),
        precision=lax.Precision.HIGHEST, preferred_element_type=F32,
    )

    tiles = NSHELL // 128
    lane = lax.broadcasted_iota(jnp.int32, (8, 128), 1)
    sums = [[jnp.zeros((8, 128), F32) for _ in range(tiles)] for _ in range(depth)]
    for tile in range(lanes // 128):
        block = move[:, tile * 128 : (tile + 1) * 128]
        at_lanes = slice(tile * 128, (tile + 1) * 128)
        for value in np.unique(block):
            if value == UNUSED:
                continue
            value = int(value)
            totals = [None] * depth
            for group in range(hrows // 8):
                if not (block[group * 8 : group * 8 + 8] == value).any():
                    continue
                rows = slice(group * 8, group * 8 + 8)
                line = slice(at_move + group * 8, at_move + group * 8 + 8)
                same = small_ref[line, at_lanes] == F32(value)
                for z in range(depth):
                    term = jnp.where(same, part_ref[z, rows, at_lanes], 0.0)
                    totals[z] = term if totals[z] is None else totals[z] + term
            shift = value % 128
            goal = tile + value // 128
            for z in range(depth):
                total = turn(totals[z], shift, 1)
                if 0 <= goal < tiles:
                    sums[z][goal] += jnp.where(lane >= shift, total, 0.0)
                if shift and 0 <= goal + 1 < tiles:
                    sums[z][goal + 1] += jnp.where(lane < shift, total, 0.0)
    counts = small_ref[at_counts : at_counts + 1, :NSHELL]
    norm = (counts + moved[depth : depth + 1]) * float(full_x * full_y)
    lines = []
    for z in range(depth):
        line = jnp.sum(jnp.concatenate(sums[z], axis=1), axis=0, keepdims=True)
        lines.append((line + moved[z : z + 1]) / norm)
    spec_ref[...] = jnp.concatenate(lines, axis=0)
    copies.append(pltpu.make_async_copy(spec_ref, spec_hbm, sems.at[len(ENDS)]))
    copies[-1].start()
    for copy in copies:
        copy.wait()


def call(kernel, outs, scratch=(), flops=0, moved=0, limit=48 << 20, **specs):
    return pl.pallas_call(
        kernel,
        out_shape=outs,
        scratch_shapes=list(scratch),
        compiler_params=pltpu.CompilerParams(vmem_limit_bytes=limit),
        cost_estimate=pl.CostEstimate(flops=flops, bytes_accessed=moved, transcendentals=0),
        **specs,
    )


def on_device(n_sec, n_row, n_col, labels, jitter, shells):
    depth, wx, wy = labels.shape
    full_x, full_y = wx * n_row, wy * n_sec
    tables = make_tables(full_x, full_y, n_row, n_sec, wx, wy)
    per, section = tables["per"], tables["section"]
    layers = depth + 4
    count = 8 * depth
    shape = jax.ShapeDtypeStruct

    part = lax.broadcasted_iota(jnp.int32, (3, depth, wx, wy), 0)
    none = (0, 0, 0)
    factor = lax.pad(jitter, F32(0.0), ((0, 1, 0), none, none, none))
    whole_numbers = jnp.where(part == 2, shells[None, None], labels[None] ^ part)
    density = jnp.where(whole_numbers == 1, F32(1.0), F32(0.2)) * factor
    own = jnp.where(part == 2, whole_numbers.astype(F32), density)
    row_msg = call(
        functools.partial(pack_kernel, n_row, n_sec, per),
        shape((depth * wx + count + whole(section), wy), BF16),
    )(own)
    col_msg, table_x = call(
        functools.partial(planes_kernel, n_row),
        [shape((2 * depth * wx, wy), BF16), shape((full_x, full_x), BF16)],
    )(own)

    col_got = [lax.ppermute(col_msg, "col", m) for m in ring_moves(n_col)]
    row_got = [lax.ppermute(row_msg, "row", xor_pairs(n_row, k)) for k in range(1, n_row)]
    relay = n_row == 2 and n_col == 4
    diag_got = []
    for a in ring_moves(n_row):
        for b in ring_moves(n_col):
            if relay and b == xor_pairs(n_col, 1):
                diag_got.append(lax.ppermute(row_got[0], "col", b))
            else:
                move = pair_product(a, b, n_col)
                diag_got.append(lax.ppermute(col_msg, ("row", "col"), move))

    at = depth * full_x
    got = {("col", i): value for i, value in enumerate(col_got)}
    got.update({("row", k + 1): value for k, value in enumerate(row_got)})
    got.update({("diag", i): value for i, value in enumerate(diag_got)})
    names = [name for name in FIRST_ROUND if name in got]
    names += [name for name in got if name not in names]
    bulk = call(
        functools.partial(half_kernel, depth, wx, n_row), shape((at + whole(section + TOP), wy), BF16),
        flops=1 << 27, moved=1 << 24
    )(row_msg, *row_got, table_x)
    msg, strip, dens, lanes_own = call(
        functools.partial(middle_kernel, n_row, n_col, section, tuple(names)),
        [
            shape((at + whole(section + TOP), wy), BF16),
            shape((whole(TOP), wy), BF16),
            shape((2 * layers, ROWS, wy), F32),
            shape((ROWS, wy), F32),
        ],
        flops=MID,
        moved=MID,
    )(own, row_msg, *[got[name] for name in names], bulk)

    ring = ring_moves(n_sec)
    early = EARLY.get(n_sec, ())
    sec_got, strip_got = [], []
    for k in swap_order(n_sec):
        move = xor_pairs(n_sec, k)
        with_columns = move in ring and k not in early
        sec_got.append(lax.ppermute(msg if with_columns else bulk, "sec", move))
    for move in ring:
        if move[0][1] in early:
            strip_got.append(lax.ppermute(strip, "sec", move))

    cells = call(
        cells_kernel,
        shape((38, depth, wx, wy), F32),
        flops=LBM,
        moved=LBM,
    )(dens)

    hrows, lanes = full_x // 2 + 8, full_y // 2 + 128
    taken = (0,) + EARLY.get(n_sec, ())
    blocks = [bulk if k == 0 else sec_got[swap_order(n_sec).index(k)] for k in taken]
    early_part = call(
        functools.partial(early_kernel, n_sec, lanes, taken),
        shape((depth * full_x, 2 * lanes), F32),
    )(*blocks, tables["large"])
    return call(
        functools.partial(
            final_kernel, n_sec, section, tables["places"], tables["total"], tables["move"]
        ),
        [shape((38, depth, wx, wy), F32), shape((depth, NSHELL), F32)],
        [
            pltpu.VMEM((whole(section), full_y), BF16),
            pltpu.VMEM((depth, hrows, lanes), F32),
            pltpu.VMEM((38, depth, wx, wy), F32),
            pltpu.VMEM((depth, NSHELL), F32),
            pltpu.SemaphoreType.DMA((len(ENDS) + 1,)),
        ],
        out_specs=[pl.BlockSpec(memory_space=pltpu.HBM)] * 2,
    )(bulk, *sec_got, *strip_got, lanes_own, cells, early_part, tables["large"], tables["small"])


def solution(mesh):
    in_specs = (P("col", "row", "sec"), P(None, "col", "row", "sec"), P("row", "sec"))
    out_specs = (P(None, "col", "row", "sec"), P("col", None))
    sizes = [mesh.shape[name] for name in ("sec", "row", "col")]
    return jax.shard_map(
        functools.partial(on_device, *sizes),
        mesh=mesh,
        in_specs=in_specs,
        out_specs=out_specs,
        check_vma=False,
    )
```
